32 devices in a mesh: row: 4 (over z), col: 8 (over y, x, core).
Axes of the slice: x: 2, y: 2, z: 4, core: 2. Of those that a mesh axis runs over, the one named last changes fastest.
Arguments:
- tokens: bfloat16 [768, 14336], P('col', 'row'), may hold values from -6 to 6
- weight_in: bfloat16 [14336, 14336], P('row', 'col'), may hold values from -0.046875 to 0.046875
- bias_hidden: float32 [14336], P('col'), may hold values from -3 to 3
- weight_out: bfloat16 [14336, 14336], P('col', 'row'), may hold values from -0.046875 to 0.046875
- out_grad: bfloat16 [768, 14336], P('col', 'row'), may hold values from -0.75 to 0.75
Outputs:
- grad_tokens: bfloat16 [768, 14336], P('col', 'row')
- grad_weight_in: float32 [14336, 14336], P('row', 'col')
- grad_bias: float32 [14336], P('col')
- grad_weight_out: float32 [14336, 14336], P('col', 'row')
The draws below stay inside these ranges and needn't reach their ends.
All inputs are finite; a program needn't handle non-finite values.
Results may differ from the reference program's by a relative error of at most 0.007.
Values may be sent and summed in bfloat16 or wider, within the bound.
No kernel may reach another device: no remote copies, remote signals or barrier semaphores. Data moves between devices by JAX's collectives and lax.ppermute only.
A program may use at most 192 MiB of HBM per device.

```python
import jax
import jax.numpy as jnp
from jax import lax

D = 14336
FFC = 14336
TOKENS = 768


def shard_levels(stream_key, dims, shards, least, high):
    gain, own = 1.0, jax.random.fold_in(stream_key, 6)
    for axis_at, shards_of in shards:
        draws = jnp.exp(jax.random.uniform(jax.random.fold_in(own, axis_at), (shards_of,), jnp.float32, least / len(shards), high / len(shards)))
        gain = gain * jnp.repeat(draws, dims[axis_at] // shards_of).reshape([-1 if axis == axis_at else 1 for axis in range(len(dims))])
    return gain


def noise(stream_key, dims, scale, reach, split=(), kind=jnp.bfloat16):
    values = scale * jax.random.normal(stream_key, dims, jnp.float32)
    if split:
        values = values * shard_levels(stream_key, dims, split, -0.22, 0.18)
    return jnp.clip(values, -reach, reach).astype(kind)


def setup_inputs(seed: int = 0) -> dict:
    streams_of = jax.random.split(jax.random.key(seed), 6)
    return {
        "tokens": noise(streams_of[0], (TOKENS, D), 1.0, 6.0, ((0, 8), (1, 4))),
        "weight_in": noise(streams_of[1], (D, FFC), D ** -0.5, 0.046875, ((0, 4), (1, 8))),
        "bias_hidden": noise(streams_of[2], (FFC,), 0.5, 3.0, ((0, 8),), jnp.float32),
        "weight_out": noise(streams_of[3], (FFC, D), FFC ** -0.5, 0.046875, ((0, 8), (1, 4))),
        "out_grad": noise(streams_of[4], (TOKENS, D), 0.125, 0.75, ((0, 8), (1, 4))),
    }


GELU_SCALE = 0.7978845608
GELU_CUBIC = 0.044715


def gelu_parts(values):
    inner = GELU_SCALE * (values + GELU_CUBIC * values * values * values)
    tangent = jnp.tanh(inner)
    result = 0.5 * values * (1.0 + tangent)
    slope = 0.5 * (1.0 + tangent) + 0.5 * values * (1.0 - tangent * tangent) * GELU_SCALE * (1.0 + 3.0 * GELU_CUBIC * values * values)
    return result, slope


def contract_rows(left, right):
    return lax.dot_general(left, right, (((0,), (0,)), ((), ())), preferred_element_type=jnp.float32)


def reference(tokens, weight_in, bias_hidden, weight_out, out_grad):
    pre = jnp.dot(tokens, weight_in, preferred_element_type=jnp.float32) + bias_hidden
    act_grad = lax.dot_general(out_grad, weight_out, (((1,), (1,)), ((), ())), preferred_element_type=jnp.float32)
    result, slope = gelu_parts(pre)
    act = result.astype(jnp.bfloat16)
    pre_grad = (act_grad * slope).astype(jnp.bfloat16)
    grad_bias = jnp.sum(pre_grad, axis=0, dtype=jnp.float32)
    grad_weight_out = contract_rows(act, out_grad)
    grad_weight_in = contract_rows(tokens, pre_grad)
    grad_tokens = lax.dot_general(pre_grad, weight_in, (((1,), (1,)), ((), ())), preferred_element_type=jnp.float32).astype(jnp.bfloat16)
    return grad_tokens, grad_weight_in, grad_bias, grad_weight_out
```

```python
import functools

import jax
import jax.numpy as jnp
from jax import lax
from jax.experimental import pallas as pl
from jax.experimental.pallas import tpu as pltpu
from jax.sharding import PartitionSpec as P

GELU_SCALE = 0.7978845608
GELU_CUBIC = 0.044715
F32, BF16 = jnp.float32, jnp.bfloat16
VMEM_LIMIT = 48 * 1024 * 1024
GROUPS, CHUNKS, TILE = 2, 7, 512


def dot(left, right, dims):
    return lax.dot_general(left, right, ((dims[:1], dims[1:]), ((), ())), preferred_element_type=F32)


def call(kernel, flops, moved, **kwargs):
    return pl.pallas_call(
        kernel,
        compiler_params=pltpu.CompilerParams(vmem_limit_bytes=VMEM_LIMIT),
        cost_estimate=pl.CostEstimate(flops=flops, bytes_accessed=moved, transcendentals=0),
        **kwargs,
    )


def partials(tok, out_grad, weight_in, weight_out, first, count):
    rows, depth = tok.shape
    width = weight_in.shape[1] // CHUNKS

    def kernel(tok_ref, grad_ref, win_ref, wout_ref, *outs):
        pre = dot(tok_ref[...], win_ref[...], (1, 0)).astype(BF16)
        act = dot(grad_ref[...], wout_ref[...], (1, 1)).astype(BF16)
        for at, out in enumerate(outs):

            @pl.when(pl.program_id(0) == at)
            def _():
                out[0] = pre
                out[1] = act

    whole = pl.BlockSpec((rows, depth), lambda i: (0, 0), pipeline_mode=pl.Buffered(1))
    return call(
        kernel,
        4 * rows * depth * width * count,
        4 * depth * (rows + width * count) + 4 * rows * width * count,
        grid=(count,),
        in_specs=[
            whole,
            whole,
            pl.BlockSpec((depth, width), lambda i: (0, first + i)),
            pl.BlockSpec((width, depth), lambda i: (first + i, 0)),
        ],
        out_specs=[pl.BlockSpec((2, rows, width), lambda i: (0, 0, 0), pipeline_mode=pl.Buffered(1))] * count,
        out_shape=[jax.ShapeDtypeStruct((2, rows, width), BF16)] * count,
    )(tok, out_grad, weight_in, weight_out)


def gelu_parts(values):
    inner = GELU_SCALE * (values + GELU_CUBIC * values * values * values)
    tangent = jnp.tanh(inner)
    result = 0.5 * values * (1.0 + tangent)
    slope = 0.5 * (1.0 + tangent) + 0.5 * values * (1.0 - tangent * tangent) * GELU_SCALE * (
        1.0 + 3.0 * GELU_CUBIC * values * values
    )
    return (result, slope)


def activate(terms, bias, at):
    _, rows, width = terms[0].shape

    def kernel(bias_ref, *refs):
        ins, (act_ref, grad_ref, sum_ref) = refs[:-3], refs[-3:]
        pre, act = (functools.reduce(jnp.add, [ref[half].astype(F32) for ref in ins]) for half in range(2))
        result, slope = gelu_parts(pre + bias_ref[...])
        act_ref[...] = result.astype(BF16)
        grad = (act * slope).astype(BF16)
        grad_ref[...] = grad
        sum_ref[...] = jnp.sum(grad.astype(F32), axis=0, keepdims=True)

    return call(
        kernel,
        40 * rows * width,
        4 * rows * width * (len(terms) + 1),
        grid=(1,),
        in_specs=[pl.BlockSpec((1, width), lambda i: (0, at))]
        + [pl.BlockSpec((2, rows, width), lambda i: (0, 0, 0))] * len(terms),
        out_specs=[pl.BlockSpec((rows, width), lambda i: (0, 0))] * 2 + [pl.BlockSpec((1, width), lambda i: (0, 0))],
        out_shape=[jax.ShapeDtypeStruct((rows, width), BF16)] * 2 + [jax.ShapeDtypeStruct((1, width), F32)],
    )(bias, *terms)


def add_bf16(left, right):
    return (left.astype(F32) + right.astype(F32)).astype(BF16)


def outer(lefts, rights, into, shape, first, count, chunk_rows):
    rows, depth = lefts[0].shape
    width = rights[0][0].shape[1]
    tile = TILE if depth % TILE == 0 else depth
    groups = len(lefts)

    def kernel(*refs):
        wide, thin, out = refs[:groups], refs[groups : groups + groups * count], refs[-1]
        for i in range(count):
            total = None
            for group in range(groups):
                chunk = thin[group * count + i][...]
                pair = (chunk, wide[group][...]) if chunk_rows else (wide[group][...], chunk)
                term = dot(*pair, (0, 0))
                total = term if total is None else total + term
            if chunk_rows:
                out[i * width : (i + 1) * width, :] = total
            else:
                out[:, i * width : (i + 1) * width] = total

    at = first // count
    block = (count * width, tile) if chunk_rows else (tile, count * width)
    place = (lambda j: (at, j)) if chunk_rows else (lambda j: (j, at))
    operands = list(lefts) + [chunk for group in rights for chunk in group]
    specs = [pl.BlockSpec((rows, tile), lambda j: (0, j))] * groups
    specs += [pl.BlockSpec((rows, width), lambda j: (0, 0))] * (groups * count)
    aliases = {}
    if into is not None:
        aliases = {len(operands): 0}
        operands.append(into)
        specs.append(pl.BlockSpec(memory_space=pl.ANY))
    return call(
        kernel,
        2 * groups * rows * depth * width * count,
        2 * groups * rows * depth + 4 * depth * width * count,
        grid=(depth // tile,),
        in_specs=specs,
        out_specs=pl.BlockSpec(block, place),
        out_shape=jax.ShapeDtypeStruct(shape, F32),
        input_output_aliases=aliases,
    )(*operands)


def back(grads, weight_in, first, base, last):
    rows, width = grads[0].shape
    depth = weight_in.shape[0]
    tile = TILE if depth % TILE == 0 else depth
    count = len(grads)

    def kernel(*refs):
        parts, weights = refs[:count], refs[count : 2 * count]
        total = None if base is None else refs[2 * count][...]
        for part, weight in zip(parts, weights):
            term = dot(part[...], weight[...], (1, 1))
            total = term if total is None else total + term
        if last:
            refs[-2][...] = total[: rows // 2].astype(BF16)
            refs[-1][...] = total[rows // 2 :].astype(BF16)
        else:
            refs[-1][...] = total

    specs = [pl.BlockSpec((rows, width), lambda j: (0, 0))] * count
    specs += [pl.BlockSpec((tile, width), lambda j, at=first + i: (j, at)) for i in range(count)]
    operands = list(grads) + [weight_in] * count
    if base is not None:
        specs.append(pl.BlockSpec((rows, tile), lambda j: (0, j)))
        operands.append(base)
    out_rows, kind = (rows // 2, BF16) if last else (rows, F32)
    outs = 2 if last else 1
    result = call(
        kernel,
        2 * rows * depth * width * count,
        2 * depth * width * count + 4 * rows * depth,
        grid=(depth // tile,),
        in_specs=specs,
        out_specs=[pl.BlockSpec((out_rows, tile), lambda j: (0, j))] * outs,
        out_shape=[jax.ShapeDtypeStruct((out_rows, depth), kind)] * outs,
    )(*operands)
    return result if last else result[0]


def swap(value, bit, size):
    return lax.ppermute(value, "col", [(i, i ^ bit) for i in range(size)])


def gather(block, bits, size):
    held = {0: block}
    for bit in bits:
        keys = list(held)
        for key in keys:
            held[key ^ bit] = swap(held[key], bit, size)
    return jnp.concatenate([held[key] for key in sorted(held)], axis=0)


def scatter(total, bits, size):
    held = dict(total)
    for bit in bits:
        sent = {key: swap(held[key], bit, size) for key in held if key & bit}
        held = {key: held[key].astype(F32) + sent[key ^ bit].astype(F32) for key in held if not key & bit}
        held = {key: value.astype(BF16) for key, value in held.items()}
    return held[0]


def gate(value, after):
    return lax.optimization_barrier((value, after))[0]


def local(rows_of, cols_of, tokens, weight_in, bias_hidden, weight_out, out_grad):
    mine, depth = tokens.shape
    hidden = bias_hidden.shape[0]
    part = mine // GROUPS
    bias = bias_hidden.reshape(1, hidden)
    chip_bits = [1 << i for i in range(1, cols_of.bit_length() - 1)]
    steps = rows_of - 1

    def send(value, step):
        pairs = [(step - 1, step), (rows_of - step, rows_of - step - 1)]
        return lax.ppermute(value, "row", pairs)

    def collect(group):
        rows = slice(group * part, (group + 1) * part)
        tok = gather(tokens[rows], chip_bits, cols_of)
        grad = gather(out_grad[rows], chip_bits[::-1], cols_of)
        return tuple(jnp.concatenate([x, swap(x, 1, cols_of)], axis=0) for x in (tok, grad))

    tok, grad = zip(*[collect(group) for group in range(GROUPS)])
    own = []
    for group in range(GROUPS):
        args = (tok[group], grad[group], weight_in, weight_out)
        for first, count in ((0, 1), (1, 2), (3, 4)):
            own += partials(*args, first, count)

    total = len(own)
    got = [[None] * steps for _ in range(total)]
    act, pre_grad, sums = [None] * total, [None] * total, [None] * total
    grad_weight_in = grad_weight_out = None
    base, grad_tokens = None, [None] * GROUPS
    got[0][0] = send(own[0], 1)
    for slot in range(total + steps - 1):
        if slot + 1 < total:
            value = own[slot + 1]
            if slot > 0:
                value = gate(value, got[slot - 1][0])
            got[slot + 1][0] = send(value, 1)
        for step in range(2, steps + 1):
            at = slot - step + 2
            if 0 <= at < total:
                got[at][step - 1] = send(add_bf16(got[at][step - 2], own[at]), step)
        at = slot - steps + 1
        if at < 0:
            continue
        group, chunk = divmod(at, CHUNKS)
        act[at], pre_grad[at], sums[at] = activate([own[at]] + got[at], bias, chunk)
        if chunk == CHUNKS - 2:
            base = back(pre_grad[group * CHUNKS : at + 1], weight_in, 0, None, False)
        if chunk == CHUNKS - 1:
            keep, other = back([pre_grad[at]], weight_in, chunk, base, True)
            pair = add_bf16(keep, swap(other, 1, cols_of))
            half = depth // 2
            pieces = []
            for side, bits in enumerate((chip_bits, chip_bits[::-1])):
                blocks = {
                    2 * key: pair[key * part : (key + 1) * part, side * half : (side + 1) * half]
                    for key in range(cols_of // 2)
                }
                pieces.append(scatter(blocks, bits, cols_of))
            grad_tokens[group] = jnp.concatenate(pieces, axis=1)
        if group == GROUPS - 1 and (chunk % 2 or chunk == CHUNKS - 1):
            count = 2 if chunk % 2 else 1
            first = chunk + 1 - count
            pick = lambda values: [
                [values[g * CHUNKS + first + i] for i in range(count)] for g in range(GROUPS)
            ]
            grad_weight_out = outer(grad, pick(act), grad_weight_out, (hidden, depth), first, count, True)
            grad_weight_in = outer(tok, pick(pre_grad), grad_weight_in, (depth, hidden), first, count, False)

    sums = jnp.concatenate(
        [functools.reduce(jnp.add, sums[chunk::CHUNKS]) for chunk in range(CHUNKS)], axis=1
    ).reshape(hidden)
    for bit in [1 << i for i in range(rows_of.bit_length() - 1)]:
        sums = sums + lax.ppermute(sums, "row", [(i, i ^ bit) for i in range(rows_of)])
    grad_bias = sums * (1.0 / rows_of)
    return (jnp.concatenate(grad_tokens, axis=0), grad_weight_in, grad_bias, grad_weight_out)


def solution(mesh):
    placed = (P("col", "row"), P("row", "col"), P("col"), P("col", "row"), P("col", "row"))
    return jax.shard_map(
        functools.partial(local, mesh.shape["row"], mesh.shape["col"]),
        mesh=mesh,
        in_specs=placed,
        out_specs=(P("col", "row"), P("row", "col"), P("col"), P("col", "row")),
        check_vma=False,
    )
```

```python
import functools

import jax
import jax.numpy as jnp
from jax import lax
from jax.experimental import pallas as pl
from jax.experimental.pallas import tpu as pltpu
from jax.sharding import PartitionSpec as P

GELU_SCALE = 0.7978845608
GELU_CUBIC = 0.044715
F32, BF16 = jnp.float32, jnp.bfloat16
VMEM_LIMIT = 24 * 1024 * 1024
HALVES, UNITS, SPLIT, TILE = 2, 7, (4, 3), 512


def dot(left, right, dims):
    return lax.dot_general(left, right, ((dims[:1], dims[1:]), ((), ())), preferred_element_type=F32)


def call(kernel, flops, moved, **kwargs):
    return pl.pallas_call(
        kernel,
        compiler_params=pltpu.CompilerParams(vmem_limit_bytes=VMEM_LIMIT),
        cost_estimate=pl.CostEstimate(flops=flops, bytes_accessed=moved, transcendentals=0),
        **kwargs,
    )


def pick_tile(size):
    return TILE if size % TILE == 0 else size


def partial_sums(rows, weight, first, count, transposed):
    tokens, depth = rows.shape
    hidden = weight.shape[0 if transposed else 1]
    width = hidden // UNITS

    def kernel(rows_ref, weight_ref, out_ref):
        out_ref[...] = dot(rows_ref[...], weight_ref[...], (1, 1) if transposed else (1, 0)).astype(BF16)

    if transposed:
        weight_spec = pl.BlockSpec((width, depth), lambda i: (first + i, 0))
    else:
        weight_spec = pl.BlockSpec((depth, width), lambda i: (0, first + i))
    return call(
        kernel,
        2 * tokens * depth * width * count,
        2 * (tokens * depth + depth * width * count + tokens * width * count),
        grid=(count,),
        in_specs=[
            pl.BlockSpec((tokens, depth), lambda i: (0, 0), pipeline_mode=pl.Buffered(1)),
            weight_spec,
        ],
        out_specs=pl.BlockSpec((tokens, width), lambda i: (0, i)),
        out_shape=jax.ShapeDtypeStruct((tokens, width * count), BF16),
    )(rows, weight)


def activate(terms, bias, first, count):
    rows, columns = terms[0].shape
    width = columns // count

    def kernel(bias_ref, *refs):
        ins, (act_ref, slope_ref) = refs[:-2], refs[-2:]
        pre = functools.reduce(jnp.add, [ref[...].astype(F32) for ref in ins]) + bias_ref[...]
        tangent = jnp.tanh(GELU_SCALE * (pre + GELU_CUBIC * pre * pre * pre))
        act_ref[...] = (0.5 * pre * (1.0 + tangent)).astype(BF16)
        slope_ref[...] = 0.5 * (1.0 + tangent) + 0.5 * pre * (1.0 - tangent * tangent) * GELU_SCALE * (
            1.0 + 3.0 * GELU_CUBIC * pre * pre
        )

    block = pl.BlockSpec((rows, width), lambda i: (0, i))
    return call(
        kernel,
        30 * rows * columns,
        rows * columns * (2 * len(terms) + 6),
        grid=(count,),
        in_specs=[pl.BlockSpec((1, width), lambda i: (0, first + i))] + [block] * len(terms),
        out_specs=[block] * 2,
        out_shape=[jax.ShapeDtypeStruct((rows, columns), kind) for kind in (BF16, F32)],
    )(bias, *terms)


def differentiate(terms, slope, count):
    rows, columns = slope.shape
    width = columns // count

    def kernel(slope_ref, *refs):
        ins, (grad_ref, sum_ref) = refs[:-2], refs[-2:]
        grad = functools.reduce(jnp.add, [ref[...].astype(F32) for ref in ins]) * slope_ref[...]
        grad = grad.astype(BF16)
        grad_ref[...] = grad
        sum_ref[...] = jnp.sum(grad.astype(F32), axis=0, keepdims=True)

    block = pl.BlockSpec((rows, width), lambda i: (0, i))
    return call(
        kernel,
        8 * rows * columns,
        rows * columns * (2 * len(terms) + 6),
        grid=(count,),
        in_specs=[block] * (1 + len(terms)),
        out_specs=[block, pl.BlockSpec((1, width), lambda i: (0, i))],
        out_shape=[
            jax.ShapeDtypeStruct((rows, columns), BF16),
            jax.ShapeDtypeStruct((1, columns), F32),
        ],
    )(slope, *terms)


def add_bf16(left, right):
    return (left.astype(F32) + right.astype(F32)).astype(BF16)


def weight_out_grad(acts, grads, into, hidden, first, count):
    rows, depth = grads[0].shape
    width = hidden // UNITS
    tile = pick_tile(depth)

    def kernel(*refs):
        acts, grads, out = refs[:HALVES], refs[HALVES : 2 * HALVES], refs[-1]
        turned = [act[...].T for act in acts]
        for at in range(0, depth, tile):
            terms = [dot(act, grad[:, at : at + tile], (1, 0)) for act, grad in zip(turned, grads)]
            out[:, at : at + tile] = functools.reduce(jnp.add, terms)

    operands = [*acts, *grads]
    specs = [pl.BlockSpec((rows, width), lambda i: (0, i))] * HALVES
    specs += [pl.BlockSpec((rows, depth), lambda i: (0, 0), pipeline_mode=pl.Buffered(1))] * HALVES
    aliases = {}
    if into is not None:
        aliases = {len(operands): 0}
        operands.append(into)
        specs.append(pl.BlockSpec(memory_space=pl.ANY))
    return call(
        kernel,
        2 * HALVES * rows * depth * width * count,
        2 * HALVES * rows * depth + 4 * depth * width * count,
        grid=(count,),
        in_specs=specs,
        out_specs=pl.BlockSpec((width, depth), lambda i: (first + i, 0)),
        out_shape=jax.ShapeDtypeStruct((hidden, depth), F32),
        input_output_aliases=aliases,
    )(*operands)


def weight_in_grad(toks, grads):
    rows, depth = toks[0].shape
    hidden = sum(piece.shape[1] for piece in grads[0])
    pieces = len(grads[0])
    tile = pick_tile(depth)

    def kernel(*refs):
        toks, parts, out = refs[:HALVES], refs[HALVES:-1], refs[-1]
        turned = [tok[...].T for tok in toks]
        at = 0
        for piece in range(pieces):
            width = parts[piece].shape[1]
            terms = [dot(turned[half], parts[half * pieces + piece][...], (1, 0)) for half in range(HALVES)]
            out[:, at : at + width] = functools.reduce(jnp.add, terms)
            at += width

    flat = [piece for half in grads for piece in half]
    return call(
        kernel,
        2 * HALVES * rows * depth * hidden,
        2 * HALVES * rows * (depth + hidden) + 4 * depth * hidden,
        grid=(depth // tile,),
        in_specs=[pl.BlockSpec((rows, tile), lambda j: (0, j))] * HALVES
        + [pl.BlockSpec(piece.shape, lambda j: (0, 0), pipeline_mode=pl.Buffered(1)) for piece in flat],
        out_specs=pl.BlockSpec((tile, hidden), lambda j: (j, 0)),
        out_shape=jax.ShapeDtypeStruct((depth, hidden), F32),
    )(*toks, *flat)


def token_grad(grads, weight_in):
    rows = grads[0].shape[0]
    depth, hidden = weight_in.shape
    tile = pick_tile(depth)

    def kernel(*refs):
        parts, weight, out = refs[:-2], refs[-2], refs[-1]
        at, terms = 0, []
        for part in parts:
            width = part.shape[1]
            terms.append(dot(part[...], weight[:, at : at + width], (1, 1)))
            at += width
        out[...] = functools.reduce(jnp.add, terms).astype(BF16)

    return call(
        kernel,
        2 * rows * depth * hidden,
        2 * (rows * depth + depth * hidden + rows * hidden),
        grid=(depth // tile,),
        in_specs=[pl.BlockSpec(grad.shape, lambda j: (0, 0), pipeline_mode=pl.Buffered(1)) for grad in grads]
        + [pl.BlockSpec((tile, hidden), lambda j: (j, 0))],
        out_specs=pl.BlockSpec((rows, tile), lambda j: (0, j)),
        out_shape=jax.ShapeDtypeStruct((rows, depth), BF16),
    )(*grads, weight_in)


def after(value, *deps):
    return lax.optimization_barrier((value, *deps))[0]


def local(rows_of, tokens, weight_in, bias_hidden, weight_out, out_grad):
    mine, depth = tokens.shape
    hidden = bias_hidden.shape[0]
    part = mine // HALVES
    bias = bias_hidden.reshape(1, hidden)
    steps = rows_of - 1
    starts = [sum(SPLIT[:i]) for i in range(len(SPLIT))]
    cuts = len(SPLIT)
    parts = 2 * HALVES
    total = parts * cuts

    def send(value, step):
        pairs = [(step - 1, step), (rows_of - step, rows_of - step - 1)]
        return lax.ppermute(value, "row", pairs)

    gathered = []
    for source in (tokens, out_grad):
        for half in range(HALVES):
            block = source[half * part : (half + 1) * part]
            if gathered:
                block = after(block, gathered[-1])
            gathered.append(lax.all_gather(block, "col", axis=0, tiled=True))
    toks, grads = gathered[:HALVES], gathered[HALVES:]

    chain = []

    def link(value):
        return after(value, chain[-1]) if chain else value

    own = [None] * total
    got = [[None] * steps for _ in range(total)]
    act, slope, pre_grad, sums = ([[None] * cuts for _ in range(HALVES)] for _ in range(4))
    held = {}

    def compute_own(at):
        where, cut = divmod(at, cuts)
        weight = weight_in if where < HALVES else weight_out
        own[at] = partial_sums(link(gathered[where]), weight, starts[cut], SPLIT[cut], where >= HALVES)
        chain.append(own[at])

    def forward(at, step):
        payload = add_bf16(got[at][step - 2], link(own[at]))
        chain.append(payload)
        got[at][step - 1] = send(payload, step)

    def finish(at):
        where, cut = divmod(at, cuts)
        half = where % HALVES
        terms = [link(own[at])] + got[at]
        if where < HALVES:
            act[half][cut], slope[half][cut] = activate(terms, bias, starts[cut], SPLIT[cut])
            chain.append(act[half][cut])
        else:
            pre_grad[half][cut], sums[half][cut] = differentiate(terms, slope[half][cut], SPLIT[cut])
            chain.append(pre_grad[half][cut])

    def out_rows(cut):
        acts = [link(act[half][cut]) for half in range(HALVES)]
        held["out"] = weight_out_grad(acts, grads, held.get("out"), hidden, starts[cut], SPLIT[cut])
        chain.append(held["out"])

    def tokens_of(half):
        part_sum = token_grad([link(piece) for piece in pre_grad[half]], weight_in)
        chain.append(part_sum)
        held[half] = lax.psum_scatter(part_sum, "col", scatter_dimension=0, tiled=True)

    def has(values):
        return all(value is not None for value in values)

    later = [(functools.partial(compute_own, at), lambda: True) for at in range(2, total)]
    later += [(functools.partial(tokens_of, 0), lambda: has(pre_grad[0]))]
    for cut in range(cuts):
        later.insert(-1 if cut == 0 else len(later), (functools.partial(out_rows, cut), lambda cut=cut: has(a[cut] for a in act)))
    compute_own(0)
    got[0][0] = send(own[0], 1)
    compute_own(1)
    for slot in range(total + steps - 1):
        if slot + 1 < total:
            got[slot + 1][0] = send(link(own[slot + 1]), 1)
        for step in range(2, steps + 1):
            if 0 <= slot - step + 2 < total:
                forward(slot - step + 2, step)
        if slot >= steps - 1:
            finish(slot - steps + 1)
        if later and later[0][1]():
            later.pop(0)[0]()
    for work, _ in later:
        work()
    for half in range(1, HALVES):
        tokens_of(half)
    grad_weight_in = weight_in_grad(toks, [[link(piece) for piece in half] for half in pre_grad])
    grad_weight_out = held["out"]
    grad_tokens = [held[half] for half in range(HALVES)]
    sums = jnp.concatenate(
        [functools.reduce(jnp.add, [sums[half][cut] for half in range(HALVES)]) for cut in range(cuts)], axis=1
    ).reshape(hidden)
    for bit in [1 << i for i in range(rows_of.bit_length() - 1)]:
        sums = sums + lax.ppermute(sums, "row", [(i, i ^ bit) for i in range(rows_of)])
    grad_bias = sums * (1.0 / rows_of)
    return (jnp.concatenate(grad_tokens, axis=0), grad_weight_in, grad_bias, grad_weight_out)


def solution(mesh):
    placed = (P("col", "row"), P("row", "col"), P("col"), P("col", "row"), P("col", "row"))
    return jax.shard_map(
        functools.partial(local, mesh.shape["row"]),
        mesh=mesh,
        in_specs=placed,
        out_specs=(P("col", "row"), P("row", "col"), P("col"), P("col", "row")),
        check_vma=False,
    )
```

```python
import functools

import jax
import jax.numpy as jnp
from jax import lax
from jax.experimental import pallas as pl
from jax.experimental.pallas import tpu as pltpu
from jax.sharding import PartitionSpec as P

GELU_SCALE = 0.7978845608
GELU_CUBIC = 0.044715
F32, BF16 = jnp.float32, jnp.bfloat16
VMEM_LIMIT = 48 * 1024 * 1024
UNITS = 7


def dot(left, right, dims):
    return lax.dot_general(left, right, ((dims[:1], dims[1:]), ((), ())), preferred_element_type=F32)


def call(kernel, flops, moved, place, operands, grid, in_specs, out_specs, out_shape, into=(), outs=()):
    scalars = 1
    aliases = {}
    in_specs, operands = list(in_specs), list(operands)
    for array, out in zip(into, outs):
        if array is not None:
            aliases[scalars + len(operands)] = out
            operands.append(array)
            in_specs.append(pl.BlockSpec(memory_space=pl.ANY))
    return pl.pallas_call(
        kernel,
        grid_spec=pltpu.PrefetchScalarGridSpec(
            num_scalar_prefetch=scalars, grid=grid, in_specs=in_specs, out_specs=out_specs
        ),
        out_shape=out_shape,
        input_output_aliases=aliases,
        compiler_params=pltpu.CompilerParams(vmem_limit_bytes=VMEM_LIMIT),
        cost_estimate=pl.CostEstimate(flops=flops, bytes_accessed=moved, transcendentals=0),
    )(place, *operands)


def whole(shape):
    return pl.BlockSpec(shape, lambda i, s: (0,) * len(shape), pipeline_mode=pl.Buffered(1))


def chip_block(rows, columns, key, tiled=False):
    return pl.BlockSpec((rows, columns), lambda i, s: (s[0] ^ key, i if tiled else 0))


def pick_tile(size):
    return size // UNITS


def weight_units(weight, transposed):
    if transposed:
        return pl.BlockSpec((weight.shape[0] // UNITS, weight.shape[1]), lambda i, s: (i, 0))
    return pl.BlockSpec((weight.shape[0], weight.shape[1] // UNITS), lambda i, s: (0, i))


def own_partial(place, mine, other, weight, transposed):
    rows, depth = mine.shape
    hidden = weight.shape[0 if transposed else 1]
    dims = (1, 1) if transposed else (1, 0)

    def kernel(s, mine_ref, other_ref, weight_ref, out):
        out[pl.ds(pl.multiple_of(s[1] * rows, rows), rows), :] = dot(mine_ref[...], weight_ref[...], dims).astype(BF16)
        out[pl.ds(pl.multiple_of((1 - s[1]) * rows, rows), rows), :] = dot(
            other_ref[...], weight_ref[...], dims
        ).astype(BF16)

    return call(
        kernel,
        4 * rows * depth * hidden,
        4 * rows * (depth + hidden) + 2 * depth * hidden,
        place,
        [mine, other, weight],
        (UNITS,),
        [whole((rows, depth))] * 2 + [weight_units(weight, transposed)],
        pl.BlockSpec((2 * rows, hidden // UNITS), lambda i, s: (0, i)),
        jax.ShapeDtypeStruct((2 * rows, hidden), BF16),
    )


def partials(place, gathered, weight, transposed, keys, rows):
    depth = gathered.shape[1]
    hidden = weight.shape[0 if transposed else 1]
    dims = (1, 1) if transposed else (1, 0)
    count = len(keys)

    def kernel(s, *refs):
        weight_ref = refs[count]
        for tokens, out in zip(refs[:count], refs[count + 1 :]):
            out[...] = dot(tokens[...], weight_ref[...], dims).astype(BF16)

    return call(
        kernel,
        2 * count * rows * depth * hidden,
        2 * count * rows * (depth + hidden) + 2 * depth * hidden,
        place,
        [gathered] * count + [weight],
        (UNITS,),
        [chip_block(rows, depth, key) for key in keys] + [weight_units(weight, transposed)],
        [pl.BlockSpec((rows, hidden // UNITS), lambda i, s: (0, i))] * count,
        [jax.ShapeDtypeStruct((rows, hidden), BF16)] * count,
    )


def activate(place, terms, bias, key, into, tokens):
    rows, hidden = terms[0].shape
    width = hidden // UNITS

    def kernel(s, bias_ref, *refs):
        ins, (act_ref, slope_ref) = refs[: len(terms)], refs[-2:]
        pre = functools.reduce(jnp.add, [ref[...].astype(F32) for ref in ins]) + bias_ref[...]
        tangent = jnp.tanh(GELU_SCALE * (pre + GELU_CUBIC * pre * pre * pre))
        act_ref[...] = (0.5 * pre * (1.0 + tangent)).astype(BF16)
        slope_ref[...] = 0.5 * (1.0 + tangent) + 0.5 * pre * (1.0 - tangent * tangent) * GELU_SCALE * (
            1.0 + 3.0 * GELU_CUBIC * pre * pre
        )

    block = pl.BlockSpec((rows, width), lambda i, s: (0, i))
    return call(
        kernel,
        30 * rows * hidden,
        rows * hidden * (2 * len(terms) + 6),
        place,
        [bias, *terms],
        (UNITS,),
        [pl.BlockSpec((1, width), lambda i, s: (0, i))] + [block] * len(terms),
        [chip_block(rows, width, key, True), block],
        [jax.ShapeDtypeStruct((tokens, hidden), BF16), jax.ShapeDtypeStruct((rows, hidden), F32)],
        [into],
        [0],
    )


def differentiate(place, terms, slope, key, into, tokens):
    rows, hidden = slope.shape
    width = hidden // UNITS

    def kernel(s, slope_ref, *refs):
        ins, (grad_ref, sum_ref) = refs[: len(terms)], refs[-2:]
        grad = functools.reduce(jnp.add, [ref[...].astype(F32) for ref in ins]) * slope_ref[...]
        grad = grad.astype(BF16)
        grad_ref[...] = grad
        sum_ref[...] = jnp.sum(grad.astype(F32), axis=0, keepdims=True)

    block = pl.BlockSpec((rows, width), lambda i, s: (0, i))
    return call(
        kernel,
        8 * rows * hidden,
        rows * hidden * (2 * len(terms) + 6),
        place,
        [slope, *terms],
        (UNITS,),
        [block] * (1 + len(terms)),
        [chip_block(rows, width, key, True), pl.BlockSpec((1, width), lambda i, s: (0, i))],
        [jax.ShapeDtypeStruct((tokens, hidden), BF16), jax.ShapeDtypeStruct((1, hidden), F32)],
        [into],
        [0],
    )


def add_bf16(left, right):
    return (left.astype(F32) + right.astype(F32)).astype(BF16)


def weight_out_grad(place, act, grad, into, first, count):
    tokens, depth = grad.shape
    hidden = act.shape[1]
    width = hidden // UNITS
    tile = pick_tile(depth)

    def kernel(s, act_ref, grad_ref, *refs):
        turned = act_ref[...].T
        for at in range(0, depth, tile):
            refs[-1][:, at : at + tile] = dot(turned, grad_ref[:, at : at + tile], (1, 0))

    return call(
        kernel,
        2 * tokens * depth * width * count,
        2 * tokens * depth + 4 * depth * width * count,
        place,
        [act, grad],
        (count,),
        [pl.BlockSpec((tokens, width), lambda i, s: (0, first + i)), whole((tokens, depth))],
        pl.BlockSpec((width, depth), lambda i, s: (first + i, 0)),
        jax.ShapeDtypeStruct((hidden, depth), F32),
        [into],
        [0],
    )


def weight_in_grad(place, tok, grad, into, first, count):
    tokens, depth = tok.shape
    hidden = grad.shape[1]
    tile = pick_tile(depth)
    width = hidden // UNITS

    def kernel(s, tok_ref, grad_ref, *refs):
        turned = tok_ref[...].T
        for at in range(0, hidden, width):
            refs[-1][:, at : at + width] = dot(turned, grad_ref[:, at : at + width], (1, 0))

    return call(
        kernel,
        2 * tokens * tile * count * hidden,
        2 * tokens * (tile * count + hidden) + 4 * tile * count * hidden,
        place,
        [tok, grad],
        (count,),
        [pl.BlockSpec((tokens, tile), lambda j, s: (0, first + j)), whole((tokens, hidden))],
        pl.BlockSpec((tile, hidden), lambda j, s: (first + j, 0)),
        jax.ShapeDtypeStruct((depth, hidden), F32),
        [into],
        [0],
    )


def token_grad(place, grad, weight_in, keys, rows, first, count):
    depth, hidden = weight_in.shape
    tile = pick_tile(depth)
    half = rows // 2
    number = len(keys)

    def kernel(s, *refs):
        weight_ref = refs[number]
        for at in range(number):
            total = dot(refs[at][...], weight_ref[...], (1, 1)).astype(BF16)
            low = s[1] == 0
            refs[number + 1 + 2 * at][...] = jnp.where(low, total[:half], total[half:])
            refs[number + 2 + 2 * at][...] = jnp.where(low, total[half:], total[:half])

    outs = call(
        kernel,
        2 * number * rows * tile * count * hidden,
        2 * (number * rows * (tile * count + hidden) + tile * count * hidden),
        place,
        [grad] * number + [weight_in],
        (count,),
        [chip_block(rows, hidden, key) for key in keys] + [pl.BlockSpec((tile, hidden), lambda j, s: (first + j, 0))],
        [pl.BlockSpec((half, tile), lambda j, s: (0, j))] * (2 * number),
        [jax.ShapeDtypeStruct((half, tile * count), BF16)] * (2 * number),
    )
    return [tuple(outs[2 * at : 2 * at + 2]) for at in range(number)]


def after(value, *deps):
    return lax.optimization_barrier((value, *deps))[0]


def local(rows_of, cols_of, tokens, weight_in, bias_hidden, weight_out, out_grad):
    mine, depth = tokens.shape
    hidden = bias_hidden.shape[0]
    rows, everyone = 2 * mine, cols_of * mine
    bias = bias_hidden.reshape(1, hidden)
    steps = rows_of - 1
    me = lax.axis_index("col")
    place = jnp.stack([me // 2, me % 2]).astype(jnp.int32)
    others = sorted(range(1, cols_of // 2), key=lambda key: (-key.bit_count(), key))
    chunks = [("pre", 0), ("act", 0)] + [(kind, key) for kind in ("pre", "act") for key in others]
    total = len(chunks)

    def send(value, step):
        pairs = [(step - 1, step), (rows_of - step, rows_of - step - 1)]
        return lax.ppermute(value, "row", pairs)

    def swap(value, bits):
        return lax.ppermute(value, "col", [(i, i ^ bits) for i in range(cols_of)])

    chain = []

    def link(value):
        return after(value, chain[-1]) if chain else value

    own = {}
    got = {chunk: [None] * steps for chunk in chunks}
    held = {}
    slopes, sums, arrived = {}, {}, []

    def compute_own(kind, keys):
        source, weight = (tokens, weight_in) if kind == "pre" else (out_grad, weight_out)
        if keys == [0]:
            outs = [own_partial(place, link(source), held["pair", kind], weight, kind == "act")]
        else:
            outs = partials(place, link(held[kind]), weight, kind == "act", keys, rows)
        chain.append(outs[0])
        for key, out in zip(keys, outs):
            own[kind, key] = out

    def first_send(at):
        got[chunks[at]][0] = send(link(own[chunks[at]]), 1)

    def forward(at, step):
        payload = add_bf16(got[chunks[at]][step - 2], link(own[chunks[at]]))
        chain.append(payload)
        got[chunks[at]][step - 1] = send(payload, step)

    def finish(at):
        kind, key = chunks[at]
        terms = [link(own[kind, key])] + got[kind, key]
        if kind == "pre":
            held["activations"], slopes[key] = activate(place, terms, bias, key, held.get("activations"), everyone)
            chain.append(held["activations"])
        else:
            held["grads"], sums[key] = differentiate(place, terms, slopes[key], key, held.get("grads"), everyone)
            chain.append(held["grads"])

    def out_rows(first, count):
        held["out"] = weight_out_grad(
            place, link(held["activations"]), held["act"], held.get("out"), first, count
        )
        chain.append(held["out"])

    def in_rows(first, count):
        held["in"] = weight_in_grad(place, held["pre"], link(held["grads"]), held.get("in"), first, count)
        chain.append(held["in"])

    def tokens_of(keys, first=0, count=UNITS):
        parts = token_grad(place, link(held["grads"]), weight_in, keys, rows, first, count)
        chain.append(parts[0][0])
        return [(key, keep, swap(give, 1)) for key, (keep, give) in zip(keys, parts)]

    def deliver(parts):
        results = []
        for key, keep, given in parts:
            pair = add_bf16(link(keep), given)
            chain.append(pair)
            results.append(swap(pair, 2 * key) if key else pair)
        return results

    held["pair", "pre"], held["pair", "act"] = swap(tokens, 1), swap(out_grad, 1)
    held["pre"] = lax.all_gather(tokens, "col", axis=0, tiled=True)
    compute_own("pre", [0])
    first_send(0)
    compute_own("act", [0])
    first_send(1)
    early = None
    last = others[-1]
    for slot in range(total + steps - 1):
        if 3 <= slot + 1 < total:
            first_send(slot + 1)
        for step in range(2, steps + 1):
            if 0 <= slot - step + 2 < total:
                forward(slot - step + 2, step)
        if slot >= steps - 1:
            finish(slot - steps + 1)
        if slot == 1:
            compute_own("pre", others[:1])
            held["act"] = lax.all_gather(link(out_grad), "col", axis=0, tiled=True)
            first_send(2)
            compute_own("pre", others[1:])
        if slot == len(others):
            compute_own("act", others[:1])
        if slot == len(others) + 1:
            compute_own("act", others[1:])
        if slot == total + steps - 6:
            early = tokens_of([0])
        if slot == total + steps - 5:
            out_rows(0, 3)
            arrived += deliver(early)
        if slot == total + steps - 4:
            out_rows(3, 2)
        if slot == total + steps - 3:
            out_rows(5, UNITS - 5)
            early = tokens_of(others[:-1])
    arrived += deliver(early)
    front = UNITS // 2
    parts = [tokens_of([last], 0, front), tokens_of([last], front, UNITS - front)]
    in_rows(0, 1)
    sides = [deliver(parts[0])[0]]
    in_rows(1, 1)
    sides.append(deliver(parts[1])[0])
    in_rows(2, UNITS - 2)
    arrived.append(jnp.concatenate(sides, axis=1))
    grad_tokens = functools.reduce(jnp.add, [part.astype(F32) for part in arrived]).astype(BF16)

    sums = functools.reduce(jnp.add, [sums[key] for key in sorted(sums)]).reshape(hidden)
    for bit in [1 << i for i in range(rows_of.bit_length() - 1)]:
        sums = sums + lax.ppermute(sums, "row", [(i, i ^ bit) for i in range(rows_of)])
    grad_bias = sums * (1.0 / rows_of)
    return (grad_tokens, held["in"], grad_bias, held["out"])


def solution(mesh):
    placed = (P("col", "row"), P("row", "col"), P("col"), P("col", "row"), P("col", "row"))
    return jax.shard_map(
        functools.partial(local, mesh.shape["row"], mesh.shape["col"]),
        mesh=mesh,
        in_specs=placed,
        out_specs=(P("col", "row"), P("row", "col"), P("col"), P("col", "row")),
        check_vma=False,
    )
```

```python
import functools

import jax
import jax.numpy as jnp
from jax import lax
from jax.experimental import pallas as pl
from jax.experimental.pallas import tpu as pltpu
from jax.sharding import PartitionSpec as P

GELU_SCALE = 0.7978845608
GELU_CUBIC = 0.044715
F32, BF16 = jnp.float32, jnp.bfloat16
VMEM_LIMIT = 48 * 1024 * 1024
UNITS, AHEAD = 7, 3


def dot(left, right, dims):
    return lax.dot_general(left, right, ((dims[:1], dims[1:]), ((), ())), preferred_element_type=F32)


def call(kernel, flops, moved, place, operands, grid, in_specs, out_specs, out_shape, into=(), outs=(), scratch=()):
    scalars = 1
    aliases = {}
    in_specs, operands = list(in_specs), list(operands)
    for array, out in zip(into, outs):
        if array is not None:
            aliases[scalars + len(operands)] = out
            operands.append(array)
            in_specs.append(pl.BlockSpec(memory_space=pl.ANY))
    return pl.pallas_call(
        kernel,
        grid_spec=pltpu.PrefetchScalarGridSpec(
            num_scalar_prefetch=scalars,
            grid=grid,
            in_specs=in_specs,
            out_specs=out_specs,
            scratch_shapes=list(scratch),
        ),
        out_shape=out_shape,
        input_output_aliases=aliases,
        compiler_params=pltpu.CompilerParams(vmem_limit_bytes=VMEM_LIMIT),
        cost_estimate=pl.CostEstimate(flops=flops, bytes_accessed=moved, transcendentals=0),
    )(place, *operands)


def whole(shape):
    return pl.BlockSpec(shape, lambda i, s: (0,) * len(shape), pipeline_mode=pl.Buffered(1))


def chip_block(rows, columns, key):
    return pl.BlockSpec((rows, columns), lambda i, s: (s[0] ^ key, 0))


def streamed(place, blocks, weight, pieces, dims, flops, write, out_shape):
    axis, first, last = pieces
    size = weight.shape[axis] // UNITS
    count = last - first
    arrays = []
    for block in blocks:
        for array, _, _ in block:
            if not any(array is other for other in arrays):
                arrays.append(array)
    rows, depth = sum(part[2] for part in blocks[0]), blocks[0][0][0].shape[1]
    parts = sum(len(block) for block in blocks)
    shape = (size, weight.shape[1]) if axis == 0 else (weight.shape[0], size)

    def kernel(s, *refs):
        sources, weight_ref = refs[: len(arrays)], refs[len(arrays)]
        outs, (block_ref, piece_ref, block_sem, piece_sem) = refs[len(arrays) + 1 : -4], refs[-4:]

        def piece(at):
            where = pl.ds(pl.multiple_of((first + at) * size, size), size)
            source = weight_ref.at[where, :] if axis == 0 else weight_ref.at[:, where]
            return pltpu.make_async_copy(source, piece_ref.at[at], piece_sem.at[at])

        copies = []
        for at, block in enumerate(blocks):
            for array, start, length, into in block_rows(s, block):
                source = next(ref for ref, other in zip(sources, arrays) if other is array)
                copies.append(
                    pltpu.make_async_copy(
                        source.at[pl.ds(pl.multiple_of(start, 16), length), :],
                        block_ref.at[at, pl.ds(pl.multiple_of(into, 16), length), :],
                        block_sem.at[len(copies)],
                    )
                )
        piece(0).start()
        for copy in copies:
            copy.start()
        for at in range(1, min(AHEAD, count)):
            piece(at).start()
        for copy in copies:
            copy.wait()

        def step(at, carry):
            piece(at).wait()

            @pl.when(at + AHEAD < count)
            def _():
                piece(at + AHEAD).start()

            for block in range(len(blocks)):
                write(s, block, at, dot(block_ref[block], piece_ref[at], dims), outs)
            return carry

        lax.fori_loop(0, count, step, 0)

    def block_rows(s, block):
        into = 0
        for array, start, length in block:
            yield array, start(s), length, (into if len(block) == 1 else start_of(s, into // length) * length)
            into += length

    def start_of(s, at):
        return s[1] if at == 0 else 1 - s[1]

    moved = 2 * (len(blocks) * rows * depth + shape[0] * shape[1] * count)
    anywhere = pl.BlockSpec(memory_space=pl.ANY)
    return call(
        kernel,
        flops,
        moved,
        place,
        [*arrays, weight],
        (1,),
        [anywhere] * (len(arrays) + 1),
        [whole(out.shape) for out in out_shape],
        out_shape,
        scratch=[
            pltpu.VMEM((len(blocks), rows, depth), BF16),
            pltpu.VMEM((count, *shape), BF16),
            pltpu.SemaphoreType.DMA((parts,)),
            pltpu.SemaphoreType.DMA((count,)),
        ],
    )


def columns_of(at, size):
    return pl.ds(pl.multiple_of(at * size, size), size)


def partials(place, blocks, weight, transposed):
    hidden = weight.shape[0 if transposed else 1]
    rows = sum(part[2] for part in blocks[0])
    width = hidden // UNITS

    def write(s, block, at, product, outs):
        outs[block][:, columns_of(at, width)] = product.astype(BF16)

    return streamed(
        place,
        blocks,
        weight,
        (0 if transposed else 1, 0, UNITS),
        (1, 1) if transposed else (1, 0),
        2 * len(blocks) * rows * weight.size,
        write,
        [jax.ShapeDtypeStruct((rows, hidden), BF16)] * len(blocks),
    )


def token_grad(place, grad, weight_in, keys, rows, first, last):
    depth, hidden = weight_in.shape
    tile = depth // UNITS
    half = rows // 2

    def write(s, block, at, product, outs):
        product = product.astype(BF16)
        low = s[1] == 0
        place_of = (slice(block * half, (block + 1) * half), columns_of(at, tile))
        outs[0][place_of] = jnp.where(low, product[:half], product[half:])
        outs[1][place_of] = jnp.where(low, product[half:], product[:half])

    return streamed(
        place,
        [[(grad, lambda s, key=key: (s[0] ^ key) * rows, rows)] for key in keys],
        weight_in,
        (0, first, last),
        (1, 1),
        2 * len(keys) * rows * tile * (last - first) * hidden,
        write,
        [jax.ShapeDtypeStruct((len(keys) * half, tile * (last - first)), BF16)] * 2,
    )


def activate(place, terms, bias, key, into, tokens):
    rows, hidden = terms[0].shape

    def kernel(s, bias_ref, *refs):
        ins, (act_ref, slope_ref) = refs[: len(terms)], refs[-2:]
        pre = functools.reduce(jnp.add, [ref[...].astype(F32) for ref in ins]) + bias_ref[...]
        tangent = jnp.tanh(GELU_SCALE * (pre + GELU_CUBIC * pre * pre * pre))
        act_ref[...] = (0.5 * pre * (1.0 + tangent)).astype(BF16)
        slope_ref[...] = 0.5 * (1.0 + tangent) + 0.5 * pre * (1.0 - tangent * tangent) * GELU_SCALE * (
            1.0 + 3.0 * GELU_CUBIC * pre * pre
        )

    block = pl.BlockSpec((rows, hidden), lambda i, s: (0, 0))
    return call(
        kernel,
        30 * rows * hidden,
        rows * hidden * (2 * len(terms) + 6),
        place,
        [bias, *terms],
        (1,),
        [pl.BlockSpec((1, hidden), lambda i, s: (0, 0))] + [block] * len(terms),
        [chip_block(rows, hidden, key), block],
        [jax.ShapeDtypeStruct((tokens, hidden), BF16), jax.ShapeDtypeStruct((rows, hidden), F32)],
        [into],
        [0],
    )


def differentiate(place, terms, slope, key, into, tokens):
    rows, hidden = slope.shape

    def kernel(s, slope_ref, *refs):
        ins, (grad_ref, sum_ref) = refs[: len(terms)], refs[-2:]
        grad = functools.reduce(jnp.add, [ref[...].astype(F32) for ref in ins]) * slope_ref[...]
        grad = grad.astype(BF16)
        grad_ref[...] = grad
        sum_ref[...] = jnp.sum(grad.astype(F32), axis=0, keepdims=True)

    block = pl.BlockSpec((rows, hidden), lambda i, s: (0, 0))
    return call(
        kernel,
        8 * rows * hidden,
        rows * hidden * (2 * len(terms) + 6),
        place,
        [slope, *terms],
        (1,),
        [block] * (1 + len(terms)),
        [chip_block(rows, hidden, key), pl.BlockSpec((1, hidden), lambda i, s: (0, 0))],
        [jax.ShapeDtypeStruct((tokens, hidden), BF16), jax.ShapeDtypeStruct((1, hidden), F32)],
        [into],
        [0],
    )


def add_bf16(left, right):
    return (left.astype(F32) + right.astype(F32)).astype(BF16)


def weight_out_grad(place, act, grad, into, first, count):
    tokens, depth = grad.shape
    hidden = act.shape[1]
    tile, width = depth // UNITS, hidden // UNITS

    def kernel(s, act_ref, grad_ref, *refs):
        out, turned = refs[-2:]

        @pl.when(pl.program_id(0) == 0)
        def _():
            for at in range(0, hidden, width):
                turned[at : at + width, :] = act_ref[:, at : at + width].T

        for at in range(0, hidden, hidden // 2):
            out[at : at + hidden // 2, :] = dot(turned[at : at + hidden // 2, :], grad_ref[...], (1, 0))

    return call(
        kernel,
        2 * tokens * tile * count * hidden,
        2 * tokens * (tile * count + hidden) + 4 * tile * count * hidden,
        place,
        [act, grad],
        (count,),
        [whole((tokens, hidden)), pl.BlockSpec((tokens, tile), lambda j, s: (0, first + j))],
        pl.BlockSpec((hidden, tile), lambda j, s: (0, first + j)),
        jax.ShapeDtypeStruct((hidden, depth), F32),
        [into],
        [0],
        [pltpu.VMEM((hidden, tokens), BF16)],
    )


def weight_in_grad(place, tok, grad, into, first, count):
    tokens, depth = tok.shape
    hidden = grad.shape[1]
    tile, width = depth // UNITS, hidden // 2

    def kernel(s, tok_ref, grad_ref, *refs):
        turned = tok_ref[...].T
        for at in range(0, hidden, width):
            refs[-1][:, at : at + width] = dot(turned, grad_ref[:, at : at + width], (1, 0))

    return call(
        kernel,
        2 * tokens * tile * count * hidden,
        2 * tokens * (tile * count + hidden) + 4 * tile * count * hidden,
        place,
        [tok, grad],
        (count,),
        [pl.BlockSpec((tokens, tile), lambda j, s: (0, first + j)), whole((tokens, hidden))],
        pl.BlockSpec((tile, hidden), lambda j, s: (first + j, 0)),
        jax.ShapeDtypeStruct((depth, hidden), F32),
        [into],
        [0],
    )


def after(value, *deps):
    return lax.optimization_barrier((value, *deps))[0]


def local(rows_of, cols_of, tokens, weight_in, bias_hidden, weight_out, out_grad):
    mine, depth = tokens.shape
    hidden = bias_hidden.shape[0]
    rows, everyone = 2 * mine, cols_of * mine
    bias = bias_hidden.reshape(1, hidden)
    steps = rows_of - 1
    me = lax.axis_index("col")
    place = jnp.stack([me // 2, me % 2]).astype(jnp.int32)
    others = sorted(range(1, cols_of // 2), key=lambda key: (-key.bit_count(), key))
    chunks = [("pre", 0), ("act", 0)] + [(kind, key) for kind in ("pre", "act") for key in others]
    total = len(chunks)

    def send(value, step):
        pairs = [(step - 1, step), (rows_of - step, rows_of - step - 1)]
        return lax.ppermute(value, "row", pairs)

    def swap(value, bits):
        return lax.ppermute(value, "col", [(i, i ^ bits) for i in range(cols_of)])

    chain = []

    def link(value):
        return after(value, chain[-1]) if chain else value

    own, ahead = {}, {}
    got = {chunk: [None] * steps for chunk in chunks}
    held = {}
    slopes, sums, arrived = {}, {}, []

    def compute_own(kind, keys):
        source, weight = (tokens, weight_in) if kind == "pre" else (out_grad, weight_out)
        if keys == [0]:
            first = lambda s: 0
            blocks = [[(link(source), first, mine), (held["pair", kind], first, mine)]]
        else:
            gathered = link(held[kind])
            blocks = [[(gathered, lambda s, key=key: (s[0] ^ key) * rows, rows)] for key in keys]
        outs = partials(place, blocks, weight, kind == "act")
        chain.append(outs[0])
        for key, out in zip(keys, outs):
            own[kind, key] = out

    def first_send(at):
        got[chunks[at]][0] = send(link(own[chunks[at]]), 1)

    def forward(at, step):
        chunk = chunks[at]
        payload = add_bf16(got[chunk][step - 2], link(own[chunk]))
        chain.append(payload)
        ahead.setdefault(chunk, payload)
        got[chunk][step - 1] = send(payload, step)

    def finish(at):
        kind, key = chunk = chunks[at]
        terms = [link(ahead[chunk])] + got[chunk][1:]
        if kind == "pre":
            held["activations"], slopes[key] = activate(place, terms, bias, key, held.get("activations"), everyone)
            chain.append(held["activations"])
        else:
            held["grads"], sums[key] = differentiate(place, terms, slopes[key], key, held.get("grads"), everyone)
            chain.append(held["grads"])

    def out_columns(first, count):
        held["out"] = weight_out_grad(
            place, link(held["activations"]), held["act"], held.get("out"), first, count
        )
        chain.append(held["out"])

    def in_rows(first, count):
        held["in"] = weight_in_grad(place, held["pre"], link(held["grads"]), held.get("in"), first, count)
        chain.append(held["in"])

    def tokens_of(keys, first, last):
        keep, give = token_grad(place, link(held["grads"]), weight_in, keys, rows, first, last)
        chain.append(keep)
        return keys, keep, swap(give, 1)

    def deliver(parts):
        keys, keep, given = parts
        results = []
        for at, key in enumerate(keys):
            block = slice(at * mine, (at + 1) * mine)
            pair = add_bf16(link(keep)[block], given[block])
            results.append(swap(pair, 2 * key) if key else pair)
        chain.append(pair)
        return results

    held["pair", "pre"], held["pair", "act"] = swap(tokens, 1), swap(out_grad, 1)
    held["pre"] = lax.all_gather(tokens, "col", axis=0, tiled=True)
    held["act"] = lax.all_gather(after(out_grad, held["pair", "pre"]), "col", axis=0, tiled=True)
    compute_own("pre", [0])
    first_send(0)
    compute_own("act", [0])
    first_send(1)
    end = total + steps - 1
    for slot in range(end):
        if 3 <= slot + 1 < total:
            first_send(slot + 1)
        late = slot == 2
        order = range(steps, 1, -1) if late else range(2, steps + 1)
        if late and slot >= steps - 1:
            finish(slot - steps + 1)
        for step in order:
            if 0 <= slot - step + 2 < total:
                forward(slot - step + 2, step)
        if slot == 1:
            compute_own("pre", others)
            first_send(2)
        if not late and slot >= steps - 1:
            finish(slot - steps + 1)
        if slot == len(others):
            compute_own("act", others)
        if slot == end - 4:
            out_columns(0, 4)
        if slot == end - 3:
            early = tokens_of([0] + others[:-2], 0, UNITS)
        if slot == end - 2:
            out_columns(4, UNITS - 4)
    arrived += deliver(early)
    front = UNITS // 2
    parts = [tokens_of(others[-2:], 0, front), tokens_of(others[-2:], front, UNITS)]
    sides = [deliver(parts[0])]
    in_rows(0, 2)
    sides.append(deliver(parts[1]))
    in_rows(2, UNITS - 2)
    arrived += [jnp.concatenate(halves, axis=1) for halves in zip(*sides)]
    grad_tokens = functools.reduce(jnp.add, [part.astype(F32) for part in arrived]).astype(BF16)

    sums = functools.reduce(jnp.add, [sums[key] for key in sorted(sums)]).reshape(hidden)
    for bit in [1 << i for i in range(rows_of.bit_length() - 1)]:
        sums = sums + lax.ppermute(sums, "row", [(i, i ^ bit) for i in range(rows_of)])
    grad_bias = sums * (1.0 / rows_of)
    return (grad_tokens, held["in"], grad_bias, held["out"])


def solution(mesh):
    placed = (P("col", "row"), P("row", "col"), P("col"), P("col", "row"), P("col", "row"))
    return jax.shard_map(
        functools.partial(local, mesh.shape["row"], mesh.shape["col"]),
        mesh=mesh,
        in_specs=placed,
        out_specs=(P("col", "row"), P("row", "col"), P("col"), P("col", "row")),
        check_vma=False,
    )
```

```python
import functools

import jax
import jax.numpy as jnp
from jax import lax
from jax.experimental import pallas as pl
from jax.experimental.pallas import tpu as pltpu
from jax.sharding import PartitionSpec as P

GELU_SCALE = 0.7978845608
GELU_CUBIC = 0.044715
F32, BF16 = jnp.float32, jnp.bfloat16
MIB = 1024 * 1024
UNITS, AHEAD = 7, 3


def dot(left, right, dims):
    return lax.dot_general(left, right, ((dims[:1], dims[1:]), ((), ())), preferred_element_type=F32)


def call(kernel, flops, moved, place, operands, grid, in_specs, out_specs, out_shape, into=(), outs=(), scratch=(), vmem=48):
    scalars = 1
    aliases = {}
    in_specs, operands = list(in_specs), list(operands)
    for array, out in zip(into, outs):
        if array is not None:
            aliases[scalars + len(operands)] = out
            operands.append(array)
            in_specs.append(pl.BlockSpec(memory_space=pl.ANY))
    return pl.pallas_call(
        kernel,
        grid_spec=pltpu.PrefetchScalarGridSpec(
            num_scalar_prefetch=scalars,
            grid=grid,
            in_specs=in_specs,
            out_specs=out_specs,
            scratch_shapes=list(scratch),
        ),
        out_shape=out_shape,
        input_output_aliases=aliases,
        compiler_params=pltpu.CompilerParams(vmem_limit_bytes=vmem * MIB),
        cost_estimate=pl.CostEstimate(flops=flops, bytes_accessed=moved, transcendentals=0),
    )(place, *operands)


def whole(shape):
    return pl.BlockSpec(shape, lambda i, s: (0,) * len(shape), pipeline_mode=pl.Buffered(1))


def chip_block(rows, columns, key):
    return pl.BlockSpec((rows, columns), lambda i, s: (s[0] ^ key, 0))


def streamed(place, blocks, weight, pieces, dims, flops, write, out_shape, vmem=48):
    axis, first, last = pieces
    size = weight.shape[axis] // UNITS
    count = last - first
    arrays = []
    for block in blocks:
        for array, _, _ in block:
            if not any(array is other for other in arrays):
                arrays.append(array)
    total, depth = sum(part[2] for block in blocks for part in block), blocks[0][0][0].shape[1]
    parts = sum(len(block) for block in blocks)
    shape = (size, weight.shape[1]) if axis == 0 else (weight.shape[0], size)

    def kernel(s, *refs):
        sources, weight_ref = refs[: len(arrays)], refs[len(arrays)]
        outs, (block_ref, piece_ref, block_sem, piece_sem) = refs[len(arrays) + 1 : -4], refs[-4:]

        def piece(at):
            where = pl.ds(pl.multiple_of((first + at) * size, size), size)
            source = weight_ref.at[where, :] if axis == 0 else weight_ref.at[:, where]
            return pltpu.make_async_copy(source, piece_ref.at[at], piece_sem.at[at])

        copies, top = [], 0
        for block in blocks:
            for at, (array, start, length) in enumerate(block):
                into = top if len(block) == 1 else top + (s[1] if at == 0 else 1 - s[1]) * length
                source = next(ref for ref, other in zip(sources, arrays) if other is array)
                copies.append(
                    pltpu.make_async_copy(
                        source.at[pl.ds(pl.multiple_of(start(s), 16), length), :],
                        block_ref.at[pl.ds(pl.multiple_of(into, 16), length), :],
                        block_sem.at[len(copies)],
                    )
                )
            top += sum(part[2] for part in block)
        piece(0).start()
        for copy in copies:
            copy.start()
        for at in range(1, min(AHEAD, count)):
            piece(at).start()
        for copy in copies:
            copy.wait()

        def step(at, carry):
            piece(at).wait()

            @pl.when(at + AHEAD < count)
            def _():
                piece(at + AHEAD).start()

            write(s, at, dot(block_ref[...], piece_ref[at], dims), outs)
            return carry

        lax.fori_loop(0, count, step, 0)

    moved = 2 * (total * depth + shape[0] * shape[1] * count)
    anywhere = pl.BlockSpec(memory_space=pl.ANY)
    return call(
        kernel,
        flops,
        moved,
        place,
        [*arrays, weight],
        (1,),
        [anywhere] * (len(arrays) + 1),
        [whole(out.shape) for out in out_shape],
        out_shape,
        scratch=[
            pltpu.VMEM((total, depth), BF16),
            pltpu.VMEM((count, *shape), BF16),
            pltpu.SemaphoreType.DMA((parts,)),
            pltpu.SemaphoreType.DMA((count,)),
        ],
        vmem=vmem,
    )


def columns_of(at, size):
    return pl.ds(pl.multiple_of(at * size, size), size)


def partials(place, blocks, weight, transposed, vmem):
    hidden = weight.shape[0 if transposed else 1]
    rows = sum(part[2] for part in blocks[0])
    width = hidden // UNITS

    def write(s, at, product, outs):
        for block, out in enumerate(outs):
            out[:, columns_of(at, width)] = product[block * rows : (block + 1) * rows].astype(BF16)

    return streamed(
        place,
        blocks,
        weight,
        (0 if transposed else 1, 0, UNITS),
        (1, 1) if transposed else (1, 0),
        2 * len(blocks) * rows * weight.size,
        write,
        [jax.ShapeDtypeStruct((rows, hidden), BF16)] * len(blocks),
        vmem,
    )


def token_grad(place, grad, weight_in, keys, rows, first, last):
    depth, hidden = weight_in.shape
    tile = depth // UNITS
    half = rows // 2

    def write(s, at, product, outs):
        low = s[1] == 0
        for block in range(len(keys)):
            first_half, second_half = (
                product[(2 * block + side) * half : (2 * block + side + 1) * half].astype(BF16) for side in range(2)
            )
            to = (slice(block * half, (block + 1) * half), columns_of(at, tile))
            outs[0][to] = jnp.where(low, first_half, second_half)
            outs[1][to] = jnp.where(low, second_half, first_half)

    return streamed(
        place,
        [[(grad, lambda s, key=key: (s[0] ^ key) * rows, rows)] for key in keys],
        weight_in,
        (0, first, last),
        (1, 1),
        2 * len(keys) * rows * tile * (last - first) * hidden,
        write,
        [jax.ShapeDtypeStruct((len(keys) * half, tile * (last - first)), BF16)] * 2,
    )


def activate(place, terms, bias, key, into, tokens):
    rows, hidden = terms[0].shape

    def kernel(s, bias_ref, *refs):
        ins, (act_ref, slope_ref) = refs[: len(terms)], refs[-2:]
        pre = functools.reduce(jnp.add, [ref[...].astype(F32) for ref in ins]) + bias_ref[...]
        tangent = jnp.tanh(GELU_SCALE * (pre + GELU_CUBIC * pre * pre * pre))
        act_ref[...] = (0.5 * pre * (1.0 + tangent)).astype(BF16)
        slope_ref[...] = 0.5 * (1.0 + tangent) + 0.5 * pre * (1.0 - tangent * tangent) * GELU_SCALE * (
            1.0 + 3.0 * GELU_CUBIC * pre * pre
        )

    block = pl.BlockSpec((rows, hidden), lambda i, s: (0, 0))
    return call(
        kernel,
        30 * rows * hidden,
        rows * hidden * (2 * len(terms) + 6),
        place,
        [bias, *terms],
        (1,),
        [pl.BlockSpec((1, hidden), lambda i, s: (0, 0))] + [block] * len(terms),
        [chip_block(rows, hidden, key), block],
        [jax.ShapeDtypeStruct((tokens, hidden), BF16), jax.ShapeDtypeStruct((rows, hidden), F32)],
        [into],
        [0],
    )


def differentiate(place, terms, slope, key, into, tokens):
    rows, hidden = slope.shape

    def kernel(s, slope_ref, *refs):
        ins, (grad_ref, sum_ref) = refs[: len(terms)], refs[-2:]
        grad = functools.reduce(jnp.add, [ref[...].astype(F32) for ref in ins]) * slope_ref[...]
        grad = grad.astype(BF16)
        grad_ref[...] = grad
        sum_ref[...] = jnp.sum(grad.astype(F32), axis=0, keepdims=True)

    block = pl.BlockSpec((rows, hidden), lambda i, s: (0, 0))
    return call(
        kernel,
        8 * rows * hidden,
        rows * hidden * (2 * len(terms) + 6),
        place,
        [slope, *terms],
        (1,),
        [block] * (1 + len(terms)),
        [chip_block(rows, hidden, key), pl.BlockSpec((1, hidden), lambda i, s: (0, 0))],
        [jax.ShapeDtypeStruct((tokens, hidden), BF16), jax.ShapeDtypeStruct((1, hidden), F32)],
        [into],
        [0],
    )


def add_bf16(left, right):
    return (left.astype(F32) + right.astype(F32)).astype(BF16)


def weight_out_grad(place, act, grad, into, first, count):
    tokens, depth = grad.shape
    hidden = act.shape[1]
    tile, width = depth // UNITS, hidden // UNITS

    def kernel(s, act_ref, grad_ref, *refs):
        out, turned = refs[-2:]

        @pl.when(pl.program_id(0) == 0)
        def _():
            for at in range(0, hidden, width):
                turned[at : at + width, :] = act_ref[:, at : at + width].T

        for at in range(0, hidden, hidden // 2):
            out[at : at + hidden // 2, :] = dot(turned[at : at + hidden // 2, :], grad_ref[...], (1, 0))

    return call(
        kernel,
        2 * tokens * tile * count * hidden,
        2 * tokens * (tile * count + hidden) + 4 * tile * count * hidden,
        place,
        [act, grad],
        (count,),
        [whole((tokens, hidden)), pl.BlockSpec((tokens, tile), lambda j, s: (0, first + j))],
        pl.BlockSpec((hidden, tile), lambda j, s: (0, first + j)),
        jax.ShapeDtypeStruct((hidden, depth), F32),
        [into],
        [0],
        [pltpu.VMEM((hidden, tokens), BF16)],
    )


def weight_in_grad(place, tok, grad, into, first, count):
    tokens, depth = tok.shape
    hidden = grad.shape[1]
    tile, width = depth // UNITS, hidden // 2

    def kernel(s, tok_ref, grad_ref, *refs):
        turned = tok_ref[...].T
        for at in range(0, hidden, width):
            refs[-1][:, at : at + width] = dot(turned, grad_ref[:, at : at + width], (1, 0))

    return call(
        kernel,
        2 * tokens * tile * count * hidden,
        2 * tokens * (tile * count + hidden) + 4 * tile * count * hidden,
        place,
        [tok, grad],
        (count,),
        [pl.BlockSpec((tokens, tile), lambda j, s: (0, first + j)), whole((tokens, hidden))],
        pl.BlockSpec((tile, hidden), lambda j, s: (first + j, 0)),
        jax.ShapeDtypeStruct((depth, hidden), F32),
        [into],
        [0],
    )


def after(value, *deps):
    return lax.optimization_barrier((value, *deps))[0]


def local(rows_of, cols_of, tokens, weight_in, bias_hidden, weight_out, out_grad):
    mine, depth = tokens.shape
    hidden = bias_hidden.shape[0]
    rows, everyone = 2 * mine, cols_of * mine
    bias = bias_hidden.reshape(1, hidden)
    steps = rows_of - 1
    me = lax.axis_index("col")
    place = jnp.stack([me // 2, me % 2]).astype(jnp.int32)
    others = sorted(range(1, cols_of // 2), key=lambda key: (-key.bit_count(), key))
    chunks = [("pre", 0), ("act", 0)] + [(kind, key) for kind in ("pre", "act") for key in others]
    total = len(chunks)

    def send(value, step):
        pairs = [(step - 1, step), (rows_of - step, rows_of - step - 1)]
        return lax.ppermute(value, "row", pairs)

    def swap(value, bits):
        return lax.ppermute(value, "col", [(i, i ^ bits) for i in range(cols_of)])

    chain = []

    def link(value):
        return after(value, chain[-1]) if chain else value

    own, ahead = {}, {}
    got = {chunk: [None] * steps for chunk in chunks}
    held = {}
    slopes, sums, arrived = {}, {}, []

    def compute_own(kind, keys):
        source, weight = (tokens, weight_in) if kind == "pre" else (out_grad, weight_out)
        if keys == [0]:
            first = lambda s: 0
            blocks = [[(link(source), first, mine), (held["pair", kind], first, mine)]]
        else:
            gathered = link(held[kind])
            blocks = [[(gathered, lambda s, key=key: (s[0] ^ key) * rows, rows)] for key in keys]
        outs = partials(place, blocks, weight, kind == "act", 58 if keys == others[:1] else 48)
        chain.append(outs[0])
        for key, out in zip(keys, outs):
            own[kind, key] = out

    def first_send(at):
        got[chunks[at]][0] = send(link(own[chunks[at]]), 1)

    def forward(at, step):
        chunk = chunks[at]
        payload = add_bf16(got[chunk][step - 2], link(own[chunk]))
        chain.append(payload)
        ahead.setdefault(chunk, payload)
        got[chunk][step - 1] = send(payload, step)

    def finish(at):
        kind, key = chunk = chunks[at]
        terms = [link(ahead[chunk])] + got[chunk][1:]
        if kind == "pre":
            held["activations"], slopes[key] = activate(place, terms, bias, key, held.get("activations"), everyone)
            chain.append(held["activations"])
        else:
            held["grads"], sums[key] = differentiate(place, terms, slopes[key], key, held.get("grads"), everyone)
            chain.append(held["grads"])

    def out_columns(first, count):
        held["out"] = weight_out_grad(
            place, link(held["activations"]), held["act"], held.get("out"), first, count
        )
        chain.append(held["out"])

    def in_rows(first, count):
        held["in"] = weight_in_grad(place, held["pre"], link(held["grads"]), held.get("in"), first, count)
        chain.append(held["in"])

    def tokens_of(keys, first, last):
        keep, give = token_grad(place, link(held["grads"]), weight_in, keys, rows, first, last)
        chain.append(keep)
        return keys, keep, give

    def exchange(parts):
        keys, keep, give = parts
        return keys, keep, swap(link(give), 1)

    def deliver(parts):
        keys, keep, given = parts
        results = []
        for at, key in enumerate(keys):
            block = slice(at * mine, (at + 1) * mine)
            pair = add_bf16(link(keep)[block], given[block])
            results.append(swap(pair, 2 * key) if key else pair)
        chain.append(pair)
        return results

    held["pair", "pre"], held["pair", "act"] = swap(tokens, 1), swap(out_grad, 1)
    held["pre"] = lax.all_gather(tokens, "col", axis=0, tiled=True)
    held["act"] = lax.all_gather(after(out_grad, held["pair", "pre"]), "col", axis=0, tiled=True)
    compute_own("pre", [0])
    first_send(0)
    compute_own("act", [0])
    first_send(1)
    end = total + steps - 1
    for slot in range(end):
        if 3 <= slot + 1 < total:
            first_send(slot + 1)
        late = slot == 2
        if late and slot >= steps - 1:
            finish(slot - steps + 1)
        for step in range(steps, 1, -1) if late else range(2, steps + 1):
            if 0 <= slot - step + 2 < total:
                forward(slot - step + 2, step)
            if step == 2 and slot == len(others):
                compute_own("act", others)
        if slot == 1:
            compute_own("pre", others[:1])
            first_send(2)
            compute_own("pre", others[1:])
        if not late and slot >= steps - 1:
            finish(slot - steps + 1)
        if slot == end - 4:
            out_columns(0, 4)
        if slot == end - 3:
            out_columns(4, UNITS - 4)
        if slot == end - 2:
            early = tokens_of([0] + others[:-1], 0, UNITS)
    early = exchange(early)
    front = UNITS // 2
    parts = [exchange(tokens_of(others[-1:], 0, front)), exchange(tokens_of(others[-1:], front, UNITS))]
    sums = link(functools.reduce(jnp.add, [sums[key] for key in sorted(sums)]).reshape(hidden))
    levels = [1 << i for i in range(rows_of.bit_length() - 1)]
    sums = sums + lax.ppermute(sums, "row", [(i, i ^ levels[0]) for i in range(rows_of)])
    arrived += deliver(early)
    sides = [deliver(part) for part in parts]
    in_rows(0, UNITS)
    sums = link(sums)
    for bit in levels[1:]:
        sums = sums + lax.ppermute(sums, "row", [(i, i ^ bit) for i in range(rows_of)])
    grad_bias = sums * (1.0 / rows_of)
    arrived += [jnp.concatenate(halves, axis=1) for halves in zip(*sides)]
    grad_tokens = functools.reduce(jnp.add, [part.astype(F32) for part in arrived]).astype(BF16)

    return (grad_tokens, held["in"], grad_bias, held["out"])


def solution(mesh):
    placed = (P("col", "row"), P("row", "col"), P("col"), P("col", "row"), P("col", "row"))
    return jax.shard_map(
        functools.partial(local, mesh.shape["row"], mesh.shape["col"]),
        mesh=mesh,
        in_specs=placed,
        out_specs=(P("col", "row"), P("row", "col"), P("col"), P("col", "row")),
        check_vma=False,
    )
```

```python
import functools

import jax
import jax.numpy as jnp
from jax import lax
from jax.experimental import pallas as pl
from jax.experimental.pallas import tpu as pltpu
from jax.sharding import PartitionSpec as P

GELU_SCALE = 0.7978845608
GELU_CUBIC = 0.044715
F32, BF16 = jnp.float32, jnp.bfloat16
VMEM_LIMIT = 48 * 1024 * 1024
UNITS, AHEAD = 7, 3


def dot(left, right, dims):
    return lax.dot_general(left, right, ((dims[:1], dims[1:]), ((), ())), preferred_element_type=F32)


def call(kernel, flops, moved, place, operands, grid, in_specs, out_specs, out_shape, into=(), outs=(), scratch=()):
    scalars = 1
    aliases = {}
    in_specs, operands = list(in_specs), list(operands)
    for array, out in zip(into, outs):
        if array is not None:
            aliases[scalars + len(operands)] = out
            operands.append(array)
            in_specs.append(pl.BlockSpec(memory_space=pl.ANY))
    return pl.pallas_call(
        kernel,
        grid_spec=pltpu.PrefetchScalarGridSpec(
            num_scalar_prefetch=scalars,
            grid=grid,
            in_specs=in_specs,
            out_specs=out_specs,
            scratch_shapes=list(scratch),
        ),
        out_shape=out_shape,
        input_output_aliases=aliases,
        compiler_params=pltpu.CompilerParams(vmem_limit_bytes=VMEM_LIMIT),
        cost_estimate=pl.CostEstimate(flops=flops, bytes_accessed=moved, transcendentals=0),
    )(place, *operands)


def whole(shape):
    return pl.BlockSpec(shape, lambda i, s: (0,) * len(shape), pipeline_mode=pl.Buffered(1))


def chip_block(rows, columns, key):
    return pl.BlockSpec((rows, columns), lambda i, s: (s[0] ^ key, 0))


def streamed(place, blocks, weight, pieces, dims, flops, write, out_shape):
    axis, first, last = pieces
    size = weight.shape[axis] // UNITS
    count = last - first
    arrays = []
    for block in blocks:
        for array, _, _, _ in block:
            if not any(array is other for other in arrays):
                arrays.append(array)
    total, depth = sum(part[2] for block in blocks for part in block), blocks[0][0][0].shape[1]
    parts = sum(len(block) for block in blocks)
    shape = (size, weight.shape[1]) if axis == 0 else (weight.shape[0], size)

    def kernel(s, *refs):
        sources, weight_ref = refs[: len(arrays)], refs[len(arrays)]
        outs, (block_ref, piece_ref, block_sem, piece_sem) = refs[len(arrays) + 1 : -4], refs[-4:]

        def piece(at):
            where = pl.ds(pl.multiple_of((first + at) * size, size), size)
            source = weight_ref.at[where, :] if axis == 0 else weight_ref.at[:, where]
            return pltpu.make_async_copy(source, piece_ref.at[at], piece_sem.at[at])

        copies, top = [], 0
        for block in blocks:
            for array, start, length, into in block:
                source = next(ref for ref, other in zip(sources, arrays) if other is array)
                copies.append(
                    pltpu.make_async_copy(
                        source.at[pl.ds(pl.multiple_of(start(s), 16), length), :],
                        block_ref.at[pl.ds(pl.multiple_of(top + into(s), 16), length), :],
                        block_sem.at[len(copies)],
                    )
                )
            top += sum(part[2] for part in block)
        piece(0).start()
        for copy in copies:
            copy.start()
        for at in range(1, min(AHEAD, count)):
            piece(at).start()
        for copy in copies:
            copy.wait()

        def step(at, carry):
            piece(at).wait()

            @pl.when(at + AHEAD < count)
            def _():
                piece(at + AHEAD).start()

            write(s, at, dot(block_ref[...], piece_ref[at], dims), outs)
            return carry

        lax.fori_loop(0, count, step, 0)

    moved = 2 * (total * depth + shape[0] * shape[1] * count)
    anywhere = pl.BlockSpec(memory_space=pl.ANY)
    return call(
        kernel,
        flops,
        moved,
        place,
        [*arrays, weight],
        (1,),
        [anywhere] * (len(arrays) + 1),
        [whole(out.shape) for out in out_shape],
        out_shape,
        scratch=[
            pltpu.VMEM((total, depth), BF16),
            pltpu.VMEM((count, *shape), BF16),
            pltpu.SemaphoreType.DMA((parts,)),
            pltpu.SemaphoreType.DMA((count,)),
        ],
    )


def zero(s):
    return 0


def columns_of(at, size):
    return pl.ds(pl.multiple_of(at * size, size), size)


def partials(place, blocks, weight, transposed):
    hidden = weight.shape[0 if transposed else 1]
    rows = sum(part[2] for part in blocks[0])
    width = hidden // UNITS

    def write(s, at, product, outs):
        for block, out in enumerate(outs):
            out[:, columns_of(at, width)] = product[block * rows : (block + 1) * rows].astype(BF16)

    return streamed(
        place,
        blocks,
        weight,
        (0 if transposed else 1, 0, UNITS),
        (1, 1) if transposed else (1, 0),
        2 * len(blocks) * rows * weight.size,
        write,
        [jax.ShapeDtypeStruct((rows, hidden), BF16)] * len(blocks),
    )


def token_grad(place, grad, weight_in, keys, rows, first, last):
    depth, hidden = weight_in.shape
    tile = depth // UNITS
    half = rows // 2

    def write(s, at, product, outs):
        low = s[1] == 0
        for block in range(len(keys)):
            first_half, second_half = (
                product[(2 * block + side) * half : (2 * block + side + 1) * half].astype(BF16) for side in range(2)
            )
            to = (slice(block * half, (block + 1) * half), columns_of(at, tile))
            outs[0][to] = jnp.where(low, first_half, second_half)
            outs[1][to] = jnp.where(low, second_half, first_half)

    return streamed(
        place,
        [[(grad, lambda s, key=key: (s[0] ^ key) * rows, rows, zero)] for key in keys],
        weight_in,
        (0, first, last),
        (1, 1),
        2 * len(keys) * rows * tile * (last - first) * hidden,
        write,
        [jax.ShapeDtypeStruct((len(keys) * half, tile * (last - first)), BF16)] * 2,
    )


def activate(place, terms, bias, key, into, tokens):
    rows, hidden = terms[0].shape

    def kernel(s, bias_ref, *refs):
        ins, (act_ref, slope_ref) = refs[: len(terms)], refs[-2:]
        pre = functools.reduce(jnp.add, [ref[...].astype(F32) for ref in ins]) + bias_ref[...]
        tangent = jnp.tanh(GELU_SCALE * (pre + GELU_CUBIC * pre * pre * pre))
        act_ref[...] = (0.5 * pre * (1.0 + tangent)).astype(BF16)
        slope_ref[...] = 0.5 * (1.0 + tangent) + 0.5 * pre * (1.0 - tangent * tangent) * GELU_SCALE * (
            1.0 + 3.0 * GELU_CUBIC * pre * pre
        )

    block = pl.BlockSpec((rows, hidden), lambda i, s: (0, 0))
    return call(
        kernel,
        30 * rows * hidden,
        rows * hidden * (2 * len(terms) + 6),
        place,
        [bias, *terms],
        (1,),
        [pl.BlockSpec((1, hidden), lambda i, s: (0, 0))] + [block] * len(terms),
        [chip_block(rows, hidden, key), block],
        [jax.ShapeDtypeStruct((tokens, hidden), BF16), jax.ShapeDtypeStruct((rows, hidden), F32)],
        [into],
        [0],
    )


def differentiate(place, terms, slope, key, into, tokens):
    rows, hidden = slope.shape

    def kernel(s, slope_ref, *refs):
        ins, (grad_ref, sum_ref) = refs[: len(terms)], refs[-2:]
        grad = functools.reduce(jnp.add, [ref[...].astype(F32) for ref in ins]) * slope_ref[...]
        grad = grad.astype(BF16)
        grad_ref[...] = grad
        sum_ref[...] = jnp.sum(grad.astype(F32), axis=0, keepdims=True)

    block = pl.BlockSpec((rows, hidden), lambda i, s: (0, 0))
    return call(
        kernel,
        8 * rows * hidden,
        rows * hidden * (2 * len(terms) + 6),
        place,
        [slope, *terms],
        (1,),
        [block] * (1 + len(terms)),
        [chip_block(rows, hidden, key), pl.BlockSpec((1, hidden), lambda i, s: (0, 0))],
        [jax.ShapeDtypeStruct((tokens, hidden), BF16), jax.ShapeDtypeStruct((1, hidden), F32)],
        [into],
        [0],
    )


def add_bf16(left, right):
    return (left.astype(F32) + right.astype(F32)).astype(BF16)


def weight_out_grad(place, act, grad, into, first, count):
    tokens, depth = grad.shape
    hidden = act.shape[1]
    tile, width = depth // UNITS, hidden // UNITS

    def kernel(s, act_ref, grad_ref, *refs):
        out, turned = refs[-2:]

        @pl.when(pl.program_id(0) == 0)
        def _():
            for at in range(0, hidden, width):
                turned[at : at + width, :] = act_ref[:, at : at + width].T

        for at in range(0, hidden, hidden // 2):
            out[at : at + hidden // 2, :] = dot(turned[at : at + hidden // 2, :], grad_ref[...], (1, 0))

    return call(
        kernel,
        2 * tokens * tile * count * hidden,
        2 * tokens * (tile * count + hidden) + 4 * tile * count * hidden,
        place,
        [act, grad],
        (count,),
        [whole((tokens, hidden)), pl.BlockSpec((tokens, tile), lambda j, s: (0, first + j))],
        pl.BlockSpec((hidden, tile), lambda j, s: (0, first + j)),
        jax.ShapeDtypeStruct((hidden, depth), F32),
        [into],
        [0],
        [pltpu.VMEM((hidden, tokens), BF16)],
    )


def weight_in_grad(place, tok, grad, into, first, count):
    tokens, depth = tok.shape
    hidden = grad.shape[1]
    tile, width = depth // UNITS, hidden // 2

    def kernel(s, tok_ref, grad_ref, *refs):
        turned = tok_ref[...].T
        for at in range(0, hidden, width):
            refs[-1][:, at : at + width] = dot(turned, grad_ref[:, at : at + width], (1, 0))

    return call(
        kernel,
        2 * tokens * tile * count * hidden // 16,
        (2 * tokens * (tile * count + hidden) + 4 * tile * count * hidden) // 16,
        place,
        [tok, grad],
        (count,),
        [pl.BlockSpec((tokens, tile), lambda j, s: (0, first + j)), whole((tokens, hidden))],
        pl.BlockSpec((tile, hidden), lambda j, s: (first + j, 0)),
        jax.ShapeDtypeStruct((depth, hidden), F32),
        [into],
        [0],
    )


def add_early(place, left, right):
    def kernel(s, left_ref, right_ref, out):
        out[...] = left_ref[...].astype(F32) + right_ref[...].astype(F32)

    return call(
        kernel,
        left.size,
        8 * left.size,
        place,
        [left, right],
        (1,),
        [whole(left.shape)] * 2,
        whole(left.shape),
        jax.ShapeDtypeStruct(left.shape, F32),
    )


def after(value, *deps):
    return lax.optimization_barrier((value, *deps))[0]


def local(rows_of, cols_of, tokens, weight_in, bias_hidden, weight_out, out_grad):
    mine, depth = tokens.shape
    hidden = bias_hidden.shape[0]
    rows, everyone = 2 * mine, cols_of * mine
    bias = bias_hidden.reshape(1, hidden)
    steps = rows_of - 1
    me = lax.axis_index("col")
    place = jnp.stack([me // 2, me % 2]).astype(jnp.int32)
    lead = 1
    others = [lead] + sorted(range(2, cols_of // 2), key=lambda key: (-key.bit_count(), key))
    chunks = [("pre", 0), ("act", 0)] + [(kind, key) for kind in ("pre", "act") for key in others]
    total = len(chunks)

    def send(value, step):
        pairs = [(step - 1, step), (rows_of - step, rows_of - step - 1)]
        return lax.ppermute(value, "row", pairs)

    def swap(value, bits):
        return lax.ppermute(value, "col", [(i, i ^ bits) for i in range(cols_of)])

    chain = []

    def link(value):
        return after(value, chain[-1]) if chain else value

    own, ahead = {}, {}
    got = {chunk: [None] * steps for chunk in chunks}
    held = {}
    slopes, sums, arrived = {}, {}, []

    def compute_own(kind, keys):
        weight = weight_in if kind == "pre" else weight_out
        blocks = []
        for key in keys:
            if (kind, key) in held:
                near, far = link(held[kind, key]), held[kind, key, "far"]
                blocks.append([(near, zero, mine, lambda s: s[1] * mine), (far, zero, mine, lambda s: (1 - s[1]) * mine)])
            else:
                blocks.append([(held[kind, "all"], lambda s, key=key: (s[0] ^ key) * rows, rows, zero)])
        if keys[0] not in (0, lead):
            held[kind, "all"] = link(held[kind, "all"])
            blocks = [[(held[kind, "all"], *part[1:]) for part in block] for block in blocks]
        outs = partials(place, blocks, weight, kind == "act")
        chain.append(outs[0])
        for key, out in zip(keys, outs):
            own[kind, key] = out

    def first_send(at):
        got[chunks[at]][0] = send(link(own[chunks[at]]), 1)

    def forward(at, step):
        chunk = chunks[at]
        payload = add_bf16(got[chunk][step - 2], link(own[chunk]))
        chain.append(payload)
        ahead.setdefault(chunk, payload)
        got[chunk][step - 1] = send(payload, step)

    def finish(at):
        kind, key = chunk = chunks[at]
        terms = [link(ahead[chunk])] + got[chunk][1:]
        if kind == "pre":
            held["activations"], slopes[key] = activate(place, terms, bias, key, held.get("activations"), everyone)
            chain.append(held["activations"])
        else:
            held["grads"], sums[key] = differentiate(place, terms, slopes[key], key, held.get("grads"), everyone)
            chain.append(held["grads"])

    def out_columns(first, count):
        held["out"] = weight_out_grad(
            place, link(held["activations"]), held["cotangents"], held.get("out"), first, count
        )
        chain.append(held["out"])

    def in_rows(first, count):
        held["in"] = weight_in_grad(place, held["tokens"], link(held["grads"]), held.get("in"), first, count)
        chain.append(held["in"])

    def tokens_of(keys, first, last):
        keep, give = token_grad(place, link(held["grads"]), weight_in, keys, rows, first, last)
        chain.append(keep)
        return keys, keep, give

    def exchange(parts):
        keys, keep, give = parts
        return keys, keep, swap(link(give), 1)

    def deliver(parts):
        keys, keep, given = parts
        results = []
        for at, key in enumerate(keys):
            block = slice(at * mine, (at + 1) * mine)
            pair = add_bf16(link(keep)[block], given[block])
            results.append(swap(pair, 2 * key) if key else pair)
        chain.append(pair)
        return results

    held["pre", 0], held["act", 0] = tokens, out_grad
    held["pre", 0, "far"], held["act", 0, "far"] = swap(tokens, 1), swap(out_grad, 1)
    held["pre", "all"] = lax.all_gather(tokens, "col", axis=0, tiled=True)
    held["act", "all"] = lax.all_gather(after(out_grad, held["pre", 0, "far"]), "col", axis=0, tiled=True)
    held["tokens"], held["cotangents"] = held["pre", "all"], held["act", "all"]
    compute_own("pre", [0])
    first_send(0)
    held["pre", lead] = swap(link(tokens), 2 * lead)
    compute_own("act", [0])
    first_send(1)
    held["act", lead] = swap(link(out_grad), 2 * lead)
    end = total + steps - 1
    for slot in range(end):
        if slot and slot + 1 < total:
            first_send(slot + 1)
        for step in range(2, steps + 1):
            if 0 <= slot - step + 2 < total:
                forward(slot - step + 2, step)
        if slot == 0:
            held["pre", lead, "far"] = swap(link(held["pre", lead]), 1)
            compute_own("pre", [lead])
        if slot == 1:
            compute_own("pre", others[1:])
            held["act", lead, "far"] = swap(link(held["act", lead]), 1)
        if slot >= steps - 1:
            finish(slot - steps + 1)
        if slot == 2:
            compute_own("act", [lead])
        if slot == len(others) + 1:
            compute_own("act", others[1:])
        if slot == end - 4:
            out_columns(0, 3)
        if slot == end - 3:
            first = tokens_of([0] + others[:-2], 0, UNITS)
        if slot == end - 2:
            first = exchange(first)
            second = tokens_of(others[-2:-1], 0, UNITS)
            arrived += deliver(first)
            second = exchange(second)
            out_columns(3, UNITS - 3)
    arrived += deliver(second)
    head = add_early(place, link(arrived[0]), arrived[1])
    chain.append(head)
    third = exchange(tokens_of(others[-1:], 0, UNITS))
    sums = link(functools.reduce(jnp.add, [sums[key] for key in sorted(sums)]).reshape(hidden))
    levels = [1 << i for i in range(rows_of.bit_length() - 1)]
    sums = sums + lax.ppermute(sums, "row", [(i, i ^ levels[0]) for i in range(rows_of)])
    arrived += deliver(third)
    in_rows(0, UNITS)
    sums = link(sums)
    for bit in levels[1:]:
        sums = sums + lax.ppermute(sums, "row", [(i, i ^ bit) for i in range(rows_of)])
    grad_bias = sums * (1.0 / rows_of)
    grad_tokens = functools.reduce(jnp.add, [part.astype(F32) for part in arrived[2:]], head).astype(BF16)
    return (grad_tokens, held["in"], grad_bias, held["out"])


def solution(mesh):
    placed = (P("col", "row"), P("row", "col"), P("col"), P("col", "row"), P("col", "row"))
    return jax.shard_map(
        functools.partial(local, mesh.shape["row"], mesh.shape["col"]),
        mesh=mesh,
        in_specs=placed,
        out_specs=(P("col", "row"), P("row", "col"), P("col"), P("col", "row")),
        check_vma=False,
    )
```

```python
import functools

import jax
import jax.numpy as jnp
from jax import lax
from jax.experimental import pallas as pl
from jax.experimental.pallas import tpu as pltpu
from jax.sharding import PartitionSpec as P

GELU_SCALE = 0.7978845608
GELU_CUBIC = 0.044715
F32, BF16 = jnp.float32, jnp.bfloat16
VMEM_LIMIT = 48 * 1024 * 1024
UNITS, AHEAD = 7, 3


def dot(left, right, dims):
    return lax.dot_general(left, right, ((dims[:1], dims[1:]), ((), ())), preferred_element_type=F32)


def call(kernel, flops, moved, place, operands, grid, in_specs, out_specs, out_shape, into=(), outs=(), scratch=()):
    scalars = 1
    aliases = {}
    in_specs, operands = list(in_specs), list(operands)
    for array, out in zip(into, outs):
        if array is not None:
            aliases[scalars + len(operands)] = out
            operands.append(array)
            in_specs.append(pl.BlockSpec(memory_space=pl.ANY))
    return pl.pallas_call(
        kernel,
        grid_spec=pltpu.PrefetchScalarGridSpec(
            num_scalar_prefetch=scalars,
            grid=grid,
            in_specs=in_specs,
            out_specs=out_specs,
            scratch_shapes=list(scratch),
        ),
        out_shape=out_shape,
        input_output_aliases=aliases,
        compiler_params=pltpu.CompilerParams(vmem_limit_bytes=VMEM_LIMIT),
        cost_estimate=pl.CostEstimate(flops=flops, bytes_accessed=moved, transcendentals=0),
    )(place, *operands)


def whole(shape):
    return pl.BlockSpec(shape, lambda i, s: (0,) * len(shape), pipeline_mode=pl.Buffered(1))


def chip_block(rows, columns, key):
    return pl.BlockSpec((rows, columns), lambda i, s: (s[0] ^ key, 0))


def streamed(place, blocks, weight, pieces, dims, flops, write, out_shape):
    axis, first, last = pieces
    size = weight.shape[axis] // UNITS
    count = last - first
    arrays = []
    for block in blocks:
        for array, _, _, _ in block:
            if not any(array is other for other in arrays):
                arrays.append(array)
    total, depth = sum(part[2] for block in blocks for part in block), blocks[0][0][0].shape[1]
    parts = sum(len(block) for block in blocks)
    shape = (size, weight.shape[1]) if axis == 0 else (weight.shape[0], size)

    def kernel(s, *refs):
        sources, weight_ref = refs[: len(arrays)], refs[len(arrays)]
        outs, (block_ref, piece_ref, block_sem, piece_sem) = refs[len(arrays) + 1 : -4], refs[-4:]

        def piece(at):
            where = pl.ds(pl.multiple_of((first + at) * size, size), size)
            source = weight_ref.at[where, :] if axis == 0 else weight_ref.at[:, where]
            return pltpu.make_async_copy(source, piece_ref.at[at], piece_sem.at[at])

        copies, top = [], 0
        for block in blocks:
            for array, start, length, into in block:
                source = next(ref for ref, other in zip(sources, arrays) if other is array)
                copies.append(
                    pltpu.make_async_copy(
                        source.at[pl.ds(pl.multiple_of(start(s), 16), length), :],
                        block_ref.at[pl.ds(pl.multiple_of(top + into(s), 16), length), :],
                        block_sem.at[len(copies)],
                    )
                )
            top += sum(part[2] for part in block)
        piece(0).start()
        for copy in copies:
            copy.start()
        for at in range(1, min(AHEAD, count)):
            piece(at).start()
        for copy in copies:
            copy.wait()

        def step(at, carry):
            piece(at).wait()

            @pl.when(at + AHEAD < count)
            def _():
                piece(at + AHEAD).start()

            write(s, at, dot(block_ref[...], piece_ref[at], dims), outs)
            return carry

        lax.fori_loop(0, count, step, 0)

    moved = 2 * (total * depth + shape[0] * shape[1] * count)
    anywhere = pl.BlockSpec(memory_space=pl.ANY)
    return call(
        kernel,
        flops,
        moved,
        place,
        [*arrays, weight],
        (1,),
        [anywhere] * (len(arrays) + 1),
        [whole(out.shape) for out in out_shape],
        out_shape,
        scratch=[
            pltpu.VMEM((total, depth), BF16),
            pltpu.VMEM((count, *shape), BF16),
            pltpu.SemaphoreType.DMA((parts,)),
            pltpu.SemaphoreType.DMA((count,)),
        ],
    )


def zero(s):
    return 0


def columns_of(at, size):
    return pl.ds(pl.multiple_of(at * size, size), size)


def partials(place, blocks, weight, transposed):
    hidden = weight.shape[0 if transposed else 1]
    rows = sum(part[2] for part in blocks[0])
    width = hidden // UNITS

    def write(s, at, product, outs):
        for block, out in enumerate(outs):
            out[:, columns_of(at, width)] = product[block * rows : (block + 1) * rows].astype(BF16)

    return streamed(
        place,
        blocks,
        weight,
        (0 if transposed else 1, 0, UNITS),
        (1, 1) if transposed else (1, 0),
        2 * len(blocks) * rows * weight.size,
        write,
        [jax.ShapeDtypeStruct((rows, hidden), BF16)] * len(blocks),
    )


def token_grad(place, grad, weight_in, keys, rows, first, last):
    depth, hidden = weight_in.shape
    tile = depth // UNITS
    half = rows // 2

    def write(s, at, product, outs):
        low = s[1] == 0
        for block in range(len(keys)):
            first_half, second_half = (
                product[(2 * block + side) * half : (2 * block + side + 1) * half].astype(BF16) for side in range(2)
            )
            to = (slice(block * half, (block + 1) * half), columns_of(at, tile))
            outs[0][to] = jnp.where(low, first_half, second_half)
            outs[1][to] = jnp.where(low, second_half, first_half)

    return streamed(
        place,
        [[(grad, lambda s, key=key: (s[0] ^ key) * rows, rows, zero)] for key in keys],
        weight_in,
        (0, first, last),
        (1, 1),
        2 * len(keys) * rows * tile * (last - first) * hidden,
        write,
        [jax.ShapeDtypeStruct((len(keys) * half, tile * (last - first)), BF16)] * 2,
    )


def activate(place, terms, bias, key, into, tokens):
    rows, hidden = terms[0].shape

    def kernel(s, bias_ref, *refs):
        ins, (act_ref, slope_ref) = refs[: len(terms)], refs[-2:]
        pre = functools.reduce(jnp.add, [ref[...].astype(F32) for ref in ins]) + bias_ref[...]
        tangent = jnp.tanh(GELU_SCALE * (pre + GELU_CUBIC * pre * pre * pre))
        act_ref[...] = (0.5 * pre * (1.0 + tangent)).astype(BF16)
        slope_ref[...] = 0.5 * (1.0 + tangent) + 0.5 * pre * (1.0 - tangent * tangent) * GELU_SCALE * (
            1.0 + 3.0 * GELU_CUBIC * pre * pre
        )

    block = pl.BlockSpec((rows, hidden), lambda i, s: (0, 0))
    return call(
        kernel,
        30 * rows * hidden,
        rows * hidden * (2 * len(terms) + 6),
        place,
        [bias, *terms],
        (1,),
        [pl.BlockSpec((1, hidden), lambda i, s: (0, 0))] + [block] * len(terms),
        [chip_block(rows, hidden, key), block],
        [jax.ShapeDtypeStruct((tokens, hidden), BF16), jax.ShapeDtypeStruct((rows, hidden), F32)],
        [into],
        [0],
    )


def differentiate(place, terms, slope, key, into, tokens):
    rows, hidden = slope.shape

    def kernel(s, slope_ref, *refs):
        ins, (grad_ref, sum_ref) = refs[: len(terms)], refs[-2:]
        grad = functools.reduce(jnp.add, [ref[...].astype(F32) for ref in ins]) * slope_ref[...]
        grad = grad.astype(BF16)
        grad_ref[...] = grad
        sum_ref[...] = jnp.sum(grad.astype(F32), axis=0, keepdims=True)

    block = pl.BlockSpec((rows, hidden), lambda i, s: (0, 0))
    return call(
        kernel,
        8 * rows * hidden,
        rows * hidden * (2 * len(terms) + 6),
        place,
        [slope, *terms],
        (1,),
        [block] * (1 + len(terms)),
        [chip_block(rows, hidden, key), pl.BlockSpec((1, hidden), lambda i, s: (0, 0))],
        [jax.ShapeDtypeStruct((tokens, hidden), BF16), jax.ShapeDtypeStruct((1, hidden), F32)],
        [into],
        [0],
    )


def add_bf16(left, right):
    return (left.astype(F32) + right.astype(F32)).astype(BF16)


def weight_out_grad(place, act, grad, into, first, count):
    tokens, depth = grad.shape
    hidden = act.shape[1]
    tile, width = depth // UNITS, hidden // UNITS

    def kernel(s, act_ref, grad_ref, *refs):
        out, turned = refs[-2:]

        @pl.when(pl.program_id(0) == 0)
        def _():
            for at in range(0, hidden, width):
                turned[at : at + width, :] = act_ref[:, at : at + width].T

        for at in range(0, hidden, hidden // 2):
            out[at : at + hidden // 2, :] = dot(turned[at : at + hidden // 2, :], grad_ref[...], (1, 0))

    return call(
        kernel,
        2 * tokens * tile * count * hidden,
        2 * tokens * (tile * count + hidden) + 4 * tile * count * hidden,
        place,
        [act, grad],
        (count,),
        [whole((tokens, hidden)), pl.BlockSpec((tokens, tile), lambda j, s: (0, first + j))],
        pl.BlockSpec((hidden, tile), lambda j, s: (0, first + j)),
        jax.ShapeDtypeStruct((hidden, depth), F32),
        [into],
        [0],
        [pltpu.VMEM((hidden, tokens), BF16)],
    )


def weight_in_grad(place, tok, grad, into, first, count):
    tokens, depth = tok.shape
    hidden = grad.shape[1]
    tile, width = depth // UNITS, hidden // 2

    def kernel(s, tok_ref, grad_ref, *refs):
        turned = tok_ref[...].T
        for at in range(0, hidden, width):
            refs[-1][:, at : at + width] = dot(turned, grad_ref[:, at : at + width], (1, 0))

    return call(
        kernel,
        2 * tokens * tile * count * hidden,
        2 * tokens * (tile * count + hidden) + 4 * tile * count * hidden,
        place,
        [tok, grad],
        (count,),
        [pl.BlockSpec((tokens, tile), lambda j, s: (0, first + j)), whole((tokens, hidden))],
        pl.BlockSpec((tile, hidden), lambda j, s: (first + j, 0)),
        jax.ShapeDtypeStruct((depth, hidden), F32),
        [into],
        [0],
    )


def add_early(place, left, right):
    def kernel(s, left_ref, right_ref, out):
        out[...] = left_ref[...].astype(F32) + right_ref[...].astype(F32)

    return call(
        kernel,
        left.size,
        8 * left.size,
        place,
        [left, right],
        (1,),
        [whole(left.shape)] * 2,
        whole(left.shape),
        jax.ShapeDtypeStruct(left.shape, F32),
    )


def after(value, *deps):
    return lax.optimization_barrier((value, *deps))[0]


def local(rows_of, cols_of, tokens, weight_in, bias_hidden, weight_out, out_grad):
    mine, depth = tokens.shape
    hidden = bias_hidden.shape[0]
    rows, everyone = 2 * mine, cols_of * mine
    bias = bias_hidden.reshape(1, hidden)
    steps = rows_of - 1
    me = lax.axis_index("col")
    place = jnp.stack([me // 2, me % 2]).astype(jnp.int32)
    others = sorted(range(1, cols_of // 2), key=lambda key: (-key.bit_count(), key))
    chunks = [("pre", 0), ("act", 0)] + [(kind, key) for kind in ("pre", "act") for key in others]
    total = len(chunks)

    def send(value, step):
        pairs = [(step - 1, step), (rows_of - step, rows_of - step - 1)]
        return lax.ppermute(value, "row", pairs)

    def swap(value, bits):
        return lax.ppermute(value, "col", [(i, i ^ bits) for i in range(cols_of)])

    chain = []

    def link(value):
        return after(value, chain[-1]) if chain else value

    own, ahead = {}, {}
    got = {chunk: [None] * steps for chunk in chunks}
    held = {}
    slopes, sums, arrived = {}, {}, []

    def compute_own(kind, keys):
        source, weight = (tokens, weight_in) if kind == "pre" else (out_grad, weight_out)
        if keys == [0]:
            far = held[kind, "far"]
            blocks = [[(link(source), zero, mine, lambda s: s[1] * mine), (far, zero, mine, lambda s: (1 - s[1]) * mine)]]
        else:
            gathered = link(held[kind])
            blocks = [[(gathered, lambda s, key=key: (s[0] ^ key) * rows, rows, zero)] for key in keys]
        outs = partials(place, blocks, weight, kind == "act")
        chain.append(outs[0])
        for key, out in zip(keys, outs):
            own[kind, key] = out

    def first_send(at):
        got[chunks[at]][0] = send(link(own[chunks[at]]), 1)

    def forward(at, step):
        chunk = chunks[at]
        payload = add_bf16(got[chunk][step - 2], link(own[chunk]))
        chain.append(payload)
        ahead.setdefault(chunk, payload)
        got[chunk][step - 1] = send(payload, step)

    def finish(at):
        kind, key = chunk = chunks[at]
        terms = [link(ahead[chunk])] + got[chunk][1:]
        if kind == "pre":
            held["activations"], slopes[key] = activate(place, terms, bias, key, held.get("activations"), everyone)
            chain.append(held["activations"])
        else:
            held["grads"], sums[key] = differentiate(place, terms, slopes[key], key, held.get("grads"), everyone)
            chain.append(held["grads"])

    def out_columns(first, count):
        held["out"] = weight_out_grad(
            place, link(held["activations"]), held["act"], held.get("out"), first, count
        )
        chain.append(held["out"])

    def in_rows(first, count):
        held["in"] = weight_in_grad(place, held["pre"], link(held["grads"]), held.get("in"), first, count)
        chain.append(held["in"])

    def tokens_of(keys, first, last):
        keep, give = token_grad(place, link(held["grads"]), weight_in, keys, rows, first, last)
        chain.append(keep)
        return keys, keep, give

    def exchange(parts):
        keys, keep, give = parts
        return keys, keep, swap(link(give), 1)

    def deliver(parts):
        keys, keep, given = parts
        results = []
        for at, key in enumerate(keys):
            block = slice(at * mine, (at + 1) * mine)
            pair = add_bf16(link(keep)[block], given[block])
            results.append(swap(pair, 2 * key) if key else pair)
        chain.append(pair)
        return results

    held["pre", "far"], held["act", "far"] = swap(tokens, 1), swap(out_grad, 1)
    held["pre"] = lax.all_gather(tokens, "col", axis=0, tiled=True)
    held["act"] = lax.all_gather(after(out_grad, held["pre", "far"]), "col", axis=0, tiled=True)
    compute_own("pre", [0])
    first_send(0)
    compute_own("act", [0])
    first_send(1)
    end = total + steps - 1
    for slot in range(end):
        if 3 <= slot + 1 < total:
            first_send(slot + 1)
        late = slot == 2
        if late and slot >= steps - 1:
            finish(slot - steps + 1)
        for step in range(steps, 1, -1) if late else range(2, steps + 1):
            if 0 <= slot - step + 2 < total:
                forward(slot - step + 2, step)
            if step == 2 and slot == len(others):
                compute_own("act", others)
        if slot == 1:
            compute_own("pre", others)
            first_send(2)
        if not late and slot >= steps - 1:
            finish(slot - steps + 1)
        if slot == end - 4:
            out_columns(0, 3)
        if slot == end - 3:
            first = tokens_of([0] + others[:-2], 0, UNITS)
        if slot == end - 2:
            arrived += deliver(exchange(first))
            out_columns(3, UNITS - 3)
    head = add_early(place, link(arrived[0]), arrived[1])
    chain.append(head)
    levels = [1 << i for i in range(rows_of.bit_length() - 1)]
    sums = link(functools.reduce(jnp.add, [sums[key] for key in sorted(sums)]).reshape(hidden))
    sums = sums + lax.ppermute(sums, "row", [(i, i ^ levels[0]) for i in range(rows_of)])
    last = exchange(tokens_of(others[-2:], 0, UNITS))
    sums = link(sums)
    for bit in levels[1:]:
        sums = sums + lax.ppermute(sums, "row", [(i, i ^ bit) for i in range(rows_of)])
    arrived += deliver(last)
    in_rows(0, UNITS)
    grad_bias = sums * (1.0 / rows_of)
    grad_tokens = functools.reduce(jnp.add, [part.astype(F32) for part in arrived[2:]], head).astype(BF16)
    return (grad_tokens, held["in"], grad_bias, held["out"])


def solution(mesh):
    placed = (P("col", "row"), P("row", "col"), P("col"), P("col", "row"), P("col", "row"))
    return jax.shard_map(
        functools.partial(local, mesh.shape["row"], mesh.shape["col"]),
        mesh=mesh,
        in_specs=placed,
        out_specs=(P("col", "row"), P("row", "col"), P("col"), P("col", "row")),
        check_vma=False,
    )
```

```python
import functools

import jax
import jax.numpy as jnp
from jax import lax
from jax.experimental import pallas as pl
from jax.experimental.pallas import tpu as pltpu
from jax.sharding import PartitionSpec as P

GELU_SCALE = 0.7978845608
GELU_CUBIC = 0.044715
F32, BF16 = jnp.float32, jnp.bfloat16
VMEM_LIMIT = 48 * 1024 * 1024
UNITS, AHEAD = 7, 3


def dot(left, right, dims):
    return lax.dot_general(left, right, ((dims[:1], dims[1:]), ((), ())), preferred_element_type=F32)


def call(kernel, flops, moved, place, operands, grid, in_specs, out_specs, out_shape, into=(), outs=(), scratch=()):
    scalars = 1
    aliases = {}
    in_specs, operands = list(in_specs), list(operands)
    for array, out in zip(into, outs):
        if array is not None:
            aliases[scalars + len(operands)] = out
            operands.append(array)
            in_specs.append(pl.BlockSpec(memory_space=pl.ANY))
    return pl.pallas_call(
        kernel,
        grid_spec=pltpu.PrefetchScalarGridSpec(
            num_scalar_prefetch=scalars,
            grid=grid,
            in_specs=in_specs,
            out_specs=out_specs,
            scratch_shapes=list(scratch),
        ),
        out_shape=out_shape,
        input_output_aliases=aliases,
        compiler_params=pltpu.CompilerParams(vmem_limit_bytes=VMEM_LIMIT),
        cost_estimate=pl.CostEstimate(flops=flops, bytes_accessed=moved, transcendentals=0),
    )(place, *operands)


def whole(shape):
    return pl.BlockSpec(shape, lambda i, s: (0,) * len(shape), pipeline_mode=pl.Buffered(1))


def chip_block(rows, columns, key):
    return pl.BlockSpec((rows, columns), lambda i, s: (s[0] ^ key, 0))


def streamed(place, blocks, weight, pieces, dims, flops, write, out_shape, shrink=1):
    axis, first, last = pieces
    size = weight.shape[axis] // UNITS
    count = last - first
    arrays = []
    for block in blocks:
        for array, _, _, _ in block:
            if not any(array is other for other in arrays):
                arrays.append(array)
    total, depth = sum(part[2] for block in blocks for part in block), blocks[0][0][0].shape[1]
    parts = sum(len(block) for block in blocks)
    shape = (size, weight.shape[1]) if axis == 0 else (weight.shape[0], size)

    def kernel(s, *refs):
        sources, weight_ref = refs[: len(arrays)], refs[len(arrays)]
        outs, (block_ref, piece_ref, block_sem, piece_sem) = refs[len(arrays) + 1 : -4], refs[-4:]

        def piece(at):
            where = pl.ds(pl.multiple_of((first + at) * size, size), size)
            source = weight_ref.at[where, :] if axis == 0 else weight_ref.at[:, where]
            return pltpu.make_async_copy(source, piece_ref.at[at], piece_sem.at[at])

        copies, top = [], 0
        for block in blocks:
            for array, start, length, into in block:
                source = next(ref for ref, other in zip(sources, arrays) if other is array)
                copies.append(
                    pltpu.make_async_copy(
                        source.at[pl.ds(pl.multiple_of(start(s), 16), length), :],
                        block_ref.at[pl.ds(pl.multiple_of(top + into(s), 16), length), :],
                        block_sem.at[len(copies)],
                    )
                )
            top += sum(part[2] for part in block)
        piece(0).start()
        for copy in copies:
            copy.start()
        for at in range(1, min(AHEAD, count)):
            piece(at).start()
        for copy in copies:
            copy.wait()

        def step(at, carry):
            piece(at).wait()

            @pl.when(at + AHEAD < count)
            def _():
                piece(at + AHEAD).start()

            write(s, at, dot(block_ref[...], piece_ref[at], dims), outs)
            return carry

        lax.fori_loop(0, count, step, 0)

    moved = 2 * (total * depth + shape[0] * shape[1] * count)
    anywhere = pl.BlockSpec(memory_space=pl.ANY)
    return call(
        kernel,
        flops // shrink,
        moved // shrink,
        place,
        [*arrays, weight],
        (1,),
        [anywhere] * (len(arrays) + 1),
        [whole(out.shape) for out in out_shape],
        out_shape,
        scratch=[
            pltpu.VMEM((total, depth), BF16),
            pltpu.VMEM((count, *shape), BF16),
            pltpu.SemaphoreType.DMA((parts,)),
            pltpu.SemaphoreType.DMA((count,)),
        ],
    )


def zero(s):
    return 0


def columns_of(at, size):
    return pl.ds(pl.multiple_of(at * size, size), size)


def partials(place, blocks, weight, transposed):
    hidden = weight.shape[0 if transposed else 1]
    rows = sum(part[2] for part in blocks[0])
    width = hidden // UNITS

    def write(s, at, product, outs):
        for block, out in enumerate(outs):
            out[:, columns_of(at, width)] = product[block * rows : (block + 1) * rows].astype(BF16)

    return streamed(
        place,
        blocks,
        weight,
        (0 if transposed else 1, 0, UNITS),
        (1, 1) if transposed else (1, 0),
        2 * len(blocks) * rows * weight.size,
        write,
        [jax.ShapeDtypeStruct((rows, hidden), BF16)] * len(blocks),
        64,
    )


def token_grad(place, grad, weight_in, keys, rows, first, last):
    depth, hidden = weight_in.shape
    tile = depth // UNITS
    half = rows // 2

    def write(s, at, product, outs):
        low = s[1] == 0
        for block in range(len(keys)):
            first_half, second_half = (
                product[(2 * block + side) * half : (2 * block + side + 1) * half].astype(BF16) for side in range(2)
            )
            to = (slice(block * half, (block + 1) * half), columns_of(at, tile))
            outs[0][to] = jnp.where(low, first_half, second_half)
            outs[1][to] = jnp.where(low, second_half, first_half)

    return streamed(
        place,
        [[(grad, lambda s, key=key: (s[0] ^ key) * rows, rows, zero)] for key in keys],
        weight_in,
        (0, first, last),
        (1, 1),
        2 * len(keys) * rows * tile * (last - first) * hidden,
        write,
        [jax.ShapeDtypeStruct((len(keys) * half, tile * (last - first)), BF16)] * 2,
    )


def activate(place, terms, bias, key, into, tokens):
    rows, hidden = terms[0].shape

    def kernel(s, bias_ref, *refs):
        ins, (act_ref, slope_ref) = refs[: len(terms)], refs[-2:]
        pre = functools.reduce(jnp.add, [ref[...].astype(F32) for ref in ins]) + bias_ref[...]
        tangent = jnp.tanh(GELU_SCALE * (pre + GELU_CUBIC * pre * pre * pre))
        act_ref[...] = (0.5 * pre * (1.0 + tangent)).astype(BF16)
        slope_ref[...] = 0.5 * (1.0 + tangent) + 0.5 * pre * (1.0 - tangent * tangent) * GELU_SCALE * (
            1.0 + 3.0 * GELU_CUBIC * pre * pre
        )

    block = pl.BlockSpec((rows, hidden), lambda i, s: (0, 0))
    return call(
        kernel,
        30 * rows * hidden,
        rows * hidden * (2 * len(terms) + 6),
        place,
        [bias, *terms],
        (1,),
        [pl.BlockSpec((1, hidden), lambda i, s: (0, 0))] + [block] * len(terms),
        [chip_block(rows, hidden, key), block],
        [jax.ShapeDtypeStruct((tokens, hidden), BF16), jax.ShapeDtypeStruct((rows, hidden), F32)],
        [into],
        [0],
    )


def differentiate(place, terms, slope, key, into, tokens):
    rows, hidden = slope.shape

    def kernel(s, slope_ref, *refs):
        ins, (grad_ref, sum_ref) = refs[: len(terms)], refs[-2:]
        grad = functools.reduce(jnp.add, [ref[...].astype(F32) for ref in ins]) * slope_ref[...]
        grad = grad.astype(BF16)
        grad_ref[...] = grad
        sum_ref[...] = jnp.sum(grad.astype(F32), axis=0, keepdims=True)

    block = pl.BlockSpec((rows, hidden), lambda i, s: (0, 0))
    return call(
        kernel,
        8 * rows * hidden,
        rows * hidden * (2 * len(terms) + 6),
        place,
        [slope, *terms],
        (1,),
        [block] * (1 + len(terms)),
        [chip_block(rows, hidden, key), pl.BlockSpec((1, hidden), lambda i, s: (0, 0))],
        [jax.ShapeDtypeStruct((tokens, hidden), BF16), jax.ShapeDtypeStruct((1, hidden), F32)],
        [into],
        [0],
    )


def add_bf16(left, right):
    return (left.astype(F32) + right.astype(F32)).astype(BF16)


def weight_out_grad(place, act, grad, into, first, count):
    tokens, depth = grad.shape
    hidden = act.shape[1]
    tile, width = depth // UNITS, hidden // UNITS

    def kernel(s, act_ref, grad_ref, *refs):
        out, turned = refs[-2:]

        @pl.when(pl.program_id(0) == 0)
        def _():
            for at in range(0, hidden, width):
                turned[at : at + width, :] = act_ref[:, at : at + width].T

        for at in range(0, hidden, hidden // 2):
            out[at : at + hidden // 2, :] = dot(turned[at : at + hidden // 2, :], grad_ref[...], (1, 0))

    return call(
        kernel,
        2 * tokens * tile * count * hidden,
        2 * tokens * (tile * count + hidden) + 4 * tile * count * hidden,
        place,
        [act, grad],
        (count,),
        [whole((tokens, hidden)), pl.BlockSpec((tokens, tile), lambda j, s: (0, first + j))],
        pl.BlockSpec((hidden, tile), lambda j, s: (0, first + j)),
        jax.ShapeDtypeStruct((hidden, depth), F32),
        [into],
        [0],
        [pltpu.VMEM((hidden, tokens), BF16)],
    )


def weight_in_grad(place, tok, grad, into, first, count):
    tokens, depth = tok.shape
    hidden = grad.shape[1]
    tile, width = depth // UNITS, hidden // 2

    def kernel(s, tok_ref, grad_ref, *refs):
        turned = tok_ref[...].T
        for at in range(0, hidden, width):
            refs[-1][:, at : at + width] = dot(turned, grad_ref[:, at : at + width], (1, 0))

    return call(
        kernel,
        2 * tokens * tile * count * hidden,
        2 * tokens * (tile * count + hidden) + 4 * tile * count * hidden,
        place,
        [tok, grad],
        (count,),
        [pl.BlockSpec((tokens, tile), lambda j, s: (0, first + j)), whole((tokens, hidden))],
        pl.BlockSpec((tile, hidden), lambda j, s: (first + j, 0)),
        jax.ShapeDtypeStruct((depth, hidden), F32),
        [into],
        [0],
    )


def add_scaled(place, left, right, scale, *done):
    def kernel(s, left_ref, right_ref, *refs):
        refs[-1][...] = (left_ref[...].astype(F32) + right_ref[...].astype(F32)) * scale

    return call(
        kernel,
        left.size,
        8 * left.size,
        place,
        [left, right, *done],
        (1,),
        [whole(left.shape)] * 2 + [pl.BlockSpec(memory_space=pl.ANY)] * len(done),
        whole(left.shape),
        jax.ShapeDtypeStruct(left.shape, F32),
    )


def after(value, *deps):
    return lax.optimization_barrier((value, *deps))[0]


def local(rows_of, cols_of, tokens, weight_in, bias_hidden, weight_out, out_grad):
    mine, depth = tokens.shape
    hidden = bias_hidden.shape[0]
    rows, everyone = 2 * mine, cols_of * mine
    bias = bias_hidden.reshape(1, hidden)
    steps = rows_of - 1
    me = lax.axis_index("col")
    place = jnp.stack([me // 2, me % 2]).astype(jnp.int32)
    others = sorted(range(1, cols_of // 2), key=lambda key: (-key.bit_count(), key))
    chunks = [("pre", 0), ("act", 0)] + [(kind, key) for kind in ("pre", "act") for key in others]
    total = len(chunks)

    def send(value, step):
        pairs = [(step - 1, step), (rows_of - step, rows_of - step - 1)]
        return lax.ppermute(value, "row", pairs)

    def swap(value, bits):
        return lax.ppermute(value, "col", [(i, i ^ bits) for i in range(cols_of)])

    chain = []

    def link(value):
        return after(value, chain[-1]) if chain else value

    own, ahead = {}, {}
    got = {chunk: [None] * steps for chunk in chunks}
    held = {}
    slopes, sums, arrived = {}, {}, []

    def compute_own(kind, keys):
        source, weight = (tokens, weight_in) if kind == "pre" else (out_grad, weight_out)
        if keys == [0]:
            far = held[kind, "far"]
            blocks = [[(link(source), zero, mine, lambda s: s[1] * mine), (far, zero, mine, lambda s: (1 - s[1]) * mine)]]
        else:
            gathered = link(held[kind])
            blocks = [[(gathered, lambda s, key=key: (s[0] ^ key) * rows, rows, zero)] for key in keys]
        outs = partials(place, blocks, weight, kind == "act")
        chain.append(outs[0])
        for key, out in zip(keys, outs):
            own[kind, key] = out

    def first_send(at):
        got[chunks[at]][0] = send(link(own[chunks[at]]), 1)

    def forward(at, step):
        chunk = chunks[at]
        payload = add_bf16(got[chunk][step - 2], link(own[chunk]))
        chain.append(payload)
        ahead.setdefault(chunk, payload)
        got[chunk][step - 1] = send(payload, step)

    def finish(at):
        kind, key = chunk = chunks[at]
        terms = [link(ahead[chunk])] + got[chunk][1:]
        if kind == "pre":
            held["activations"], slopes[key] = activate(place, terms, bias, key, held.get("activations"), everyone)
            chain.append(held["activations"])
        else:
            held["grads"], sums[key] = differentiate(place, terms, slopes[key], key, held.get("grads"), everyone)
            chain.append(held["grads"])

    def out_columns(first, count):
        held["out"] = weight_out_grad(
            place, link(held["activations"]), held["act"], held.get("out"), first, count
        )
        chain.append(held["out"])

    def in_rows(first, count):
        held["in"] = weight_in_grad(place, held["pre"], link(held["grads"]), held.get("in"), first, count)
        chain.append(held["in"])

    def tokens_of(keys, first, last):
        keep, give = token_grad(place, link(held["grads"]), weight_in, keys, rows, first, last)
        chain.append(keep)
        return keys, keep, give

    def exchange(parts):
        keys, keep, give = parts
        return keys, keep, swap(link(give), 1)

    def deliver(parts):
        keys, keep, given = parts
        results = []
        for at, key in enumerate(keys):
            block = slice(at * mine, (at + 1) * mine)
            pair = add_bf16(link(keep)[block], given[block])
            results.append(swap(pair, 2 * key) if key else pair)
        chain.append(pair)
        return results

    held["pre", "far"], held["act", "far"] = swap(tokens, 1), swap(out_grad, 1)
    held["pre"] = lax.all_gather(tokens, "col", axis=0, tiled=True)
    held["act"] = lax.all_gather(after(out_grad, held["pre", "far"]), "col", axis=0, tiled=True)
    compute_own("pre", [0])
    first_send(0)
    compute_own("act", [0])
    first_send(1)
    end = total + steps - 1
    gathered = len(others) + 2
    for slot in range(end):
        if 2 < slot + 1 < total and slot + 1 != gathered - 1:
            first_send(slot + 1)
        late = slot == 2
        if late and slot >= steps - 1:
            finish(slot - steps + 1)
        for step in range(steps, 1, -1) if late else range(2, steps + 1):
            if 0 <= slot - step + 2 < total:
                forward(slot - step + 2, step)
        if slot == 1:
            compute_own("pre", others)
            first_send(2)
        if slot == gathered - 3:
            first_send(gathered - 1)
            compute_own("act", others)
        if not late and slot >= steps - 1:
            finish(slot - steps + 1)
        if slot == end - 3:
            first = tokens_of([0] + others[:-2], 0, UNITS)
        if slot == end - 2:
            arrived += deliver(exchange(first))
            out_columns(0, UNITS)
    levels = [1 << i for i in range(rows_of.bit_length() - 1)]
    sums = link(functools.reduce(jnp.add, [sums[key] for key in sorted(sums)]))
    for bit in levels[:-1]:
        sums = sums + lax.ppermute(sums, "row", [(i, i ^ bit) for i in range(rows_of)])
    head = add_scaled(place, link(arrived[0]), arrived[1], 1.0)
    chain.append(head)
    sums = link(sums)
    given = lax.ppermute(sums, "row", [(i, i ^ levels[-1]) for i in range(rows_of)])
    chain.append(sums)
    last = exchange(tokens_of(others[-2:], 0, UNITS))
    arrived += deliver(last)
    in_rows(0, UNITS)
    grad_bias = add_scaled(place, sums, given, 1.0 / rows_of, held["in"]).reshape(hidden)
    grad_tokens = functools.reduce(jnp.add, [part.astype(F32) for part in arrived[2:]], head).astype(BF16)
    return (grad_tokens, held["in"], grad_bias, held["out"])


def solution(mesh):
    placed = (P("col", "row"), P("row", "col"), P("col"), P("col", "row"), P("col", "row"))
    return jax.shard_map(
        functools.partial(local, mesh.shape["row"], mesh.shape["col"]),
        mesh=mesh,
        in_specs=placed,
        out_specs=(P("col", "row"), P("row", "col"), P("col"), P("col", "row")),
        check_vma=False,
    )
```

```python
import functools

import jax
import jax.numpy as jnp
from jax import lax
from jax.experimental import pallas as pl
from jax.experimental.pallas import tpu as pltpu
from jax.sharding import PartitionSpec as P

GELU_SCALE = 0.7978845608
GELU_CUBIC = 0.044715
F32, BF16 = jnp.float32, jnp.bfloat16
VMEM_LIMIT = 48 * 1024 * 1024
UNITS, AHEAD = 7, 3


def dot(left, right, dims):
    return lax.dot_general(left, right, ((dims[:1], dims[1:]), ((), ())), preferred_element_type=F32)


def call(kernel, flops, moved, place, operands, grid, in_specs, out_specs, out_shape, into=(), outs=(), scratch=()):
    scalars = 1
    aliases = {}
    in_specs, operands = list(in_specs), list(operands)
    for array, out in zip(into, outs):
        if array is not None:
            aliases[scalars + len(operands)] = out
            operands.append(array)
            in_specs.append(pl.BlockSpec(memory_space=pl.ANY))
    return pl.pallas_call(
        kernel,
        grid_spec=pltpu.PrefetchScalarGridSpec(
            num_scalar_prefetch=scalars,
            grid=grid,
            in_specs=in_specs,
            out_specs=out_specs,
            scratch_shapes=list(scratch),
        ),
        out_shape=out_shape,
        input_output_aliases=aliases,
        compiler_params=pltpu.CompilerParams(vmem_limit_bytes=VMEM_LIMIT),
        cost_estimate=pl.CostEstimate(flops=flops, bytes_accessed=moved, transcendentals=0),
    )(place, *operands)


def whole(shape):
    return pl.BlockSpec(shape, lambda i, s: (0,) * len(shape), pipeline_mode=pl.Buffered(1))


def chip_block(rows, columns, key):
    return pl.BlockSpec((rows, columns), lambda i, s: (s[0] ^ key, 0))


def streamed(place, blocks, weight, pieces, dims, flops, write, out_shape, shrink=1):
    axis, first, last = pieces
    size = weight.shape[axis] // UNITS
    count = last - first
    arrays = []
    for block in blocks:
        for array, _, _, _ in block:
            if not any(array is other for other in arrays):
                arrays.append(array)
    total, depth = sum(part[2] for block in blocks for part in block), blocks[0][0][0].shape[1]
    parts = sum(len(block) for block in blocks)
    shape = (size, weight.shape[1]) if axis == 0 else (weight.shape[0], size)

    def kernel(s, *refs):
        sources, weight_ref = refs[: len(arrays)], refs[len(arrays)]
        outs, (block_ref, piece_ref, block_sem, piece_sem) = refs[len(arrays) + 1 : -4], refs[-4:]

        def piece(at):
            where = pl.ds(pl.multiple_of((first + at) * size, size), size)
            source = weight_ref.at[where, :] if axis == 0 else weight_ref.at[:, where]
            return pltpu.make_async_copy(source, piece_ref.at[at], piece_sem.at[at])

        copies, top = [], 0
        for block in blocks:
            for array, start, length, into in block:
                source = next(ref for ref, other in zip(sources, arrays) if other is array)
                copies.append(
                    pltpu.make_async_copy(
                        source.at[pl.ds(pl.multiple_of(start(s), 16), length), :],
                        block_ref.at[pl.ds(pl.multiple_of(top + into(s), 16), length), :],
                        block_sem.at[len(copies)],
                    )
                )
            top += sum(part[2] for part in block)
        piece(0).start()
        for copy in copies:
            copy.start()
        for at in range(1, min(AHEAD, count)):
            piece(at).start()
        for copy in copies:
            copy.wait()

        def step(at, carry):
            piece(at).wait()

            @pl.when(at + AHEAD < count)
            def _():
                piece(at + AHEAD).start()

            write(s, at, dot(block_ref[...], piece_ref[at], dims), outs)
            return carry

        lax.fori_loop(0, count, step, 0)

    moved = 2 * (total * depth + shape[0] * shape[1] * count)
    anywhere = pl.BlockSpec(memory_space=pl.ANY)
    return call(
        kernel,
        flops // shrink,
        moved // shrink,
        place,
        [*arrays, weight],
        (1,),
        [anywhere] * (len(arrays) + 1),
        [whole(out.shape) for out in out_shape],
        out_shape,
        scratch=[
            pltpu.VMEM((total, depth), BF16),
            pltpu.VMEM((count, *shape), BF16),
            pltpu.SemaphoreType.DMA((parts,)),
            pltpu.SemaphoreType.DMA((count,)),
        ],
    )


def zero(s):
    return 0


def columns_of(at, size):
    return pl.ds(pl.multiple_of(at * size, size), size)


def partials(place, blocks, weight, transposed):
    hidden = weight.shape[0 if transposed else 1]
    rows = sum(part[2] for part in blocks[0])
    width = hidden // UNITS

    def write(s, at, product, outs):
        for block, out in enumerate(outs):
            out[:, columns_of(at, width)] = product[block * rows : (block + 1) * rows].astype(BF16)

    return streamed(
        place,
        blocks,
        weight,
        (0 if transposed else 1, 0, UNITS),
        (1, 1) if transposed else (1, 0),
        2 * len(blocks) * rows * weight.size,
        write,
        [jax.ShapeDtypeStruct((rows, hidden), BF16)] * len(blocks),
        64,
    )


def token_grad(place, grad, weight_in, keys, rows, first, last):
    depth, hidden = weight_in.shape
    tile = depth // UNITS
    half = rows // 2

    def write(s, at, product, outs):
        low = s[1] == 0
        for block in range(len(keys)):
            first_half, second_half = (
                product[(2 * block + side) * half : (2 * block + side + 1) * half].astype(BF16) for side in range(2)
            )
            to = (slice(block * half, (block + 1) * half), columns_of(at, tile))
            outs[0][to] = jnp.where(low, first_half, second_half)
            outs[1][to] = jnp.where(low, second_half, first_half)

    return streamed(
        place,
        [[(grad, lambda s, key=key: (s[0] ^ key) * rows, rows, zero)] for key in keys],
        weight_in,
        (0, first, last),
        (1, 1),
        2 * len(keys) * rows * tile * (last - first) * hidden,
        write,
        [jax.ShapeDtypeStruct((len(keys) * half, tile * (last - first)), BF16)] * 2,
    )


def activate(place, terms, bias, key, into, tokens):
    rows, hidden = terms[0].shape

    def kernel(s, bias_ref, *refs):
        ins, (act_ref, slope_ref) = refs[: len(terms)], refs[-2:]
        pre = functools.reduce(jnp.add, [ref[...].astype(F32) for ref in ins]) + bias_ref[...]
        tangent = jnp.tanh(GELU_SCALE * (pre + GELU_CUBIC * pre * pre * pre))
        act_ref[...] = (0.5 * pre * (1.0 + tangent)).astype(BF16)
        slope_ref[...] = 0.5 * (1.0 + tangent) + 0.5 * pre * (1.0 - tangent * tangent) * GELU_SCALE * (
            1.0 + 3.0 * GELU_CUBIC * pre * pre
        )

    block = pl.BlockSpec((rows, hidden), lambda i, s: (0, 0))
    return call(
        kernel,
        30 * rows * hidden,
        rows * hidden * (2 * len(terms) + 6),
        place,
        [bias, *terms],
        (1,),
        [pl.BlockSpec((1, hidden), lambda i, s: (0, 0))] + [block] * len(terms),
        [chip_block(rows, hidden, key), block],
        [jax.ShapeDtypeStruct((tokens, hidden), BF16), jax.ShapeDtypeStruct((rows, hidden), F32)],
        [into],
        [0],
    )


def differentiate(place, terms, slope, key, into, tokens):
    rows, hidden = slope.shape

    def kernel(s, slope_ref, *refs):
        ins, (grad_ref, sum_ref) = refs[: len(terms)], refs[-2:]
        grad = functools.reduce(jnp.add, [ref[...].astype(F32) for ref in ins]) * slope_ref[...]
        grad = grad.astype(BF16)
        grad_ref[...] = grad
        sum_ref[...] = jnp.sum(grad.astype(F32), axis=0, keepdims=True)

    block = pl.BlockSpec((rows, hidden), lambda i, s: (0, 0))
    return call(
        kernel,
        8 * rows * hidden,
        rows * hidden * (2 * len(terms) + 6),
        place,
        [slope, *terms],
        (1,),
        [block] * (1 + len(terms)),
        [chip_block(rows, hidden, key), pl.BlockSpec((1, hidden), lambda i, s: (0, 0))],
        [jax.ShapeDtypeStruct((tokens, hidden), BF16), jax.ShapeDtypeStruct((1, hidden), F32)],
        [into],
        [0],
    )


def add_bf16(left, right):
    return (left.astype(F32) + right.astype(F32)).astype(BF16)


def weight_out_grad(place, act, grad, into, first, count):
    tokens, depth = grad.shape
    hidden = act.shape[1]
    tile, width = depth // UNITS, hidden // UNITS

    def kernel(s, act_ref, grad_ref, *refs):
        out, turned = refs[-2:]

        @pl.when(pl.program_id(0) == 0)
        def _():
            for at in range(0, hidden, width):
                turned[at : at + width, :] = act_ref[:, at : at + width].T

        for at in range(0, hidden, hidden // 2):
            out[at : at + hidden // 2, :] = dot(turned[at : at + hidden // 2, :], grad_ref[...], (1, 0))

    return call(
        kernel,
        2 * tokens * tile * count * hidden,
        2 * tokens * (tile * count + hidden) + 4 * tile * count * hidden,
        place,
        [act, grad],
        (count,),
        [whole((tokens, hidden)), pl.BlockSpec((tokens, tile), lambda j, s: (0, first + j))],
        pl.BlockSpec((hidden, tile), lambda j, s: (0, first + j)),
        jax.ShapeDtypeStruct((hidden, depth), F32),
        [into],
        [0],
        [pltpu.VMEM((hidden, tokens), BF16)],
    )


def weight_in_grad(place, tok, grad, into, first, count):
    tokens, depth = tok.shape
    hidden = grad.shape[1]
    tile, width = depth // UNITS, hidden // 2

    def kernel(s, tok_ref, grad_ref, *refs):
        turned = tok_ref[...].T
        for at in range(0, hidden, width):
            refs[-1][:, at : at + width] = dot(turned, grad_ref[:, at : at + width], (1, 0))

    return call(
        kernel,
        2 * tokens * tile * count * hidden,
        2 * tokens * (tile * count + hidden) + 4 * tile * count * hidden,
        place,
        [tok, grad],
        (count,),
        [pl.BlockSpec((tokens, tile), lambda j, s: (0, first + j)), whole((tokens, hidden))],
        pl.BlockSpec((tile, hidden), lambda j, s: (first + j, 0)),
        jax.ShapeDtypeStruct((depth, hidden), F32),
        [into],
        [0],
    )


def add_scaled(place, left, right, scale, *done):
    def kernel(s, left_ref, right_ref, *refs):
        refs[-1][...] = (left_ref[...].astype(F32) + right_ref[...].astype(F32)) * scale

    return call(
        kernel,
        left.size,
        8 * left.size,
        place,
        [left, right, *done],
        (1,),
        [whole(left.shape)] * 2 + [pl.BlockSpec(memory_space=pl.ANY)] * len(done),
        whole(left.shape),
        jax.ShapeDtypeStruct(left.shape, F32),
    )


def after(value, *deps):
    return lax.optimization_barrier((value, *deps))[0]


def local(rows_of, cols_of, tokens, weight_in, bias_hidden, weight_out, out_grad):
    mine, depth = tokens.shape
    hidden = bias_hidden.shape[0]
    rows, everyone = 2 * mine, cols_of * mine
    bias = bias_hidden.reshape(1, hidden)
    steps = rows_of - 1
    me = lax.axis_index("col")
    place = jnp.stack([me // 2, me % 2]).astype(jnp.int32)
    others = sorted(range(1, cols_of // 2), key=lambda key: (-key.bit_count(), key))
    chunks = [("pre", 0), ("act", 0)] + [(kind, key) for kind in ("pre", "act") for key in others]
    total = len(chunks)

    def send(value, step):
        pairs = [(step - 1, step), (rows_of - step, rows_of - step - 1)]
        return lax.ppermute(value, "row", pairs)

    def swap(value, bits):
        return lax.ppermute(value, "col", [(i, i ^ bits) for i in range(cols_of)])

    chain = []

    def link(value):
        return after(value, chain[-1]) if chain else value

    own, ahead = {}, {}
    got = {chunk: [None] * steps for chunk in chunks}
    held = {}
    slopes, sums, arrived = {}, {}, []

    def compute_own(kind, keys):
        source, weight = (tokens, weight_in) if kind == "pre" else (out_grad, weight_out)
        if keys == [0]:
            far = held[kind, "far"]
            blocks = [[(link(source), zero, mine, lambda s: s[1] * mine), (far, zero, mine, lambda s: (1 - s[1]) * mine)]]
        else:
            gathered = link(held[kind])
            blocks = [[(gathered, lambda s, key=key: (s[0] ^ key) * rows, rows, zero)] for key in keys]
        outs = partials(place, blocks, weight, kind == "act")
        chain.append(outs[0])
        for key, out in zip(keys, outs):
            own[kind, key] = out

    def first_send(at):
        got[chunks[at]][0] = send(link(own[chunks[at]]), 1)

    def forward(at, step):
        chunk = chunks[at]
        payload = add_bf16(got[chunk][step - 2], link(own[chunk]))
        chain.append(payload)
        ahead.setdefault(chunk, payload)
        got[chunk][step - 1] = send(payload, step)

    def finish(at):
        kind, key = chunk = chunks[at]
        terms = [link(ahead[chunk])] + got[chunk][1:]
        if kind == "pre":
            held["activations"], slopes[key] = activate(place, terms, bias, key, held.get("activations"), everyone)
            chain.append(held["activations"])
        else:
            held["grads"], sums[key] = differentiate(place, terms, slopes[key], key, held.get("grads"), everyone)
            chain.append(held["grads"])

    def out_columns(first, count):
        held["out"] = weight_out_grad(
            place, link(held["activations"]), held["act"], held.get("out"), first, count
        )
        chain.append(held["out"])

    def in_rows(first, count):
        held["in"] = weight_in_grad(place, held["pre"], link(held["grads"]), held.get("in"), first, count)
        chain.append(held["in"])

    def tokens_of(keys, first, last):
        keep, give = token_grad(place, link(held["grads"]), weight_in, keys, rows, first, last)
        chain.append(keep)
        return keys, keep, give

    def exchange(parts):
        keys, keep, give = parts
        return keys, keep, swap(link(give), 1)

    def deliver(parts):
        keys, keep, given = parts
        results = []
        for at, key in enumerate(keys):
            block = slice(at * mine, (at + 1) * mine)
            pair = add_bf16(link(keep)[block], given[block])
            results.append(swap(pair, 2 * key) if key else pair)
        chain.append(pair)
        return results

    held["pre", "far"], held["act", "far"] = swap(tokens, 1), swap(out_grad, 1)
    held["pre"] = lax.all_gather(tokens, "col", axis=0, tiled=True)
    held["act"] = lax.all_gather(after(out_grad, held["pre", "far"]), "col", axis=0, tiled=True)
    compute_own("pre", [0])
    first_send(0)
    compute_own("act", [0])
    first_send(1)
    end = total + steps - 1
    for slot in range(end):
        if slot > 1 and slot + 1 < total:
            first_send(slot + 1)
        if slot == 1:
            compute_own("pre", others[:1])
            first_send(2)
        for step in range(2, steps + 1):
            if 0 <= slot - step + 2 < total:
                forward(slot - step + 2, step)
            if step == 2 and slot == len(others):
                compute_own("act", others)
        if slot == 1:
            compute_own("pre", others[1:])
        if slot >= steps - 1:
            finish(slot - steps + 1)
        if slot == end - 3:
            first = tokens_of([0] + others[:-2], 0, UNITS)
        if slot == end - 2:
            arrived += deliver(exchange(first))
            out_columns(0, UNITS)
    levels = [1 << i for i in range(rows_of.bit_length() - 1)]
    sums = link(functools.reduce(jnp.add, [sums[key] for key in sorted(sums)]))
    for bit in levels[:-1]:
        sums = sums + lax.ppermute(sums, "row", [(i, i ^ bit) for i in range(rows_of)])
    head = add_scaled(place, link(arrived[0]), arrived[1], 1.0)
    chain.append(head)
    last = exchange(tokens_of(others[-2:], 0, UNITS))
    sums = link(sums)
    given = lax.ppermute(sums, "row", [(i, i ^ levels[-1]) for i in range(rows_of)])
    arrived += deliver(last)
    in_rows(0, UNITS)
    grad_bias = add_scaled(place, sums, given, 1.0 / rows_of, held["in"]).reshape(hidden)
    grad_tokens = functools.reduce(jnp.add, [part.astype(F32) for part in arrived[2:]], head).astype(BF16)
    return (grad_tokens, held["in"], grad_bias, held["out"])


def solution(mesh):
    placed = (P("col", "row"), P("row", "col"), P("col"), P("col", "row"), P("col", "row"))
    return jax.shard_map(
        functools.partial(local, mesh.shape["row"], mesh.shape["col"]),
        mesh=mesh,
        in_specs=placed,
        out_specs=(P("col", "row"), P("row", "col"), P("col"), P("col", "row")),
        check_vma=False,
    )
```

```python
import functools

import jax
import jax.numpy as jnp
from jax import lax
from jax.experimental import pallas as pl
from jax.experimental.pallas import tpu as pltpu
from jax.sharding import PartitionSpec as P

GELU_SCALE = 0.7978845608
GELU_CUBIC = 0.044715
F32, BF16 = jnp.float32, jnp.bfloat16
VMEM_LIMIT = 48 * 1024 * 1024
UNITS, AHEAD, SUBLANES = 7, 3, 8


def dot(left, right, dims):
    return lax.dot_general(left, right, ((dims[:1], dims[1:]), ((), ())), preferred_element_type=F32)


def call(kernel, flops, moved, place, operands, grid, in_specs, out_specs, out_shape, into=(), outs=(), scratch=()):
    scalars = 1
    aliases = {}
    in_specs, operands = list(in_specs), list(operands)
    for array, out in zip(into, outs):
        if array is not None:
            aliases[scalars + len(operands)] = out
            operands.append(array)
            in_specs.append(pl.BlockSpec(memory_space=pl.ANY))
    return pl.pallas_call(
        kernel,
        grid_spec=pltpu.PrefetchScalarGridSpec(
            num_scalar_prefetch=scalars,
            grid=grid,
            in_specs=in_specs,
            out_specs=out_specs,
            scratch_shapes=list(scratch),
        ),
        out_shape=out_shape,
        input_output_aliases=aliases,
        compiler_params=pltpu.CompilerParams(vmem_limit_bytes=VMEM_LIMIT),
        cost_estimate=pl.CostEstimate(flops=flops, bytes_accessed=moved, transcendentals=0),
    )(place, *operands)


def whole(shape):
    return pl.BlockSpec(shape, lambda i, s: (0,) * len(shape), pipeline_mode=pl.Buffered(1))


def chip_block(rows, columns, key):
    return pl.BlockSpec((rows, columns), lambda i, s: (s[0] ^ key, 0))


def streamed(place, blocks, weight, pieces, dims, flops, write, out_shape, shrink=1):
    axis, first, last = pieces
    size = weight.shape[axis] // UNITS
    count = last - first
    arrays = []
    for block in blocks:
        for array, _, _, _ in block:
            if not any(array is other for other in arrays):
                arrays.append(array)
    total, depth = sum(part[2] for block in blocks for part in block), blocks[0][0][0].shape[1]
    parts = sum(len(block) for block in blocks)
    shape = (size, weight.shape[1]) if axis == 0 else (weight.shape[0], size)

    def kernel(s, *refs):
        sources, weight_ref = refs[: len(arrays)], refs[len(arrays)]
        outs, (block_ref, piece_ref, block_sem, piece_sem) = refs[len(arrays) + 1 : -4], refs[-4:]

        def piece(at):
            where = pl.ds(pl.multiple_of((first + at) * size, size), size)
            source = weight_ref.at[where, :] if axis == 0 else weight_ref.at[:, where]
            return pltpu.make_async_copy(source, piece_ref.at[at], piece_sem.at[at])

        copies, top = [], 0
        for block in blocks:
            for array, start, length, into in block:
                source = next(ref for ref, other in zip(sources, arrays) if other is array)
                copies.append(
                    pltpu.make_async_copy(
                        source.at[pl.ds(pl.multiple_of(start(s), 16), length), :],
                        block_ref.at[pl.ds(pl.multiple_of(top + into(s), 16), length), :],
                        block_sem.at[len(copies)],
                    )
                )
            top += sum(part[2] for part in block)
        piece(0).start()
        for copy in copies:
            copy.start()
        for at in range(1, min(AHEAD, count)):
            piece(at).start()
        for copy in copies:
            copy.wait()

        def step(at, carry):
            piece(at).wait()

            @pl.when(at + AHEAD < count)
            def _():
                piece(at + AHEAD).start()

            write(s, at, dot(block_ref[...], piece_ref[at], dims), outs)
            return carry

        lax.fori_loop(0, count, step, 0)

    moved = 2 * (total * depth + shape[0] * shape[1] * count)
    anywhere = pl.BlockSpec(memory_space=pl.ANY)
    return call(
        kernel,
        flops // shrink,
        moved // shrink,
        place,
        [*arrays, weight],
        (1,),
        [anywhere] * (len(arrays) + 1),
        [whole(out.shape) for out in out_shape],
        out_shape,
        scratch=[
            pltpu.VMEM((total, depth), BF16),
            pltpu.VMEM((count, *shape), BF16),
            pltpu.SemaphoreType.DMA((parts,)),
            pltpu.SemaphoreType.DMA((count,)),
        ],
    )


def zero(s):
    return 0


def columns_of(at, size):
    return pl.ds(pl.multiple_of(at * size, size), size)


def partials(place, blocks, weight, transposed):
    hidden = weight.shape[0 if transposed else 1]
    rows = sum(part[2] for part in blocks[0])
    width = hidden // UNITS

    def write(s, at, product, outs):
        for block, out in enumerate(outs):
            out[:, columns_of(at, width)] = product[block * rows : (block + 1) * rows].astype(BF16)

    return streamed(
        place,
        blocks,
        weight,
        (0 if transposed else 1, 0, UNITS),
        (1, 1) if transposed else (1, 0),
        2 * len(blocks) * rows * weight.size,
        write,
        [jax.ShapeDtypeStruct((rows, hidden), BF16)] * len(blocks),
        64,
    )


def token_grad(place, grad, weight_in, keys, rows, first, last):
    depth, hidden = weight_in.shape
    tile = depth // UNITS
    half = rows // 2

    def write(s, at, product, outs):
        low = s[1] == 0
        for block in range(len(keys)):
            first_half, second_half = (
                product[(2 * block + side) * half : (2 * block + side + 1) * half].astype(BF16) for side in range(2)
            )
            to = (slice(block * half, (block + 1) * half), columns_of(at, tile))
            outs[0][to] = jnp.where(low, first_half, second_half)
            outs[1][to] = jnp.where(low, second_half, first_half)

    return streamed(
        place,
        [[(grad, lambda s, key=key: (s[0] ^ key) * rows, rows, zero)] for key in keys],
        weight_in,
        (0, first, last),
        (1, 1),
        2 * len(keys) * rows * tile * (last - first) * hidden,
        write,
        [jax.ShapeDtypeStruct((len(keys) * half, tile * (last - first)), BF16)] * 2,
    )


def activate(place, terms, bias, key, into, tokens):
    rows, hidden = terms[0].shape

    def kernel(s, bias_ref, *refs):
        ins, (act_ref, slope_ref) = refs[: len(terms)], refs[-2:]
        pre = functools.reduce(jnp.add, [ref[...].astype(F32) for ref in ins]) + bias_ref[...]
        tangent = jnp.tanh(GELU_SCALE * (pre + GELU_CUBIC * pre * pre * pre))
        act_ref[...] = (0.5 * pre * (1.0 + tangent)).astype(BF16)
        slope_ref[...] = 0.5 * (1.0 + tangent) + 0.5 * pre * (1.0 - tangent * tangent) * GELU_SCALE * (
            1.0 + 3.0 * GELU_CUBIC * pre * pre
        )

    block = pl.BlockSpec((rows, hidden), lambda i, s: (0, 0))
    return call(
        kernel,
        30 * rows * hidden,
        rows * hidden * (2 * len(terms) + 6),
        place,
        [bias, *terms],
        (1,),
        [pl.BlockSpec((1, hidden), lambda i, s: (0, 0))] + [block] * len(terms),
        [chip_block(rows, hidden, key), block],
        [jax.ShapeDtypeStruct((tokens, hidden), BF16), jax.ShapeDtypeStruct((rows, hidden), F32)],
        [into],
        [0],
    )


def differentiate(place, terms, slope, key, into, tokens):
    rows, hidden = slope.shape

    def kernel(s, slope_ref, *refs):
        ins, (grad_ref, sum_ref) = refs[: len(terms)], refs[-2:]
        grad = functools.reduce(jnp.add, [ref[...].astype(F32) for ref in ins]) * slope_ref[...]
        grad = grad.astype(BF16)
        grad_ref[...] = grad
        sum_ref[...] = jnp.broadcast_to(jnp.sum(grad.astype(F32), axis=0, keepdims=True), sum_ref.shape)

    block = pl.BlockSpec((rows, hidden), lambda i, s: (0, 0))
    return call(
        kernel,
        8 * rows * hidden,
        rows * hidden * (2 * len(terms) + 6),
        place,
        [slope, *terms],
        (1,),
        [block] * (1 + len(terms)),
        [chip_block(rows, hidden, key), pl.BlockSpec((SUBLANES, hidden), lambda i, s: (0, 0))],
        [jax.ShapeDtypeStruct((tokens, hidden), BF16), jax.ShapeDtypeStruct((SUBLANES, hidden), F32)],
        [into],
        [0],
    )


def add_bf16(left, right):
    return (left.astype(F32) + right.astype(F32)).astype(BF16)


def weight_out_grad(place, act, grad, into, first, count):
    tokens, depth = grad.shape
    hidden = act.shape[1]
    tile, width = depth // UNITS, hidden // UNITS

    def kernel(s, act_ref, grad_ref, *refs):
        out, turned = refs[-2:]

        @pl.when(pl.program_id(0) == 0)
        def _():
            for at in range(0, hidden, width):
                turned[at : at + width, :] = act_ref[:, at : at + width].T

        for at in range(0, hidden, hidden // 2):
            out[at : at + hidden // 2, :] = dot(turned[at : at + hidden // 2, :], grad_ref[...], (1, 0))

    return call(
        kernel,
        2 * tokens * tile * count * hidden,
        2 * tokens * (tile * count + hidden) + 4 * tile * count * hidden,
        place,
        [act, grad],
        (count,),
        [whole((tokens, hidden)), pl.BlockSpec((tokens, tile), lambda j, s: (0, first + j))],
        pl.BlockSpec((hidden, tile), lambda j, s: (0, first + j)),
        jax.ShapeDtypeStruct((hidden, depth), F32),
        [into],
        [0],
        [pltpu.VMEM((hidden, tokens), BF16)],
    )


def weight_in_grad(place, tok, grad, into, first, count):
    tokens, depth = tok.shape
    hidden = grad.shape[1]
    tile, width = depth // UNITS, hidden // 2

    def kernel(s, tok_ref, grad_ref, *refs):
        turned = tok_ref[...].T
        for at in range(0, hidden, width):
            refs[-1][:, at : at + width] = dot(turned, grad_ref[:, at : at + width], (1, 0))

    return call(
        kernel,
        2 * tokens * tile * count * hidden,
        2 * tokens * (tile * count + hidden) + 4 * tile * count * hidden,
        place,
        [tok, grad],
        (count,),
        [pl.BlockSpec((tokens, tile), lambda j, s: (0, first + j)), whole((tokens, hidden))],
        pl.BlockSpec((tile, hidden), lambda j, s: (first + j, 0)),
        jax.ShapeDtypeStruct((depth, hidden), F32),
        [into],
        [0],
    )


def add_early(place, left, right):
    def kernel(s, left_ref, right_ref, out):
        out[...] = left_ref[...].astype(F32) + right_ref[...].astype(F32)

    return call(
        kernel,
        left.size,
        8 * left.size,
        place,
        [left, right],
        (1,),
        [whole(left.shape)] * 2,
        whole(left.shape),
        jax.ShapeDtypeStruct(left.shape, F32),
    )


def mean_of(place, values, done):
    count = values.shape[0] // SUBLANES

    def kernel(s, values_ref, done_ref, out):
        total = functools.reduce(jnp.add, [values_ref[at * SUBLANES : at * SUBLANES + 1, :] for at in range(count)])
        out[...] = total * (1.0 / count)

    return call(
        kernel,
        values.size,
        4 * values.size,
        place,
        [values, done],
        (1,),
        [whole(values.shape), pl.BlockSpec(memory_space=pl.ANY)],
        whole((1, values.shape[1])),
        jax.ShapeDtypeStruct((1, values.shape[1]), F32),
    )


def after(value, *deps):
    return lax.optimization_barrier((value, *deps))[0]


def local(rows_of, cols_of, tokens, weight_in, bias_hidden, weight_out, out_grad):
    mine, depth = tokens.shape
    hidden = bias_hidden.shape[0]
    rows, everyone = 2 * mine, cols_of * mine
    bias = bias_hidden.reshape(1, hidden)
    steps = rows_of - 1
    me = lax.axis_index("col")
    place = jnp.stack([me // 2, me % 2]).astype(jnp.int32)
    others = sorted(range(1, cols_of // 2), key=lambda key: (-key.bit_count(), key))
    chunks = [("pre", 0), ("act", 0)] + [(kind, key) for kind in ("pre", "act") for key in others]
    total = len(chunks)

    def send(value, step):
        pairs = [(step - 1, step), (rows_of - step, rows_of - step - 1)]
        return lax.ppermute(value, "row", pairs)

    def swap(value, bits):
        return lax.ppermute(value, "col", [(i, i ^ bits) for i in range(cols_of)])

    chain = []

    def link(value):
        return after(value, chain[-1]) if chain else value

    own, ahead = {}, {}
    got = {chunk: [None] * steps for chunk in chunks}
    held = {}
    slopes, sums, arrived = {}, {}, []

    def compute_own(kind, keys):
        source, weight = (tokens, weight_in) if kind == "pre" else (out_grad, weight_out)
        if keys == [0]:
            far = held[kind, "far"]
            blocks = [[(link(source), zero, mine, lambda s: s[1] * mine), (far, zero, mine, lambda s: (1 - s[1]) * mine)]]
        else:
            gathered = link(held[kind])
            blocks = [[(gathered, lambda s, key=key: (s[0] ^ key) * rows, rows, zero)] for key in keys]
        outs = partials(place, blocks, weight, kind == "act")
        chain.append(outs[0])
        for key, out in zip(keys, outs):
            own[kind, key] = out

    def first_send(at):
        got[chunks[at]][0] = send(link(own[chunks[at]]), 1)

    def forward(at, step):
        chunk = chunks[at]
        payload = add_bf16(got[chunk][step - 2], link(own[chunk]))
        chain.append(payload)
        ahead.setdefault(chunk, payload)
        got[chunk][step - 1] = send(payload, step)

    def finish(at):
        kind, key = chunk = chunks[at]
        terms = [link(ahead[chunk])] + got[chunk][1:]
        if kind == "pre":
            held["activations"], slopes[key] = activate(place, terms, bias, key, held.get("activations"), everyone)
            chain.append(held["activations"])
        else:
            held["grads"], sums[key] = differentiate(place, terms, slopes[key], key, held.get("grads"), everyone)
            chain.append(held["grads"])

    def out_columns(first, count):
        held["out"] = weight_out_grad(
            place, link(held["activations"]), held["act"], held.get("out"), first, count
        )
        chain.append(held["out"])

    def in_rows(first, count):
        held["in"] = weight_in_grad(place, held["pre"], link(held["grads"]), held.get("in"), first, count)
        chain.append(held["in"])

    def tokens_of(keys, first, last):
        keep, give = token_grad(place, link(held["grads"]), weight_in, keys, rows, first, last)
        chain.append(keep)
        return keys, keep, give

    def exchange(parts):
        keys, keep, give = parts
        return keys, keep, swap(link(give), 1)

    def deliver(parts):
        keys, keep, given = parts
        results = []
        for at, key in enumerate(keys):
            block = slice(at * mine, (at + 1) * mine)
            pair = add_bf16(link(keep)[block], given[block])
            results.append(swap(pair, 2 * key) if key else pair)
        chain.append(pair)
        return results

    held["pre", "far"], held["act", "far"] = swap(tokens, 1), swap(out_grad, 1)
    held["pre"] = lax.all_gather(tokens, "col", axis=0, tiled=True)
    held["act"] = lax.all_gather(after(out_grad, held["pre", "far"]), "col", axis=0, tiled=True)
    compute_own("pre", [0])
    first_send(0)
    compute_own("act", [0])
    first_send(1)
    end = total + steps - 1
    begun = set()

    def begin(at):
        if at < total and at not in begun:
            begun.add(at)
            first_send(at)

    def second(at):
        if 0 <= at < total and ("second", at) not in begun:
            begun.add(("second", at))
            forward(at, 2)

    for slot in range(end):
        if slot > 1:
            begin(slot + 1)
        if slot == 1:
            compute_own("pre", others[:1])
            begin(2)
        second(slot)
        if slot == len(others):
            compute_own("act", others)
            begin(slot + 2)
            second(slot + 1)
        for step in range(3, steps + 1):
            if 0 <= slot - step + 2 < total:
                forward(slot - step + 2, step)
        if slot == 1:
            compute_own("pre", others[1:])
        if slot >= steps - 1:
            finish(slot - steps + 1)
        if slot == end - 3:
            first = tokens_of([0] + others[:-2], 0, UNITS)
        if slot == end - 2:
            arrived += deliver(exchange(first))
            out_columns(0, UNITS)
    sums = link(functools.reduce(jnp.add, [sums[key] for key in sorted(sums)]))
    sums = lax.all_gather(sums, "row", axis=0, tiled=True)
    head = add_early(place, link(arrived[0]), arrived[1])
    chain.append(head)
    last = exchange(tokens_of(others[-2:], 0, UNITS))
    arrived += deliver(last)
    in_rows(0, UNITS)
    grad_bias = mean_of(place, sums, held["in"]).reshape(hidden)
    grad_tokens = functools.reduce(jnp.add, [part.astype(F32) for part in arrived[2:]], head).astype(BF16)
    return (grad_tokens, held["in"], grad_bias, held["out"])


def solution(mesh):
    placed = (P("col", "row"), P("row", "col"), P("col"), P("col", "row"), P("col", "row"))
    return jax.shard_map(
        functools.partial(local, mesh.shape["row"], mesh.shape["col"]),
        mesh=mesh,
        in_specs=placed,
        out_specs=(P("col", "row"), P("row", "col"), P("col"), P("col", "row")),
        check_vma=False,
    )
```

```python
import functools

import jax
import jax.numpy as jnp
from jax import lax
from jax.experimental import pallas as pl
from jax.experimental.pallas import tpu as pltpu
from jax.sharding import PartitionSpec as P

GELU_SCALE = 0.7978845608
GELU_CUBIC = 0.044715
F32, BF16 = jnp.float32, jnp.bfloat16
VMEM_LIMIT = 40 * 1024 * 1024
UNITS, AHEAD = 7, 3


def dot(left, right, dims):
    return lax.dot_general(left, right, ((dims[:1], dims[1:]), ((), ())), preferred_element_type=F32)


def call(kernel, flops, moved, place, operands, grid, in_specs, out_specs, out_shape, into=(), outs=(), scratch=()):
    scalars = 1
    aliases = {}
    in_specs, operands = list(in_specs), list(operands)
    for array, out in zip(into, outs):
        if array is not None:
            aliases[scalars + len(operands)] = out
            operands.append(array)
            in_specs.append(pl.BlockSpec(memory_space=pl.ANY))
    return pl.pallas_call(
        kernel,
        grid_spec=pltpu.PrefetchScalarGridSpec(
            num_scalar_prefetch=scalars,
            grid=grid,
            in_specs=in_specs,
            out_specs=out_specs,
            scratch_shapes=list(scratch),
        ),
        out_shape=out_shape,
        input_output_aliases=aliases,
        compiler_params=pltpu.CompilerParams(vmem_limit_bytes=VMEM_LIMIT),
        cost_estimate=pl.CostEstimate(flops=flops, bytes_accessed=moved, transcendentals=0),
    )(place, *operands)


def whole(shape):
    return pl.BlockSpec(shape, lambda i, s: (0,) * len(shape), pipeline_mode=pl.Buffered(1))


def chip_block(rows, columns, key):
    return pl.BlockSpec((rows, columns), lambda i, s: (s[0] ^ key, 0))


def streamed(place, blocks, weight, pieces, dims, flops, write, out_shape, shrink=1):
    axis, first, last = pieces
    size = weight.shape[axis] // UNITS
    count = last - first
    arrays = []
    for block in blocks:
        for array, _, _, _ in block:
            if not any(array is other for other in arrays):
                arrays.append(array)
    total, depth = sum(part[2] for block in blocks for part in block), blocks[0][0][0].shape[1]
    parts = sum(len(block) for block in blocks)
    shape = (size, weight.shape[1]) if axis == 0 else (weight.shape[0], size)

    def kernel(s, *refs):
        sources, weight_ref = refs[: len(arrays)], refs[len(arrays)]
        outs, (block_ref, piece_ref, block_sem, piece_sem) = refs[len(arrays) + 1 : -4], refs[-4:]

        def piece(at):
            where = pl.ds(pl.multiple_of((first + at) * size, size), size)
            source = weight_ref.at[where, :] if axis == 0 else weight_ref.at[:, where]
            return pltpu.make_async_copy(source, piece_ref.at[at], piece_sem.at[at])

        copies, top = [], 0
        for block in blocks:
            for array, start, length, into in block:
                source = next(ref for ref, other in zip(sources, arrays) if other is array)
                copies.append(
                    pltpu.make_async_copy(
                        source.at[pl.ds(pl.multiple_of(start(s), 16), length), :],
                        block_ref.at[pl.ds(pl.multiple_of(top + into(s), 16), length), :],
                        block_sem.at[len(copies)],
                    )
                )
            top += sum(part[2] for part in block)
        piece(0).start()
        for copy in copies:
            copy.start()
        for at in range(1, min(AHEAD, count)):
            piece(at).start()
        for copy in copies:
            copy.wait()

        def step(at, carry):
            piece(at).wait()

            @pl.when(at + AHEAD < count)
            def _():
                piece(at + AHEAD).start()

            write(s, at, dot(block_ref[...], piece_ref[at], dims), outs)
            return carry

        lax.fori_loop(0, count, step, 0)

    moved = 2 * (total * depth + shape[0] * shape[1] * count)
    anywhere = pl.BlockSpec(memory_space=pl.ANY)
    return call(
        kernel,
        flops // shrink,
        moved // shrink,
        place,
        [*arrays, weight],
        (1,),
        [anywhere] * (len(arrays) + 1),
        [whole(out.shape) for out in out_shape],
        out_shape,
        scratch=[
            pltpu.VMEM((total, depth), BF16),
            pltpu.VMEM((count, *shape), BF16),
            pltpu.SemaphoreType.DMA((parts,)),
            pltpu.SemaphoreType.DMA((count,)),
        ],
    )


def zero(s):
    return 0


def columns_of(at, size):
    return pl.ds(pl.multiple_of(at * size, size), size)


def partials(place, blocks, weight, transposed):
    hidden = weight.shape[0 if transposed else 1]
    rows = sum(part[2] for part in blocks[0])
    width = hidden // UNITS

    def write(s, at, product, outs):
        for block, out in enumerate(outs):
            out[:, columns_of(at, width)] = product[block * rows : (block + 1) * rows].astype(BF16)

    return streamed(
        place,
        blocks,
        weight,
        (0 if transposed else 1, 0, UNITS),
        (1, 1) if transposed else (1, 0),
        2 * len(blocks) * rows * weight.size,
        write,
        [jax.ShapeDtypeStruct((rows, hidden), BF16)] * len(blocks),
        64,
    )


def token_grad(place, grad, weight_in, keys, rows, first, last):
    depth, hidden = weight_in.shape
    tile = depth // UNITS
    half = rows // 2

    def write(s, at, product, outs):
        low = s[1] == 0
        for block in range(len(keys)):
            first_half, second_half = (
                product[(2 * block + side) * half : (2 * block + side + 1) * half].astype(BF16) for side in range(2)
            )
            to = (slice(block * half, (block + 1) * half), columns_of(at, tile))
            outs[0][to] = jnp.where(low, first_half, second_half)
            outs[1][to] = jnp.where(low, second_half, first_half)

    return streamed(
        place,
        [[(grad, lambda s, key=key: (s[0] ^ key) * rows, rows, zero)] for key in keys],
        weight_in,
        (0, first, last),
        (1, 1),
        2 * len(keys) * rows * tile * (last - first) * hidden,
        write,
        [jax.ShapeDtypeStruct((len(keys) * half, tile * (last - first)), BF16)] * 2,
    )


def activate(place, terms, bias, key, into, tokens):
    rows, hidden = terms[0].shape

    def kernel(s, bias_ref, *refs):
        ins, (act_ref, slope_ref) = refs[: len(terms)], refs[-2:]
        pre = functools.reduce(jnp.add, [ref[...].astype(F32) for ref in ins]) + bias_ref[...]
        tangent = jnp.tanh(GELU_SCALE * (pre + GELU_CUBIC * pre * pre * pre))
        act_ref[...] = (0.5 * pre * (1.0 + tangent)).astype(BF16)
        slope_ref[...] = 0.5 * (1.0 + tangent) + 0.5 * pre * (1.0 - tangent * tangent) * GELU_SCALE * (
            1.0 + 3.0 * GELU_CUBIC * pre * pre
        )

    block = pl.BlockSpec((rows, hidden), lambda i, s: (0, 0))
    return call(
        kernel,
        30 * rows * hidden,
        rows * hidden * (2 * len(terms) + 6),
        place,
        [bias, *terms],
        (1,),
        [pl.BlockSpec((1, hidden), lambda i, s: (0, 0))] + [block] * len(terms),
        [chip_block(rows, hidden, key), block],
        [jax.ShapeDtypeStruct((tokens, hidden), BF16), jax.ShapeDtypeStruct((rows, hidden), F32)],
        [into],
        [0],
    )


def differentiate(place, terms, slope, key, into, tokens):
    rows, hidden = slope.shape

    def kernel(s, slope_ref, *refs):
        ins, (grad_ref, sum_ref) = refs[: len(terms)], refs[-2:]
        grad = functools.reduce(jnp.add, [ref[...].astype(F32) for ref in ins]) * slope_ref[...]
        grad = grad.astype(BF16)
        grad_ref[...] = grad
        sum_ref[...] = jnp.sum(grad.astype(F32), axis=0, keepdims=True)

    block = pl.BlockSpec((rows, hidden), lambda i, s: (0, 0))
    return call(
        kernel,
        8 * rows * hidden,
        rows * hidden * (2 * len(terms) + 6),
        place,
        [slope, *terms],
        (1,),
        [block] * (1 + len(terms)),
        [chip_block(rows, hidden, key), pl.BlockSpec((1, hidden), lambda i, s: (0, 0))],
        [jax.ShapeDtypeStruct((tokens, hidden), BF16), jax.ShapeDtypeStruct((1, hidden), F32)],
        [into],
        [0],
    )


def add_bf16(left, right):
    return (left.astype(F32) + right.astype(F32)).astype(BF16)


def weight_out_grad(place, act, grad, into, first, count):
    tokens, depth = grad.shape
    hidden = act.shape[1]
    tile, width = depth // UNITS, hidden // UNITS

    def kernel(s, act_ref, grad_ref, *refs):
        out, turned = refs[-2:]

        @pl.when(pl.program_id(0) == 0)
        def _():
            for at in range(0, hidden, width):
                turned[at : at + width, :] = act_ref[:, at : at + width].T

        for at in range(0, hidden, hidden // 2):
            out[at : at + hidden // 2, :] = dot(turned[at : at + hidden // 2, :], grad_ref[...], (1, 0))

    return call(
        kernel,
        2 * tokens * tile * count * hidden,
        2 * tokens * (tile * count + hidden) + 4 * tile * count * hidden,
        place,
        [act, grad],
        (count,),
        [whole((tokens, hidden)), pl.BlockSpec((tokens, tile), lambda j, s: (0, first + j))],
        pl.BlockSpec((hidden, tile), lambda j, s: (0, first + j)),
        jax.ShapeDtypeStruct((hidden, depth), F32),
        [into],
        [0],
        [pltpu.VMEM((hidden, tokens), BF16)],
    )


def weight_in_grad(place, tok, grad, into, first, count):
    tokens, depth = tok.shape
    hidden = grad.shape[1]
    tile, width = depth // UNITS, hidden // 2

    def kernel(s, tok_ref, grad_ref, *refs):
        turned = tok_ref[...].T
        for at in range(0, hidden, width):
            refs[-1][:, at : at + width] = dot(turned, grad_ref[:, at : at + width], (1, 0))

    return call(
        kernel,
        2 * tokens * tile * count * hidden,
        2 * tokens * (tile * count + hidden) + 4 * tile * count * hidden,
        place,
        [tok, grad],
        (count,),
        [pl.BlockSpec((tokens, tile), lambda j, s: (0, first + j)), whole((tokens, hidden))],
        pl.BlockSpec((tile, hidden), lambda j, s: (first + j, 0)),
        jax.ShapeDtypeStruct((depth, hidden), F32),
        [into],
        [0],
    )


def add_scaled(place, left, right, scale, *done):
    def kernel(s, left_ref, right_ref, *refs):
        refs[-1][...] = (left_ref[...].astype(F32) + right_ref[...].astype(F32)) * scale

    return call(
        kernel,
        left.size,
        8 * left.size,
        place,
        [left, right, *done],
        (1,),
        [whole(left.shape)] * 2 + [pl.BlockSpec(memory_space=pl.ANY)] * len(done),
        whole(left.shape),
        jax.ShapeDtypeStruct(left.shape, F32),
    )


def after(value, *deps):
    return lax.optimization_barrier((value, *deps))[0]


def local(rows_of, cols_of, tokens, weight_in, bias_hidden, weight_out, out_grad):
    mine, depth = tokens.shape
    hidden = bias_hidden.shape[0]
    rows, everyone = 2 * mine, cols_of * mine
    bias = bias_hidden.reshape(1, hidden)
    steps = rows_of - 1
    me = lax.axis_index("col")
    place = jnp.stack([me // 2, me % 2]).astype(jnp.int32)
    others = sorted(range(1, cols_of // 2), key=lambda key: (-key.bit_count(), key))
    chunks = [("pre", 0), ("act", 0)] + [(kind, key) for kind in ("pre", "act") for key in others]
    total = len(chunks)

    def send(value, step):
        pairs = [(step - 1, step), (rows_of - step, rows_of - step - 1)]
        return lax.ppermute(value, "row", pairs)

    def swap(value, bits):
        return lax.ppermute(value, "col", [(i, i ^ bits) for i in range(cols_of)])

    chain = []

    def link(value):
        return after(value, chain[-1]) if chain else value

    own, ahead = {}, {}
    got = {chunk: [None] * steps for chunk in chunks}
    held = {}
    slopes, sums, arrived = {}, {}, []

    def compute_own(kind, keys):
        source, weight = (tokens, weight_in) if kind == "pre" else (out_grad, weight_out)
        if keys == [0]:
            far = held[kind, "far"]
            blocks = [[(link(source), zero, mine, lambda s: s[1] * mine), (far, zero, mine, lambda s: (1 - s[1]) * mine)]]
        else:
            gathered = link(held[kind])
            blocks = [[(gathered, lambda s, key=key: (s[0] ^ key) * rows, rows, zero)] for key in keys]
        outs = partials(place, blocks, weight, kind == "act")
        chain.append(outs[0])
        for key, out in zip(keys, outs):
            own[kind, key] = out

    def first_send(at):
        got[chunks[at]][0] = send(link(own[chunks[at]]), 1)

    def forward(at, step):
        chunk = chunks[at]
        payload = add_bf16(got[chunk][step - 2], link(own[chunk]))
        chain.append(payload)
        ahead.setdefault(chunk, payload)
        got[chunk][step - 1] = send(payload, step)

    def finish(at):
        kind, key = chunk = chunks[at]
        terms = [link(ahead[chunk])] + got[chunk][1:]
        if kind == "pre":
            held["activations"], slopes[key] = activate(place, terms, bias, key, held.get("activations"), everyone)
            chain.append(held["activations"])
        else:
            held["grads"], sums[key] = differentiate(place, terms, slopes[key], key, held.get("grads"), everyone)
            chain.append(held["grads"])

    def out_columns(first, count):
        held["out"] = weight_out_grad(
            place, link(held["activations"]), held["act"], held.get("out"), first, count
        )
        chain.append(held["out"])

    def in_rows(first, count):
        held["in"] = weight_in_grad(place, held["pre"], link(held["grads"]), held.get("in"), first, count)
        chain.append(held["in"])

    def tokens_of(keys, first, last):
        keep, give = token_grad(place, link(held["grads"]), weight_in, keys, rows, first, last)
        chain.append(keep)
        return keys, keep, give

    def exchange(parts):
        keys, keep, give = parts
        return keys, keep, swap(link(give), 1)

    def deliver(parts):
        keys, keep, given = parts
        results = []
        for at, key in enumerate(keys):
            block = slice(at * mine, (at + 1) * mine)
            pair = add_bf16(link(keep)[block], given[block])
            results.append(swap(pair, 2 * key) if key else pair)
        chain.append(pair)
        return results

    held["pre", "far"], held["act", "far"] = swap(tokens, 1), swap(out_grad, 1)
    held["pre"] = lax.all_gather(tokens, "col", axis=0, tiled=True)
    held["act"] = lax.all_gather(after(out_grad, held["pre", "far"]), "col", axis=0, tiled=True)
    compute_own("pre", [0])
    first_send(0)
    compute_own("act", [0])
    first_send(1)
    end = total + steps - 1
    for slot in range(end):
        if slot > 1 and slot + 1 < total:
            first_send(slot + 1)
        if slot == 1:
            compute_own("pre", others[:1])
            first_send(2)
        for step in range(2, steps + 1):
            if 0 <= slot - step + 2 < total:
                forward(slot - step + 2, step)
            if step == 2 and slot == len(others):
                compute_own("act", others)
        if slot == 1:
            compute_own("pre", others[1:])
        if slot >= steps - 1:
            finish(slot - steps + 1)
        if slot == end - 3:
            first = tokens_of([0] + others[:-2], 0, UNITS)
        if slot == end - 2:
            arrived += deliver(exchange(first))
            out_columns(0, UNITS)
    levels = [1 << i for i in range(rows_of.bit_length() - 1)]
    sums = link(functools.reduce(jnp.add, [sums[key] for key in sorted(sums)]))
    for bit in levels[:-1]:
        sums = sums + lax.ppermute(sums, "row", [(i, i ^ bit) for i in range(rows_of)])
    head = add_scaled(place, link(arrived[0]), arrived[1], 1.0)
    chain.append(head)
    last = exchange(tokens_of(others[-2:], 0, UNITS))
    sums = link(sums)
    given = lax.ppermute(sums, "row", [(i, i ^ levels[-1]) for i in range(rows_of)])
    arrived += deliver(last)
    in_rows(0, UNITS)
    grad_bias = add_scaled(place, sums, given, 1.0 / rows_of, held["in"]).reshape(hidden)
    grad_tokens = functools.reduce(jnp.add, [part.astype(F32) for part in arrived[2:]], head).astype(BF16)
    return (grad_tokens, held["in"], grad_bias, held["out"])


def solution(mesh):
    placed = (P("col", "row"), P("row", "col"), P("col"), P("col", "row"), P("col", "row"))
    return jax.shard_map(
        functools.partial(local, mesh.shape["row"], mesh.shape["col"]),
        mesh=mesh,
        in_specs=placed,
        out_specs=(P("col", "row"), P("row", "col"), P("col"), P("col", "row")),
        check_vma=False,
    )
```

```python
import functools

import jax
import jax.numpy as jnp
from jax import lax
from jax.experimental import pallas as pl
from jax.experimental.pallas import tpu as pltpu
from jax.sharding import PartitionSpec as P

GELU_SCALE = 0.7978845608
GELU_CUBIC = 0.044715
F32, BF16 = jnp.float32, jnp.bfloat16
VMEM_LIMIT = 40 * 1024 * 1024
UNITS, AHEAD = 7, 3


def dot(left, right, dims):
    return lax.dot_general(left, right, ((dims[:1], dims[1:]), ((), ())), preferred_element_type=F32)


def call(kernel, flops, moved, place, operands, grid, in_specs, out_specs, out_shape, into=(), outs=(), scratch=()):
    scalars = 1
    aliases = {}
    in_specs, operands = list(in_specs), list(operands)
    for array, out in zip(into, outs):
        if array is not None:
            aliases[scalars + len(operands)] = out
            operands.append(array)
            in_specs.append(pl.BlockSpec(memory_space=pl.ANY))
    return pl.pallas_call(
        kernel,
        grid_spec=pltpu.PrefetchScalarGridSpec(
            num_scalar_prefetch=scalars,
            grid=grid,
            in_specs=in_specs,
            out_specs=out_specs,
            scratch_shapes=list(scratch),
        ),
        out_shape=out_shape,
        input_output_aliases=aliases,
        compiler_params=pltpu.CompilerParams(vmem_limit_bytes=VMEM_LIMIT),
        cost_estimate=pl.CostEstimate(flops=flops, bytes_accessed=moved, transcendentals=0),
    )(place, *operands)


def whole(shape):
    return pl.BlockSpec(shape, lambda i, s: (0,) * len(shape), pipeline_mode=pl.Buffered(1))


def chip_block(rows, columns, key):
    return pl.BlockSpec((rows, columns), lambda i, s: (s[0] ^ key, 0))


def streamed(place, blocks, weight, pieces, dims, flops, write, out_shape, shrink=1):
    axis, first, last = pieces
    size = weight.shape[axis] // UNITS
    count = last - first
    arrays = []
    for block in blocks:
        for array, _, _, _ in block:
            if not any(array is other for other in arrays):
                arrays.append(array)
    total, depth = sum(part[2] for block in blocks for part in block), blocks[0][0][0].shape[1]
    parts = sum(len(block) for block in blocks)
    shape = (size, weight.shape[1]) if axis == 0 else (weight.shape[0], size)

    def kernel(s, *refs):
        sources, weight_ref = refs[: len(arrays)], refs[len(arrays)]
        outs, (block_ref, piece_ref, block_sem, piece_sem) = refs[len(arrays) + 1 : -4], refs[-4:]

        def piece(at):
            where = pl.ds(pl.multiple_of((first + at) * size, size), size)
            source = weight_ref.at[where, :] if axis == 0 else weight_ref.at[:, where]
            return pltpu.make_async_copy(source, piece_ref.at[at], piece_sem.at[at])

        copies, top = [], 0
        for block in blocks:
            for array, start, length, into in block:
                source = next(ref for ref, other in zip(sources, arrays) if other is array)
                copies.append(
                    pltpu.make_async_copy(
                        source.at[pl.ds(pl.multiple_of(start(s), 16), length), :],
                        block_ref.at[pl.ds(pl.multiple_of(top + into(s), 16), length), :],
                        block_sem.at[len(copies)],
                    )
                )
            top += sum(part[2] for part in block)
        piece(0).start()
        for copy in copies:
            copy.start()
        for at in range(1, min(AHEAD, count)):
            piece(at).start()
        for copy in copies:
            copy.wait()

        def step(at, carry):
            piece(at).wait()

            @pl.when(at + AHEAD < count)
            def _():
                piece(at + AHEAD).start()

            write(s, at, dot(block_ref[...], piece_ref[at], dims), outs)
            return carry

        lax.fori_loop(0, count, step, 0)

    moved = 2 * (total * depth + shape[0] * shape[1] * count)
    anywhere = pl.BlockSpec(memory_space=pl.ANY)
    return call(
        kernel,
        flops // shrink,
        moved // shrink,
        place,
        [*arrays, weight],
        (1,),
        [anywhere] * (len(arrays) + 1),
        [whole(out.shape) for out in out_shape],
        out_shape,
        scratch=[
            pltpu.VMEM((total, depth), BF16),
            pltpu.VMEM((count, *shape), BF16),
            pltpu.SemaphoreType.DMA((parts,)),
            pltpu.SemaphoreType.DMA((count,)),
        ],
    )


def zero(s):
    return 0


def columns_of(at, size):
    return pl.ds(pl.multiple_of(at * size, size), size)


def partials(place, blocks, weight, transposed):
    hidden = weight.shape[0 if transposed else 1]
    rows = sum(part[2] for part in blocks[0])
    width = hidden // UNITS

    def write(s, at, product, outs):
        for block, out in enumerate(outs):
            out[:, columns_of(at, width)] = product[block * rows : (block + 1) * rows].astype(BF16)

    return streamed(
        place,
        blocks,
        weight,
        (0 if transposed else 1, 0, UNITS),
        (1, 1) if transposed else (1, 0),
        2 * len(blocks) * rows * weight.size,
        write,
        [jax.ShapeDtypeStruct((rows, hidden), BF16)] * len(blocks),
        64,
    )


def token_grad(place, grad, weight_in, keys, rows, first, last):
    depth, hidden = weight_in.shape
    tile = depth // UNITS
    half = rows // 2

    def write(s, at, product, outs):
        low = s[1] == 0
        for block in range(len(keys)):
            first_half, second_half = (
                product[(2 * block + side) * half : (2 * block + side + 1) * half].astype(BF16) for side in range(2)
            )
            to = (slice(block * half, (block + 1) * half), columns_of(at, tile))
            outs[0][to] = jnp.where(low, first_half, second_half)
            outs[1][to] = jnp.where(low, second_half, first_half)

    return streamed(
        place,
        [[(grad, lambda s, key=key: (s[0] ^ key) * rows, rows, zero)] for key in keys],
        weight_in,
        (0, first, last),
        (1, 1),
        2 * len(keys) * rows * tile * (last - first) * hidden,
        write,
        [jax.ShapeDtypeStruct((len(keys) * half, tile * (last - first)), BF16)] * 2,
    )


def activate(place, terms, bias, key, into, tokens):
    rows, hidden = terms[0].shape

    def kernel(s, bias_ref, *refs):
        ins, (act_ref, slope_ref) = refs[: len(terms)], refs[-2:]
        pre = functools.reduce(jnp.add, [ref[...].astype(F32) for ref in ins]) + bias_ref[...]
        tangent = jnp.tanh(GELU_SCALE * (pre + GELU_CUBIC * pre * pre * pre))
        act_ref[...] = (0.5 * pre * (1.0 + tangent)).astype(BF16)
        slope_ref[...] = 0.5 * (1.0 + tangent) + 0.5 * pre * (1.0 - tangent * tangent) * GELU_SCALE * (
            1.0 + 3.0 * GELU_CUBIC * pre * pre
        )

    block = pl.BlockSpec((rows, hidden), lambda i, s: (0, 0))
    return call(
        kernel,
        30 * rows * hidden,
        rows * hidden * (2 * len(terms) + 6),
        place,
        [bias, *terms],
        (1,),
        [pl.BlockSpec((1, hidden), lambda i, s: (0, 0))] + [block] * len(terms),
        [chip_block(rows, hidden, key), block],
        [jax.ShapeDtypeStruct((tokens, hidden), BF16), jax.ShapeDtypeStruct((rows, hidden), F32)],
        [into],
        [0],
    )


def differentiate(place, terms, slope, key, into, tokens):
    rows, hidden = slope.shape

    def kernel(s, slope_ref, *refs):
        ins, (grad_ref, sum_ref) = refs[: len(terms)], refs[-2:]
        grad = functools.reduce(jnp.add, [ref[...].astype(F32) for ref in ins]) * slope_ref[...]
        grad = grad.astype(BF16)
        grad_ref[...] = grad
        sum_ref[...] = jnp.sum(grad.astype(F32), axis=0, keepdims=True)

    block = pl.BlockSpec((rows, hidden), lambda i, s: (0, 0))
    return call(
        kernel,
        8 * rows * hidden,
        rows * hidden * (2 * len(terms) + 6),
        place,
        [slope, *terms],
        (1,),
        [block] * (1 + len(terms)),
        [chip_block(rows, hidden, key), pl.BlockSpec((1, hidden), lambda i, s: (0, 0))],
        [jax.ShapeDtypeStruct((tokens, hidden), BF16), jax.ShapeDtypeStruct((1, hidden), F32)],
        [into],
        [0],
    )


def add_bf16(left, right):
    return (left.astype(F32) + right.astype(F32)).astype(BF16)


def weight_out_grad(place, act, grad, into, first, count):
    tokens, depth = grad.shape
    hidden = act.shape[1]
    tile, width = depth // UNITS, hidden // UNITS

    def kernel(s, act_ref, grad_ref, *refs):
        out, turned = refs[-2:]

        @pl.when(pl.program_id(0) == 0)
        def _():
            for at in range(0, hidden, width):
                turned[at : at + width, :] = act_ref[:, at : at + width].T

        for at in range(0, hidden, hidden // 2):
            out[at : at + hidden // 2, :] = dot(turned[at : at + hidden // 2, :], grad_ref[...], (1, 0))

    return call(
        kernel,
        2 * tokens * tile * count * hidden,
        2 * tokens * (tile * count + hidden) + 4 * tile * count * hidden,
        place,
        [act, grad],
        (count,),
        [whole((tokens, hidden)), pl.BlockSpec((tokens, tile), lambda j, s: (0, first + j))],
        pl.BlockSpec((hidden, tile), lambda j, s: (0, first + j)),
        jax.ShapeDtypeStruct((hidden, depth), F32),
        [into],
        [0],
        [pltpu.VMEM((hidden, tokens), BF16)],
    )


def weight_in_grad(place, tok, grad, into, first, count):
    tokens, depth = tok.shape
    hidden = grad.shape[1]
    tile, width = depth // UNITS, hidden // 2

    def kernel(s, tok_ref, grad_ref, *refs):
        turned = tok_ref[...].T
        for at in range(0, hidden, width):
            refs[-1][:, at : at + width] = dot(turned, grad_ref[:, at : at + width], (1, 0))

    return call(
        kernel,
        2 * tokens * tile * count * hidden,
        2 * tokens * (tile * count + hidden) + 4 * tile * count * hidden,
        place,
        [tok, grad],
        (count,),
        [pl.BlockSpec((tokens, tile), lambda j, s: (0, first + j)), whole((tokens, hidden))],
        pl.BlockSpec((tile, hidden), lambda j, s: (first + j, 0)),
        jax.ShapeDtypeStruct((depth, hidden), F32),
        [into],
        [0],
    )


def add_scaled(place, left, right, scale, *done):
    def kernel(s, left_ref, right_ref, *refs):
        refs[-1][...] = (left_ref[...].astype(F32) + right_ref[...].astype(F32)) * scale

    return call(
        kernel,
        left.size,
        8 * left.size,
        place,
        [left, right, *done],
        (1,),
        [whole(left.shape)] * 2 + [pl.BlockSpec(memory_space=pl.ANY)] * len(done),
        whole(left.shape),
        jax.ShapeDtypeStruct(left.shape, F32),
    )


def after(value, *deps):
    return lax.optimization_barrier((value, *deps))[0]


def local(rows_of, cols_of, tokens, weight_in, bias_hidden, weight_out, out_grad):
    mine, depth = tokens.shape
    hidden = bias_hidden.shape[0]
    rows, everyone = 2 * mine, cols_of * mine
    bias = bias_hidden.reshape(1, hidden)
    steps = rows_of - 1
    me = lax.axis_index("col")
    place = jnp.stack([me // 2, me % 2]).astype(jnp.int32)
    others = sorted(range(1, cols_of // 2), key=lambda key: (-key.bit_count(), key))
    chunks = [("pre", 0), ("act", 0)] + [(kind, key) for kind in ("pre", "act") for key in others]
    total = len(chunks)

    def send(value, step):
        pairs = [(step - 1, step), (rows_of - step, rows_of - step - 1)]
        return lax.ppermute(value, "row", pairs)

    def swap(value, bits):
        return lax.ppermute(value, "col", [(i, i ^ bits) for i in range(cols_of)])

    chain = []

    def link(value):
        return after(value, chain[-1]) if chain else value

    own, ahead = {}, {}
    got = {chunk: [None] * steps for chunk in chunks}
    held = {}
    slopes, sums, arrived = {}, {}, []

    def compute_own(kind, keys):
        source, weight = (tokens, weight_in) if kind == "pre" else (out_grad, weight_out)
        if keys == [0]:
            far = held[kind, "far"]
            blocks = [[(link(source), zero, mine, lambda s: s[1] * mine), (far, zero, mine, lambda s: (1 - s[1]) * mine)]]
        else:
            gathered = link(held[kind])
            blocks = [[(gathered, lambda s, key=key: (s[0] ^ key) * rows, rows, zero)] for key in keys]
        outs = partials(place, blocks, weight, kind == "act")
        chain.append(outs[0])
        for key, out in zip(keys, outs):
            own[kind, key] = out

    def first_send(at):
        got[chunks[at]][0] = send(link(own[chunks[at]]), 1)

    def forward(at, step):
        chunk = chunks[at]
        payload = add_bf16(got[chunk][step - 2], link(own[chunk]))
        chain.append(payload)
        ahead.setdefault(chunk, payload)
        got[chunk][step - 1] = send(payload, step)

    def finish(at):
        kind, key = chunk = chunks[at]
        terms = [link(ahead[chunk])] + got[chunk][1:]
        if kind == "pre":
            held["activations"], slopes[key] = activate(place, terms, bias, key, held.get("activations"), everyone)
            chain.append(held["activations"])
        else:
            held["grads"], sums[key] = differentiate(place, terms, slopes[key], key, held.get("grads"), everyone)
            chain.append(held["grads"])

    def out_columns(first, count):
        held["out"] = weight_out_grad(
            place, link(held["activations"]), held["act"], held.get("out"), first, count
        )
        chain.append(held["out"])

    def in_rows(first, count):
        held["in"] = weight_in_grad(place, held["pre"], link(held["grads"]), held.get("in"), first, count)
        chain.append(held["in"])

    def tokens_of(keys, first, last):
        keep, give = token_grad(place, link(held["grads"]), weight_in, keys, rows, first, last)
        chain.append(keep)
        return keys, keep, give

    def exchange(parts):
        keys, keep, give = parts
        return keys, keep, swap(link(give), 1)

    def deliver(parts):
        keys, keep, given = parts
        results = []
        for at, key in enumerate(keys):
            block = slice(at * mine, (at + 1) * mine)
            pair = add_bf16(link(keep)[block], given[block])
            results.append(swap(pair, 2 * key) if key else pair)
        chain.append(pair)
        return results

    held["pre", "far"], held["act", "far"] = swap(tokens, 1), swap(out_grad, 1)
    held["pre"] = lax.all_gather(tokens, "col", axis=0, tiled=True)
    held["act"] = lax.all_gather(after(out_grad, held["pre", "far"]), "col", axis=0, tiled=True)
    compute_own("pre", [0])
    first_send(0)
    compute_own("act", [0])
    first_send(1)
    end = total + steps - 1
    begun = set()

    def begin(at):
        if at < total and at not in begun:
            begun.add(at)
            first_send(at)

    def second(at):
        if 0 <= at < total and ("second", at) not in begun:
            begun.add(("second", at))
            forward(at, 2)

    for slot in range(end):
        if slot > 1:
            begin(slot + 1)
        if slot == 1:
            compute_own("pre", others[:1])
            begin(2)
        second(slot)
        for step in range(3, steps + 1):
            if 0 <= slot - step + 2 < total:
                forward(slot - step + 2, step)
        if slot == 1:
            compute_own("pre", others[1:])
        if slot == len(others):
            compute_own("act", others)
            second(slot + 1)
            begin(slot + 2)
        if slot == end - 3:
            out_columns(0, 2)
        if slot >= steps - 1:
            finish(slot - steps + 1)
        if slot == end - 3:
            first = tokens_of([0] + others[:-2], 0, UNITS)
        if slot == end - 2:
            arrived += deliver(exchange(first))
            out_columns(2, UNITS - 2)
    levels = [1 << i for i in range(rows_of.bit_length() - 1)]
    sums = link(functools.reduce(jnp.add, [sums[key] for key in sorted(sums)]))
    for bit in levels[:-1]:
        sums = sums + lax.ppermute(sums, "row", [(i, i ^ bit) for i in range(rows_of)])
    head = add_scaled(place, link(arrived[0]), arrived[1], 1.0)
    chain.append(head)
    last = exchange(tokens_of(others[-2:], 0, UNITS))
    sums = link(sums)
    given = lax.ppermute(sums, "row", [(i, i ^ levels[-1]) for i in range(rows_of)])
    arrived += deliver(last)
    in_rows(0, UNITS)
    grad_bias = add_scaled(place, sums, given, 1.0 / rows_of, held["in"]).reshape(hidden)
    grad_tokens = functools.reduce(jnp.add, [part.astype(F32) for part in arrived[2:]], head).astype(BF16)
    return (grad_tokens, held["in"], grad_bias, held["out"])


def solution(mesh):
    placed = (P("col", "row"), P("row", "col"), P("col"), P("col", "row"), P("col", "row"))
    return jax.shard_map(
        functools.partial(local, mesh.shape["row"], mesh.shape["col"]),
        mesh=mesh,
        in_specs=placed,
        out_specs=(P("col", "row"), P("row", "col"), P("col"), P("col", "row")),
        check_vma=False,
    )
```

```python
import functools

import jax
import jax.numpy as jnp
from jax import lax
from jax.experimental import pallas as pl
from jax.experimental.pallas import tpu as pltpu
from jax.sharding import PartitionSpec as P

GELU_SCALE = 0.7978845608
GELU_CUBIC = 0.044715
F32, BF16 = jnp.float32, jnp.bfloat16
VMEM_LIMIT = 40 * 1024 * 1024
UNITS, AHEAD = 7, 5


def dot(left, right, dims):
    return lax.dot_general(left, right, ((dims[:1], dims[1:]), ((), ())), preferred_element_type=F32)


def call(kernel, flops, moved, place, operands, grid, in_specs, out_specs, out_shape, into=(), outs=(), scratch=()):
    scalars = 1
    aliases = {}
    in_specs, operands = list(in_specs), list(operands)
    for array, out in zip(into, outs):
        if array is not None:
            aliases[scalars + len(operands)] = out
            operands.append(array)
            in_specs.append(pl.BlockSpec(memory_space=pl.ANY))
    return pl.pallas_call(
        kernel,
        grid_spec=pltpu.PrefetchScalarGridSpec(
            num_scalar_prefetch=scalars,
            grid=grid,
            in_specs=in_specs,
            out_specs=out_specs,
            scratch_shapes=list(scratch),
        ),
        out_shape=out_shape,
        input_output_aliases=aliases,
        compiler_params=pltpu.CompilerParams(vmem_limit_bytes=VMEM_LIMIT),
        cost_estimate=pl.CostEstimate(flops=flops, bytes_accessed=moved, transcendentals=0),
    )(place, *operands)


def whole(shape):
    return pl.BlockSpec(shape, lambda i, s: (0,) * len(shape), pipeline_mode=pl.Buffered(1))


def chip_block(rows, columns, key):
    return pl.BlockSpec((rows, columns), lambda i, s: (s[0] ^ key, 0))


def streamed(place, blocks, weight, pieces, dims, flops, write, out_shape, shrink=1):
    axis, first, last = pieces
    size = weight.shape[axis] // UNITS
    count = last - first
    arrays = []
    for block in blocks:
        for array, _, _, _ in block:
            if not any(array is other for other in arrays):
                arrays.append(array)
    total, depth = sum(part[2] for block in blocks for part in block), blocks[0][0][0].shape[1]
    parts = sum(len(block) for block in blocks)
    shape = (size, weight.shape[1]) if axis == 0 else (weight.shape[0], size)

    def kernel(s, *refs):
        sources, weight_ref = refs[: len(arrays)], refs[len(arrays)]
        outs, (block_ref, piece_ref, block_sem, piece_sem) = refs[len(arrays) + 1 : -4], refs[-4:]

        def piece(at):
            where = pl.ds(pl.multiple_of((first + at) * size, size), size)
            source = weight_ref.at[where, :] if axis == 0 else weight_ref.at[:, where]
            return pltpu.make_async_copy(source, piece_ref.at[at], piece_sem.at[at])

        copies, top = [], 0
        for block in blocks:
            for array, start, length, into in block:
                source = next(ref for ref, other in zip(sources, arrays) if other is array)
                copies.append(
                    pltpu.make_async_copy(
                        source.at[pl.ds(pl.multiple_of(start(s), 16), length), :],
                        block_ref.at[pl.ds(pl.multiple_of(top + into(s), 16), length), :],
                        block_sem.at[len(copies)],
                    )
                )
            top += sum(part[2] for part in block)
        piece(0).start()
        for copy in copies:
            copy.start()
        for at in range(1, min(AHEAD, count)):
            piece(at).start()
        for copy in copies:
            copy.wait()

        def step(at, carry):
            piece(at).wait()

            @pl.when(at + AHEAD < count)
            def _():
                piece(at + AHEAD).start()

            write(s, at, dot(block_ref[...], piece_ref[at], dims), outs)
            return carry

        lax.fori_loop(0, count, step, 0)

    moved = 2 * (total * depth + shape[0] * shape[1] * count)
    anywhere = pl.BlockSpec(memory_space=pl.ANY)
    return call(
        kernel,
        flops // shrink,
        moved // shrink,
        place,
        [*arrays, weight],
        (1,),
        [anywhere] * (len(arrays) + 1),
        [whole(out.shape) for out in out_shape],
        out_shape,
        scratch=[
            pltpu.VMEM((total, depth), BF16),
            pltpu.VMEM((count, *shape), BF16),
            pltpu.SemaphoreType.DMA((parts,)),
            pltpu.SemaphoreType.DMA((count,)),
        ],
    )


def zero(s):
    return 0


def columns_of(at, size):
    return pl.ds(pl.multiple_of(at * size, size), size)


def partials(place, blocks, weight, transposed):
    hidden = weight.shape[0 if transposed else 1]
    rows = sum(part[2] for part in blocks[0])
    width = hidden // UNITS

    def write(s, at, product, outs):
        for block, out in enumerate(outs):
            out[:, columns_of(at, width)] = product[block * rows : (block + 1) * rows].astype(BF16)

    return streamed(
        place,
        blocks,
        weight,
        (0 if transposed else 1, 0, UNITS),
        (1, 1) if transposed else (1, 0),
        2 * len(blocks) * rows * weight.size,
        write,
        [jax.ShapeDtypeStruct((rows, hidden), BF16)] * len(blocks),
        64,
    )


def token_grad(place, grad, weight_in, keys, rows, first, last):
    depth, hidden = weight_in.shape
    tile = depth // UNITS
    half = rows // 2

    def write(s, at, product, outs):
        low = s[1] == 0
        for block in range(len(keys)):
            first_half, second_half = (
                product[(2 * block + side) * half : (2 * block + side + 1) * half].astype(BF16) for side in range(2)
            )
            to = (slice(block * half, (block + 1) * half), columns_of(at, tile))
            outs[0][to] = jnp.where(low, first_half, second_half)
            outs[1][to] = jnp.where(low, second_half, first_half)

    return streamed(
        place,
        [[(grad, lambda s, key=key: (s[0] ^ key) * rows, rows, zero)] for key in keys],
        weight_in,
        (0, first, last),
        (1, 1),
        2 * len(keys) * rows * tile * (last - first) * hidden,
        write,
        [jax.ShapeDtypeStruct((len(keys) * half, tile * (last - first)), BF16)] * 2,
    )


def activate(place, terms, bias, key, into, tokens):
    rows, hidden = terms[0].shape

    def kernel(s, bias_ref, *refs):
        ins, (act_ref, slope_ref) = refs[: len(terms)], refs[-2:]
        pre = functools.reduce(jnp.add, [ref[...].astype(F32) for ref in ins]) + bias_ref[...]
        tangent = jnp.tanh(GELU_SCALE * (pre + GELU_CUBIC * pre * pre * pre))
        act_ref[...] = (0.5 * pre * (1.0 + tangent)).astype(BF16)
        slope_ref[...] = 0.5 * (1.0 + tangent) + 0.5 * pre * (1.0 - tangent * tangent) * GELU_SCALE * (
            1.0 + 3.0 * GELU_CUBIC * pre * pre
        )

    block = pl.BlockSpec((rows, hidden), lambda i, s: (0, 0))
    return call(
        kernel,
        30 * rows * hidden,
        rows * hidden * (2 * len(terms) + 6),
        place,
        [bias, *terms],
        (1,),
        [pl.BlockSpec((1, hidden), lambda i, s: (0, 0))] + [block] * len(terms),
        [chip_block(rows, hidden, key), block],
        [jax.ShapeDtypeStruct((tokens, hidden), BF16), jax.ShapeDtypeStruct((rows, hidden), F32)],
        [into],
        [0],
    )


def differentiate(place, terms, slope, key, into, tokens):
    rows, hidden = slope.shape

    def kernel(s, slope_ref, *refs):
        ins, (grad_ref, sum_ref) = refs[: len(terms)], refs[-2:]
        grad = functools.reduce(jnp.add, [ref[...].astype(F32) for ref in ins]) * slope_ref[...]
        grad = grad.astype(BF16)
        grad_ref[...] = grad
        sum_ref[...] = jnp.sum(grad.astype(F32), axis=0, keepdims=True)

    block = pl.BlockSpec((rows, hidden), lambda i, s: (0, 0))
    return call(
        kernel,
        8 * rows * hidden,
        rows * hidden * (2 * len(terms) + 6),
        place,
        [slope, *terms],
        (1,),
        [block] * (1 + len(terms)),
        [chip_block(rows, hidden, key), pl.BlockSpec((1, hidden), lambda i, s: (0, 0))],
        [jax.ShapeDtypeStruct((tokens, hidden), BF16), jax.ShapeDtypeStruct((1, hidden), F32)],
        [into],
        [0],
    )


def add_bf16(left, right):
    return (left.astype(F32) + right.astype(F32)).astype(BF16)


def weight_out_grad(place, act, grad, into, first, count):
    tokens, depth = grad.shape
    hidden = act.shape[1]
    tile, width = depth // UNITS, hidden // UNITS

    def kernel(s, act_ref, grad_ref, *refs):
        out, turned = refs[-2:]

        @pl.when(pl.program_id(0) == 0)
        def _():
            for at in range(0, hidden, width):
                turned[at : at + width, :] = act_ref[:, at : at + width].T

        for at in range(0, hidden, hidden // 2):
            out[at : at + hidden // 2, :] = dot(turned[at : at + hidden // 2, :], grad_ref[...], (1, 0))

    return call(
        kernel,
        2 * tokens * tile * count * hidden,
        2 * tokens * (tile * count + hidden) + 4 * tile * count * hidden,
        place,
        [act, grad],
        (count,),
        [whole((tokens, hidden)), pl.BlockSpec((tokens, tile), lambda j, s: (0, first + j))],
        pl.BlockSpec((hidden, tile), lambda j, s: (0, first + j)),
        jax.ShapeDtypeStruct((hidden, depth), F32),
        [into],
        [0],
        [pltpu.VMEM((hidden, tokens), BF16)],
    )


def weight_in_grad(place, tok, grad, into, first, count):
    tokens, depth = tok.shape
    hidden = grad.shape[1]
    tile, width = depth // UNITS, hidden // 2

    def kernel(s, tok_ref, grad_ref, *refs):
        turned = tok_ref[...].T
        for at in range(0, hidden, width):
            refs[-1][:, at : at + width] = dot(turned, grad_ref[:, at : at + width], (1, 0))

    return call(
        kernel,
        2 * tokens * tile * count * hidden,
        2 * tokens * (tile * count + hidden) + 4 * tile * count * hidden,
        place,
        [tok, grad],
        (count,),
        [pl.BlockSpec((tokens, tile), lambda j, s: (0, first + j)), whole((tokens, hidden))],
        pl.BlockSpec((tile, hidden), lambda j, s: (first + j, 0)),
        jax.ShapeDtypeStruct((depth, hidden), F32),
        [into],
        [0],
    )


def add_scaled(place, left, right, scale, *done):
    def kernel(s, left_ref, right_ref, *refs):
        refs[-1][...] = (left_ref[...].astype(F32) + right_ref[...].astype(F32)) * scale

    return call(
        kernel,
        left.size,
        8 * left.size,
        place,
        [left, right, *done],
        (1,),
        [whole(left.shape)] * 2 + [pl.BlockSpec(memory_space=pl.ANY)] * len(done),
        whole(left.shape),
        jax.ShapeDtypeStruct(left.shape, F32),
    )


def after(value, *deps):
    return lax.optimization_barrier((value, *deps))[0]


def local(rows_of, cols_of, tokens, weight_in, bias_hidden, weight_out, out_grad):
    mine, depth = tokens.shape
    hidden = bias_hidden.shape[0]
    rows, everyone = 2 * mine, cols_of * mine
    bias = bias_hidden.reshape(1, hidden)
    steps = rows_of - 1
    me = lax.axis_index("col")
    place = jnp.stack([me // 2, me % 2]).astype(jnp.int32)
    others = sorted(range(1, cols_of // 2), key=lambda key: (-key.bit_count(), key))
    chunks = [("pre", 0), ("act", 0)] + [(kind, key) for kind in ("pre", "act") for key in others]
    total = len(chunks)

    def send(value, step):
        pairs = [(step - 1, step), (rows_of - step, rows_of - step - 1)]
        return lax.ppermute(value, "row", pairs)

    def swap(value, bits):
        return lax.ppermute(value, "col", [(i, i ^ bits) for i in range(cols_of)])

    chain = []

    def link(value):
        return after(value, chain[-1]) if chain else value

    own, ahead = {}, {}
    got = {chunk: [None] * steps for chunk in chunks}
    held = {}
    slopes, sums, arrived = {}, {}, []

    def compute_own(kind, keys):
        source, weight = (tokens, weight_in) if kind == "pre" else (out_grad, weight_out)
        if keys == [0]:
            far = held[kind, "far"]
            blocks = [[(link(source), zero, mine, lambda s: s[1] * mine), (far, zero, mine, lambda s: (1 - s[1]) * mine)]]
        else:
            gathered = link(held[kind])
            blocks = [[(gathered, lambda s, key=key: (s[0] ^ key) * rows, rows, zero)] for key in keys]
        outs = partials(place, blocks, weight, kind == "act")
        chain.append(outs[0])
        for key, out in zip(keys, outs):
            own[kind, key] = out

    def first_send(at):
        got[chunks[at]][0] = send(link(own[chunks[at]]), 1)

    def forward(at, step):
        chunk = chunks[at]
        payload = add_bf16(got[chunk][step - 2], link(own[chunk]))
        chain.append(payload)
        ahead.setdefault(chunk, payload)
        got[chunk][step - 1] = send(payload, step)

    def finish(at):
        kind, key = chunk = chunks[at]
        terms = [link(ahead[chunk])] + got[chunk][1:]
        if kind == "pre":
            held["activations"], slopes[key] = activate(place, terms, bias, key, held.get("activations"), everyone)
            chain.append(held["activations"])
        else:
            held["grads"], sums[key] = differentiate(place, terms, slopes[key], key, held.get("grads"), everyone)
            chain.append(held["grads"])

    def out_columns(first, count):
        held["out"] = weight_out_grad(
            place, link(held["activations"]), held["act"], held.get("out"), first, count
        )
        chain.append(held["out"])

    def in_rows(first, count):
        held["in"] = weight_in_grad(place, held["pre"], link(held["grads"]), held.get("in"), first, count)
        chain.append(held["in"])

    def tokens_of(keys, first, last):
        keep, give = token_grad(place, link(held["grads"]), weight_in, keys, rows, first, last)
        chain.append(keep)
        return keys, keep, give

    def exchange(parts):
        keys, keep, give = parts
        return keys, keep, swap(link(give), 1)

    def deliver(parts):
        keys, keep, given = parts
        results = []
        for at, key in enumerate(keys):
            block = slice(at * mine, (at + 1) * mine)
            pair = add_bf16(link(keep)[block], given[block])
            results.append(swap(pair, 2 * key) if key else pair)
        chain.append(pair)
        return results

    held["pre", "far"], held["act", "far"] = swap(tokens, 1), swap(out_grad, 1)
    held["pre"] = lax.all_gather(tokens, "col", axis=0, tiled=True)
    held["act"] = lax.all_gather(after(out_grad, held["pre", "far"]), "col", axis=0, tiled=True)
    compute_own("pre", [0])
    first_send(0)
    compute_own("act", [0])
    first_send(1)
    end = total + steps - 1
    begun = set()

    def begin(at):
        if at < total and at not in begun:
            begun.add(at)
            first_send(at)

    def second(at):
        if 0 <= at < total and ("second", at) not in begun:
            begun.add(("second", at))
            forward(at, 2)

    for slot in range(end):
        if slot > 1:
            begin(slot + 1)
        if slot == 1:
            compute_own("pre", others[:1])
            begin(2)
        second(slot)
        for step in range(3, steps + 1):
            if 0 <= slot - step + 2 < total:
                forward(slot - step + 2, step)
        if slot == 1:
            compute_own("pre", others[1:])
        if slot == len(others):
            compute_own("act", others)
            second(slot + 1)
            begin(slot + 2)
        if slot == end - 3:
            out_columns(0, 2)
        if slot >= steps - 1:
            finish(slot - steps + 1)
        if slot == end - 3:
            first = tokens_of([0] + others[:-2], 0, UNITS)
        if slot == end - 2:
            arrived += deliver(exchange(first))
            out_columns(2, UNITS - 2)
    levels = [1 << i for i in range(rows_of.bit_length() - 1)]
    sums = link(functools.reduce(jnp.add, [sums[key] for key in sorted(sums)]))
    for bit in levels[:-1]:
        sums = sums + lax.ppermute(sums, "row", [(i, i ^ bit) for i in range(rows_of)])
    head = add_scaled(place, link(arrived[0]), arrived[1], 1.0)
    chain.append(head)
    sums = link(sums)
    chain.append(sums)
    last = exchange(tokens_of(others[-2:], 0, UNITS))
    given = lax.ppermute(sums, "row", [(i, i ^ levels[-1]) for i in range(rows_of)])
    arrived += deliver(last)
    in_rows(0, UNITS)
    grad_bias = add_scaled(place, sums, given, 1.0 / rows_of, held["in"]).reshape(hidden)
    grad_tokens = functools.reduce(jnp.add, [part.astype(F32) for part in arrived[2:]], head).astype(BF16)
    return (grad_tokens, held["in"], grad_bias, held["out"])


def solution(mesh):
    placed = (P("col", "row"), P("row", "col"), P("col"), P("col", "row"), P("col", "row"))
    return jax.shard_map(
        functools.partial(local, mesh.shape["row"], mesh.shape["col"]),
        mesh=mesh,
        in_specs=placed,
        out_specs=(P("col", "row"), P("row", "col"), P("col"), P("col", "row")),
        check_vma=False,
    )
```
